32 devices in a mesh: dp: 16 (over z, y, core), fsdp: 2 (over x).
Axes of the slice: x: 2, y: 2, z: 4, core: 2. Of those that a mesh axis runs over, the one named last changes fastest.
Arguments:
- tokens: bfloat16 [128, 256, 384], P(('dp', 'fsdp')), may hold values from -6 to 6
- condition: bfloat16 [128, 384], P(('dp', 'fsdp')), may hold values from -6 to 6
- image_grid: int32 [128, 2], P(('dp', 'fsdp')), may hold values from 12 to 20, as said below
- image_counts: int32 [32], P(('dp', 'fsdp')), may hold values from 1 to 4, as said below
- cotangent: bfloat16 [128, 256, 384], P(('dp', 'fsdp')), may hold values from -6 to 6
- entry_master: float32 [2, 384, 5376], P(None, 'fsdp'), as said below
- exit_master: float32 [2, 1536, 384], P(None, 'fsdp'), may hold values from -0.15625 to 0.15625
- bias_master: float32 [2, 5760], P(None, 'fsdp'), may hold values from -0.6 to 0.6
- entry_moment: float32 [2, 384, 5376], P(None, 'fsdp'), may hold values from -6 to 6
- exit_moment: float32 [2, 1536, 384], P(None, 'fsdp'), may hold values from -6 to 6
- bias_moment: float32 [2, 5760], P(None, 'fsdp'), may hold values from -6 to 6
- entry_square: float32 [2, 384, 5376], P(None, 'fsdp'), may hold values from 0.3 to 3
- exit_square: float32 [2, 1536, 384], P(None, 'fsdp'), may hold values from 0.3 to 3
- bias_square: float32 [2, 5760], P(None, 'fsdp'), may hold values from 0.3 to 3
Outputs:
- block_output: bfloat16 [128, 256, 384], P(('dp', 'fsdp'))
- grad_tokens: float32 [128, 256, 384], P(('dp', 'fsdp'))
- grad_condition: float32 [128, 384], P(('dp', 'fsdp'))
- entry_grad: float32 [2, 384, 5376], P(None, 'fsdp')
- entry_moment_new: float32 [2, 384, 5376], P(None, 'fsdp')
- entry_square_new: float32 [2, 384, 5376], P(None, 'fsdp')
- entry_master_new: float32 [2, 384, 5376], P(None, 'fsdp')
- entry_weight: bfloat16 [2, 384, 5376], P(None, 'fsdp')
- exit_grad: float32 [2, 1536, 384], P(None, 'fsdp')
- exit_moment_new: float32 [2, 1536, 384], P(None, 'fsdp')
- exit_square_new: float32 [2, 1536, 384], P(None, 'fsdp')
- exit_master_new: float32 [2, 1536, 384], P(None, 'fsdp')
- exit_weight: bfloat16 [2, 1536, 384], P(None, 'fsdp')
- bias_grad: float32 [2, 5760], P(None, 'fsdp')
- bias_moment_new: float32 [2, 5760], P(None, 'fsdp')
- bias_square_new: float32 [2, 5760], P(None, 'fsdp')
- bias_master_new: float32 [2, 5760], P(None, 'fsdp')
- bias_weight: bfloat16 [2, 5760], P(None, 'fsdp')
- exit_bias_grad: float32 [2, 384], P(None, 'fsdp')
The draws below stay inside these ranges and needn't reach their ends.
Inputs may be any that keep to these rules, and one draw needn't show every extreme that they name: `image_grid`: each image has 12 to 20 patch rows and columns and rows times columns at most 256; its patches take the first rows times columns slots. In every draw some image fills all 256 slots and some has 20 rows. `image_counts`: image slot j of a device is live when j is below the device's count; some device holds 4 live images and some holds one. `entry_master`: packed weights of each block.
All inputs are finite; a program needn't handle non-finite values.
Results may differ from the reference program's by a relative error of at most 0.018.
The reference program's roundings to bfloat16 on the way count: a program that leaves them out, or rounds other values in their place, can miss the bound.
Values may be sent and summed in bfloat16 or wider, within the bound.
No kernel may reach another device: no remote copies, remote signals or barrier semaphores. Data moves between devices by JAX's collectives and lax.ppermute only.
A program may use at most 256 MiB of HBM per device.

```python
import math
import jax
import jax.numpy as jnp
from jax import lax

D = 384
HEADS = 6
HEAD_DIM = 64
FF = 1536
LAYERS = 2
IMG_DEV = 4
GRID = 16
SIDE_MIN = 12
SIDE_MAX = 20
STEP = 4
SLOTS = 256
IMAGES = 128
TOKENS = 32768
ENTRY_COLS = 5376
BIAS_LEN = 5760
N_DP = 16
N_FSDP = 2


def draw_image_grid(key, part):
    key_rows = jax.random.fold_in(key, 11)
    key_cols = jax.random.fold_in(key, 12)
    key_pick = jax.random.fold_in(key, 13)
    key_other = jax.random.fold_in(key, 14)
    row_sides = jax.random.randint(key_rows, (IMAGES,), SIDE_MIN, SIDE_MAX + 1)
    widest = jnp.minimum(SIDE_MAX, SLOTS // row_sides)
    raw_cols = jax.random.randint(key_cols, (IMAGES,), 0, 1 << 20)
    col_sides = SIDE_MIN + raw_cols % (widest - SIDE_MIN + 1)
    chosen = jax.random.randint(key_pick, (), 0, IMAGES)
    second = (chosen + 1 + jax.random.randint(key_other, (), 0, IMAGES - 1)) % IMAGES
    places = jnp.arange(IMAGES)
    row_sides = jnp.where(places == chosen, GRID, jnp.where(places == second, SIDE_MAX, row_sides))
    col_sides = jnp.where(places == chosen, GRID, jnp.where(places == second, SIDE_MIN, col_sides))
    return jnp.stack([row_sides, col_sides], axis=1).astype(jnp.int32)


def draw_image_counts(key, part):
    device_total = N_DP * N_FSDP
    key_values = jax.random.fold_in(key, 21)
    key_pick = jax.random.fold_in(key, 22)
    key_other = jax.random.fold_in(key, 23)
    counted = jax.random.randint(key_values, (device_total,), 1, IMG_DEV + 1)
    chosen = jax.random.randint(key_pick, (), 0, device_total)
    second = (chosen + 1 + jax.random.randint(key_other, (), 0, device_total - 1)) % device_total
    places = jnp.arange(device_total)
    counted = jnp.where(places == chosen, IMG_DEV, jnp.where(places == second, 1, counted))
    return counted.astype(jnp.int32)


def draw_entry_master(key, part):
    columns = 10 * D + FF
    column_index = jnp.arange(columns)
    widened = jnp.logical_and(column_index >= 3 * D, column_index < 4 * D)
    scaling = jnp.where(widened, 3.0, 1.0).astype(jnp.float32) * D ** (-0.5)
    base = jax.random.normal(key, (LAYERS, D, columns), jnp.float32)
    return base * scaling[None, None, :]


def block_levels(rng, dims, cuts, least, largest):
    gain, own = 1.0, jax.random.fold_in(rng, 6)
    for position, parts in cuts:
        heights = jnp.exp(jax.random.uniform(jax.random.fold_in(own, position), (parts,), jnp.float32, least / len(cuts), largest / len(cuts)))
        gain = gain * jnp.repeat(heights, dims[position] // parts).reshape([-1 if axis == position else 1 for axis in range(len(dims))])
    return gain


def bell_draw(stream_key, extent, spread, most, cuts=(), dtype=jnp.bfloat16):
    loudness = block_levels(stream_key, extent, cuts, -0.22, 0.18) if cuts else 1.0
    drawn = jax.random.normal(stream_key, extent, jnp.float32) * spread * loudness
    return jnp.minimum(jnp.maximum(drawn, -most), most).astype(dtype)


def setup_inputs(seed: int = 0) -> dict:
    splits = jax.random.split(jax.random.key(seed), 15)
    tokens = bell_draw(splits[0], (IMAGES, SLOTS, D), 1.0, 6.0, ((0, 32),))
    condition = bell_draw(splits[1], (IMAGES, D), 1.0, 6.0, ((0, 32),))
    image_grid = draw_image_grid(jax.random.fold_in(splits[14], 71), 0)
    image_counts = draw_image_counts(jax.random.fold_in(splits[14], 71), 0)
    cotangent = bell_draw(splits[4], (IMAGES, SLOTS, D), 1.0, 6.0, ((0, 32),))
    entry_master = draw_entry_master(jax.random.fold_in(splits[14], 71), 0)
    exit_master = bell_draw(splits[6], (LAYERS, FF, D), FF ** -0.5, 0.15625, ((1, 2),), jnp.float32)
    bias_master = bell_draw(splits[7], (LAYERS, BIAS_LEN), 0.1, 0.6, ((1, 2),), jnp.float32)
    entry_moment = bell_draw(splits[8], (LAYERS, D, ENTRY_COLS), 1.0, 6.0, ((1, 2),), jnp.float32)
    exit_moment = bell_draw(splits[9], (LAYERS, FF, D), 1.0, 6.0, ((1, 2),), jnp.float32)
    bias_moment = bell_draw(splits[10], (LAYERS, BIAS_LEN), 1.0, 6.0, ((1, 2),), jnp.float32)
    entry_square = jnp.clip(jnp.exp(math.log(3.0) - 2.3025851 * jax.random.uniform(splits[11], (LAYERS, D, ENTRY_COLS), jnp.float32) ** block_levels(splits[11], (LAYERS, D, ENTRY_COLS), ((1, 2),), -0.2, 0.2)), 0.3, 3.0)
    exit_square = jnp.clip(jnp.exp(math.log(3.0) - 2.3025851 * jax.random.uniform(splits[12], (LAYERS, FF, D), jnp.float32) ** block_levels(splits[12], (LAYERS, FF, D), ((1, 2),), -0.2, 0.2)), 0.3, 3.0)
    bias_square = jnp.clip(jnp.exp(math.log(3.0) - 2.3025851 * jax.random.uniform(splits[13], (LAYERS, BIAS_LEN), jnp.float32) ** block_levels(splits[13], (LAYERS, BIAS_LEN), ((1, 2),), -0.2, 0.2)), 0.3, 3.0)
    return {"tokens": tokens, "condition": condition, "image_grid": image_grid, "image_counts": image_counts, "cotangent": cotangent, "entry_master": entry_master, "exit_master": exit_master, "bias_master": bias_master, "entry_moment": entry_moment, "exit_moment": exit_moment, "bias_moment": bias_moment, "entry_square": entry_square, "exit_square": exit_square, "bias_square": bias_square}


@jax.custom_vjp
def low(v):
    return lax.optimization_barrier(v.astype(jnp.bfloat16)).astype(jnp.float32)

@jax.custom_vjp
def low_back(v):
    return v

def low_keep(v):
    return (low(v), None)

def low_pass(kept, grad):
    return (grad,)

def back_keep(v):
    return (v, None)

def back_low(kept, grad):
    return (low(grad),)
low.defvjp(low_keep, low_pass)
low_back.defvjp(back_keep, back_low)
eps_norm = 1e-06
neg_big = -1e+30
beta_one = 0.5
beta_two = 0.6
adam_eps = 1e-08
learn_rate = 0.02
decay_rate = 0.1
images_per_step = 16

def rounded(values):
    return low(low_back(values))

def product(left, right):
    return jnp.dot(left, right, precision=lax.Precision.HIGHEST, preferred_element_type=jnp.float32)

def normalize(values):
    row_mean = lax.optimization_barrier(jnp.mean(values, axis=-1, keepdims=True))
    centered = values - row_mean
    variance = lax.optimization_barrier(jnp.mean(centered * centered, axis=-1, keepdims=True))
    return centered * lax.rsqrt(variance + eps_norm)

def modulate(values, offset, scaling):
    return normalize(values) * (1.0 + scaling[:, None, :]) + offset[:, None, :]

def adam_update(gradient, master, moment, square):
    new_moment = beta_one * moment + (1.0 - beta_one) * gradient
    new_square = beta_two * square + (1.0 - beta_two) * gradient * gradient
    first_fix = 1.0 - beta_one ** STEP
    second_fix = 1.0 - beta_two ** STEP
    direction = new_moment / first_fix / (jnp.sqrt(new_square / second_fix) + adam_eps) + decay_rate * master
    new_master = master - learn_rate * direction
    return (new_moment, new_square, new_master)

def block_forward(residual, live_mask, cond_act, entry_weights, exit_weights, bias_all):
    entry_weights = low(entry_weights)
    exit_weights = low(exit_weights)
    bias_all = low(bias_all)
    images = residual.shape[0]
    row_count = images * SLOTS
    query_end = 3 * D
    proj_end = 4 * D
    hidden_end = 4 * D + FF
    ada_end = 10 * D + FF
    modulation = low_back(product(cond_act, entry_weights[:, hidden_end:ada_end]) + bias_all[hidden_end:ada_end])
    mod_parts = jnp.split(modulation, 6, axis=-1)
    normed_one = low(modulate(residual, mod_parts[0], mod_parts[1])).reshape(row_count, D)
    projected = rounded(product(normed_one, entry_weights[:, :query_end]) + bias_all[:query_end])
    projected = projected.reshape(images, SLOTS, 3, HEADS, HEAD_DIM)
    queries = projected[:, :, 0]
    keys_all = projected[:, :, 1]
    values_all = projected[:, :, 2]
    scores = jnp.einsum('gqhd,gkhd->ghqk', queries, keys_all, precision=lax.Precision.HIGHEST)
    scores = low_back(scores * HEAD_DIM ** (-0.5))
    scores = jnp.where(live_mask[:, None, None, :] > 0, scores, neg_big)
    weights_low = low(jax.nn.softmax(scores, axis=-1))
    attended = jnp.einsum('ghqk,gkhd->gqhd', weights_low, values_all, precision=lax.Precision.HIGHEST)
    attended = rounded(attended).reshape(row_count, D)
    branch = low_back(product(attended, entry_weights[:, query_end:proj_end]) + bias_all[query_end:proj_end])
    middle = residual + mod_parts[2][:, None, :] * branch.reshape(images, SLOTS, D)
    normed_two = low(modulate(middle, mod_parts[3], mod_parts[4])).reshape(row_count, D)
    pre_act = low_back(product(normed_two, entry_weights[:, proj_end:hidden_end]) + bias_all[proj_end:hidden_end])
    activated = low(jax.nn.gelu(pre_act, approximate=True))
    leaving = low_back(product(activated, exit_weights) + bias_all[ada_end:])
    return middle + mod_parts[5][:, None, :] * leaving.reshape(images, SLOTS, D)

def reference(tokens, condition, image_grid, image_counts, cotangent, entry_master, exit_master, bias_master, entry_moment, exit_moment, bias_moment, entry_square, exit_square, bias_square):
    image_index = jnp.arange(IMAGES)
    live_image = image_index % IMG_DEV < image_counts[image_index // IMG_DEV]
    cell_count = image_grid[:, 0] * image_grid[:, 1]
    live_mask = jnp.logical_and(live_image[:, None], jnp.arange(SLOTS)[None, :] < cell_count[:, None]).astype(jnp.float32)
    step_count = IMAGES // images_per_step
    scan_items = (tokens.astype(jnp.float32).reshape(step_count, images_per_step, SLOTS, D), condition.astype(jnp.float32).reshape(step_count, images_per_step, D), live_mask.reshape(step_count, images_per_step, SLOTS), cotangent.astype(jnp.float32).reshape(step_count, images_per_step, SLOTS, D))

    def advance(totals, scan_item):
        tokens_part, cond_part, live_part, cot_part = scan_item

        def forward(tokens_in, cond_in, entry_in, exit_in, bias_in):
            cond_act = low(jax.nn.silu(cond_in))
            carried = tokens_in
            for layer_index in range(LAYERS):
                carried = block_forward(carried, live_part, cond_act, entry_in[layer_index], exit_in[layer_index], bias_in[layer_index])
            return carried
        result, pullback = jax.vjp(forward, tokens_part, cond_part, entry_master, exit_master, bias_master)
        gradients = pullback(cot_part * live_part[..., None])
        totals = (totals[0] + gradients[2], totals[1] + gradients[3], totals[2] + gradients[4])
        return (totals, (result.astype(jnp.bfloat16), gradients[0], gradients[1]))
    zero_grads = (jnp.zeros_like(entry_master), jnp.zeros_like(exit_master), jnp.zeros_like(bias_master))
    totals, (outputs_all, grad_tokens, grad_condition) = lax.scan(advance, zero_grads, scan_items)
    scale_grad = TOKENS ** (-0.5)
    entry_grad = totals[0] * scale_grad
    exit_grad = totals[1] * scale_grad
    bias_grad = totals[2] * scale_grad
    exit_bias_grad = bias_grad[:, 10 * D + FF:]
    entry_moment_new, entry_square_new, entry_master_new = adam_update(entry_grad, entry_master, entry_moment, entry_square)
    exit_moment_new, exit_square_new, exit_master_new = adam_update(exit_grad, exit_master, exit_moment, exit_square)
    bias_moment_new, bias_square_new, bias_master_new = adam_update(bias_grad, bias_master, bias_moment, bias_square)
    return (outputs_all.reshape(IMAGES, SLOTS, D), grad_tokens.reshape(IMAGES, SLOTS, D), grad_condition.reshape(IMAGES, D), entry_grad, entry_moment_new, entry_square_new, entry_master_new, entry_master_new.astype(jnp.bfloat16), exit_grad, exit_moment_new, exit_square_new, exit_master_new, exit_master_new.astype(jnp.bfloat16), bias_grad, bias_moment_new, bias_square_new, bias_master_new, bias_master_new.astype(jnp.bfloat16), exit_bias_grad)
```

```python
from functools import partial

import jax
import jax.numpy as jnp
from jax import lax
from jax.experimental import pallas as pl
from jax.experimental.pallas import tpu as pltpu
from jax.sharding import PartitionSpec as P

D = 384
HEADS = 6
HEAD_DIM = 64
FF = 1536
LAYERS = 2
IMG = 4
STEP = 4
SLOTS = 256
ADA = 6 * D

eps_norm = 1e-06
neg_big = -1e30
beta_one = 0.5
beta_two = 0.6
adam_eps = 1e-08
learn_rate = 0.02
decay_rate = 0.1

f32 = jnp.float32
bf16 = jnp.bfloat16
VMEM_BYTES = 56 * 1024 * 1024


def nn(a, b):
    return lax.dot_general(a, b, (((1,), (0,)), ((), ())), preferred_element_type=f32)


def nt(a, b):
    return lax.dot_general(a, b, (((1,), (1,)), ((), ())), preferred_element_type=f32)


def tn(a, b):
    return lax.dot_general(a, b, (((0,), (0,)), ((), ())), preferred_element_type=f32)


def standardize(x):
    mean = jnp.mean(x, axis=-1, keepdims=True)
    cen = x - mean
    var = jnp.mean(cen * cen, axis=-1, keepdims=True)
    rstd = lax.rsqrt(var + eps_norm)
    return cen * rstd, rstd


def norm_back(g, xhat, rstd, scale):
    t = g * (1.0 + scale)
    mean_t = jnp.mean(t, axis=-1, keepdims=True)
    mean_tx = jnp.mean(t * xhat, axis=-1, keepdims=True)
    return (t - mean_t - xhat * mean_tx) * rstd


def colsum(x):
    return jnp.sum(x, axis=0, keepdims=True)


def at_lane(i):
    return pl.ds(pl.multiple_of(i * D, 128), D)


def at_row(i, r):
    return pl.ds(pl.multiple_of(i * r, 16), r)


def assemble_attn(sc, parts, w_ref, r, fsdp):
    c, y, f = sc[0], sc[1], sc[2]
    for kc in range(2):
        for j in range(fsdp):
            for ky in range(2):
                col = (c ^ kc) * 2 + (y ^ ky)
                w_ref[at_row(f ^ j, r), at_lane(col)] = parts[kc][j][ky, 0]


def assemble_ffn(sc, parts, w1_ref, w2_ref, r, fsdp):
    c, y, f = sc[0], sc[1], sc[2]
    for kc in range(2):
        for cb in range(2):

            @pl.when((c ^ kc) == cb)
            def _(kc=kc, cb=cb):
                for j in range(fsdp):
                    for ky in range(2):
                        for i in range(2):
                            blk = parts[kc][j][ky, i]
                            pos = (y ^ ky) * 2 + i
                            if cb == 0:
                                w1_ref[at_row(f ^ j, r), at_lane(pos)] = blk
                            else:
                                w2_ref[at_row((f ^ j) * 4 + pos, r), :] = blk


def emit_attn(sc, acc, keep, send, r, fsdp):
    c, y, f = sc[0], sc[1], sc[2]
    for j in range(fsdp):
        for ky in range(2):
            for kc in range(2):
                blk = acc[at_row(f ^ j, r), at_lane((c ^ kc) * 2 + (y ^ ky))]
                if kc == 0:
                    keep[j, ky, 0] = blk
                else:
                    send[j, ky, 0] = blk.astype(bf16)


def emit_ffn(sc, acc1, acc2, keep, send, r, fsdp):
    c, y, f = sc[0], sc[1], sc[2]
    for kc in range(2):
        for cb in range(2):

            @pl.when((c ^ kc) == cb)
            def _(kc=kc, cb=cb):
                for j in range(fsdp):
                    for ky in range(2):
                        for i in range(2):
                            pos = (y ^ ky) * 2 + i
                            if cb == 0:
                                blk = acc1[at_row(f ^ j, r), at_lane(pos)]
                            else:
                                blk = acc2[at_row((f ^ j) * 4 + pos, r), :]
                            if kc == 0:
                                keep[j, ky, i] = blk
                            else:
                                send[j, ky, i] = blk.astype(bf16)


def half_lane():
    return lax.broadcasted_iota(jnp.int32, (1, 2 * HEAD_DIM), 1) < HEAD_DIM


def attn_forward_body(fsdp, r, *refs):
    sc, x_ref, mod_ref, bias_ref = refs[:4]
    n = 2 * fsdp
    parts = refs[4 : 4 + n]
    mid_ref, qkv_ref, probs_ref, att_ref, branch_ref, w_ref = refs[4 + n :]
    img = pl.program_id(0)

    @pl.when(img == 0)
    def _():
        assemble_attn(sc, (parts[:fsdp], parts[fsdp:]), w_ref, r, fsdp)

    x = x_ref[0].astype(f32)
    xhat, _ = standardize(x)
    normed = (xhat * (1.0 + mod_ref[0, 1:2]) + mod_ref[0, 0:1]).astype(bf16)
    qkv = (nn(normed, w_ref[:, : 3 * D]) + bias_ref[:, : 3 * D]).astype(bf16)
    qkv_ref[0] = qkv
    live = lax.broadcasted_iota(jnp.int32, (1, SLOTS), 1) < sc[4 + img]
    low_half = half_lane()
    for p in range(3):
        lanes = slice(2 * HEAD_DIM * p, 2 * HEAD_DIM * (p + 1))
        q = qkv[:, : D][:, lanes] * jnp.asarray(HEAD_DIM ** (-0.5), bf16)
        k = qkv[:, D : 2 * D][:, lanes]
        v = qkv[:, 2 * D :][:, lanes]
        outs = []
        for h in range(2):
            qm = jnp.where(low_half == (h == 0), q, jnp.zeros_like(q))
            s = jnp.where(live, nt(qm, k), neg_big)
            e = jnp.exp(s - jnp.max(s, axis=-1, keepdims=True))
            probs = e * (1.0 / jnp.sum(e, axis=-1, keepdims=True))
            probs_ref[0, 2 * p + h] = probs
            outs.append(nn(probs.astype(bf16), v))
        att_ref[0, :, lanes] = jnp.where(low_half, outs[0], outs[1]).astype(bf16)
    branch = nn(att_ref[0], w_ref[:, 3 * D :]) + bias_ref[:, 3 * D :]
    branch_ref[0] = branch
    mid_ref[0] = x + mod_ref[0, 2:3] * branch


def gelu_parts(v):
    inner = 0.7978845608 * (v + 0.044715 * v * v * v)
    th = jnp.tanh(inner)
    return th


def gelu(v):
    return 0.5 * v * (1.0 + gelu_parts(v))


def gelu_grad(v):
    sq = v * v
    th = jnp.tanh(0.7978845608 * (v + 0.044715 * sq * v))
    slope = 0.7978845608 * (1.0 + 3.0 * 0.044715 * sq)
    return 0.5 * (1.0 + th) + 0.5 * v * (1.0 - th * th) * slope


def ffn_forward_body(fsdp, r, *refs):
    sc, mid_ref, mod_ref, b1_ref, b2_ref = refs[:5]
    n = 2 * fsdp
    parts = refs[5 : 5 + n]
    y_ref, pre_ref, act_ref, leave_ref, w1_ref, w2_ref = refs[5 + n :]
    img = pl.program_id(0)

    @pl.when(img == 0)
    def _():
        assemble_ffn(sc, (parts[:fsdp], parts[fsdp:]), w1_ref, w2_ref, r, fsdp)

    mid = mid_ref[0]
    xhat, _ = standardize(mid)
    normed = (xhat * (1.0 + mod_ref[0, 4:5]) + mod_ref[0, 3:4]).astype(bf16)
    pre = nn(normed, w1_ref[...]) + b1_ref[...]
    pre_ref[0] = pre
    act = gelu(pre).astype(bf16)
    act_ref[0] = act
    leaving = nn(act, w2_ref[...]) + b2_ref[...]
    leave_ref[0] = leaving
    y_ref[0] = mid + mod_ref[0, 5:6] * leaving


def ffn_back_core(
    img, g_y, mid, xhat, rstd, normed, pre, act, leaving, mod_ref, w1, w2,
    gmid_ref, gmod_ref, bs1_ref, bs2_ref, acc1, acc2,
):
    gate = mod_ref[0, 5:6]
    g_leave = (gate * g_y).astype(bf16)
    gmod_ref[0, 2:3] = colsum(g_y * leaving)
    first = img == 0

    def add(ref, val):
        ref[...] = jnp.where(first, val, ref[...] + val)

    bias_two = colsum(g_leave.astype(f32))
    d_two = tn(act, g_leave)
    g_act = nt(g_leave, w2[...])
    g_pre = (gelu_grad(pre) * g_act).astype(bf16)
    bias_one = colsum(g_pre.astype(f32))
    d_one = tn(normed, g_pre)
    g_n = nt(g_pre, w1[...])
    gmod_ref[0, 0:1] = colsum(g_n)
    gmod_ref[0, 1:2] = colsum(g_n * xhat)
    gmid_ref[0] = g_y + norm_back(g_n, xhat, rstd, mod_ref[0, 4:5])

    @pl.when(first)
    def _():
        acc1[...] = d_one
        acc2[...] = d_two
        bs1_ref[...] = bias_one
        bs2_ref[...] = bias_two

    @pl.when(img > 0)
    def _():
        acc1[...] += d_one
        acc2[...] += d_two
        bs1_ref[...] += bias_one
        bs2_ref[...] += bias_two


def ffn_last_body(fsdp, r, *refs):
    sc, mid_ref, cot_ref, mod_ref, b1_ref, b2_ref = refs[:6]
    n = 2 * fsdp
    parts = refs[6 : 6 + n]
    (out_ref, gmid_ref, gmod_ref, bs1_ref, bs2_ref, keep, send, w1_ref, w2_ref, acc1, acc2) = refs[6 + n :]
    img = pl.program_id(0)

    @pl.when(img == 0)
    def _():
        assemble_ffn(sc, (parts[:fsdp], parts[fsdp:]), w1_ref, w2_ref, r, fsdp)

    mid = mid_ref[0]
    xhat, rstd = standardize(mid)
    normed = (xhat * (1.0 + mod_ref[0, 4:5]) + mod_ref[0, 3:4]).astype(bf16)
    pre = nn(normed, w1_ref[...]) + b1_ref[...]
    act = gelu(pre).astype(bf16)
    leaving = nn(act, w2_ref[...]) + b2_ref[...]
    out_ref[0] = (mid + mod_ref[0, 5:6] * leaving).astype(bf16)
    live = lax.broadcasted_iota(jnp.int32, (SLOTS, 1), 0) < sc[4 + img]
    g_y = jnp.where(live, cot_ref[0].astype(f32), 0.0)
    ffn_back_core(
        img, g_y, mid, xhat, rstd, normed, pre, act, leaving, mod_ref, w1_ref, w2_ref,
        gmid_ref, gmod_ref, bs1_ref, bs2_ref, acc1, acc2,
    )

    @pl.when(img == IMG - 1)
    def _():
        emit_ffn(sc, acc1, acc2, keep, send, r, fsdp)


def ffn_back_body(fsdp, r, *refs):
    sc, gy_ref, mid_ref, mod_ref, pre_ref, act_ref, leave_ref, w1_ref, w2_ref = refs[:9]
    (gmid_ref, gmod_ref, bs1_ref, bs2_ref, keep, send, acc1, acc2) = refs[9:]
    img = pl.program_id(0)
    mid = mid_ref[0]
    xhat, rstd = standardize(mid)
    normed = (xhat * (1.0 + mod_ref[0, 4:5]) + mod_ref[0, 3:4]).astype(bf16)
    ffn_back_core(
        img, gy_ref[0], mid, xhat, rstd, normed, pre_ref[0], act_ref[0], leave_ref[0], mod_ref,
        w1_ref, w2_ref, gmid_ref, gmod_ref, bs1_ref, bs2_ref, acc1, acc2,
    )

    @pl.when(img == IMG - 1)
    def _():
        emit_ffn(sc, acc1, acc2, keep, send, r, fsdp)


def attn_back_body(fsdp, r, *refs):
    (sc, gmid_ref, x_ref, mod_ref, qkv_ref, probs_ref, att_ref, branch_ref, w_ref) = refs[:9]
    (gx_ref, gmod_ref, bs_ref, keep, send, acc, gproj) = refs[9:]
    img = pl.program_id(0)
    gmid = gmid_ref[0]
    x = x_ref[0].astype(f32)
    xhat, rstd = standardize(x)
    normed = (xhat * (1.0 + mod_ref[0, 1:2]) + mod_ref[0, 0:1]).astype(bf16)
    g_branch = (mod_ref[0, 2:3] * gmid).astype(bf16)
    gmod_ref[0, 2:3] = colsum(gmid * branch_ref[0])
    bias_proj = colsum(g_branch.astype(f32))
    d_proj = tn(att_ref[0], g_branch)
    g_att = nt(g_branch, w_ref[:, 3 * D :]).astype(bf16)
    live = lax.broadcasted_iota(jnp.int32, (1, SLOTS), 1) < sc[4 + img]
    low_half = half_lane()
    qkv = qkv_ref[0]
    for p in range(3):
        lanes = slice(2 * HEAD_DIM * p, 2 * HEAD_DIM * (p + 1))
        q = qkv[:, : D][:, lanes]
        k = qkv[:, D : 2 * D][:, lanes]
        v = qkv[:, 2 * D :][:, lanes]
        ga = g_att[:, lanes]
        gq, gk, gv = [], [], []
        for h in range(2):
            gam = jnp.where(low_half == (h == 0), ga, jnp.zeros_like(ga))
            g_probs = nt(gam, v)
            probs = probs_ref[0, 2 * p + h]
            row = jnp.sum(g_probs * probs, axis=-1, keepdims=True)
            g_s = probs * (g_probs - row)
            g_s = jnp.where(live, g_s, 0.0).astype(bf16) * jnp.asarray(HEAD_DIM ** (-0.5), bf16)
            gq.append(nn(g_s, k))
            gk.append(tn(g_s, q))
            gv.append(tn(probs.astype(bf16), ga))
        for t, pair in enumerate((gq, gk, gv)):
            at = slice(t * D + 2 * HEAD_DIM * p, t * D + 2 * HEAD_DIM * (p + 1))
            gproj[:, at] = jnp.where(low_half, pair[0], pair[1]).astype(bf16)
    gp = gproj[...]
    bias_qkv = colsum(gp.astype(f32))
    d_qkv = tn(normed, gp)
    g_n = nt(gp, w_ref[:, : 3 * D])
    gmod_ref[0, 0:1] = colsum(g_n)
    gmod_ref[0, 1:2] = colsum(g_n * xhat)
    gx_ref[0] = gmid + norm_back(g_n, xhat, rstd, mod_ref[0, 1:2])

    @pl.when(img == 0)
    def _():
        acc[:, : 3 * D] = d_qkv
        acc[:, 3 * D :] = d_proj
        bs_ref[:, : 3 * D] = bias_qkv
        bs_ref[:, 3 * D :] = bias_proj

    @pl.when(img > 0)
    def _():
        acc[:, : 3 * D] += d_qkv
        acc[:, 3 * D :] += d_proj
        bs_ref[:, : 3 * D] += bias_qkv
        bs_ref[:, 3 * D :] += bias_proj

    @pl.when(img == IMG - 1)
    def _():
        emit_attn(sc, acc, keep, send, r, fsdp)


def per_image(*tail):
    return pl.BlockSpec((1, *tail), lambda i, s: (i, *([0] * len(tail))))


def whole(*shape):
    return pl.BlockSpec(shape, lambda i, s: (0,) * len(shape))


def shape_of(dims, dt):
    return jax.ShapeDtypeStruct(dims, dt)


def image_call(body, sc, ins, in_specs, outs, scratch=(), flops=0, moved=0):
    return pl.pallas_call(
        body,
        out_shape=[o[0] for o in outs],
        grid_spec=pltpu.PrefetchScalarGridSpec(
            num_scalar_prefetch=1,
            grid=(IMG,),
            in_specs=in_specs,
            out_specs=[o[1] for o in outs],
            scratch_shapes=list(scratch),
        ),
        compiler_params=pltpu.CompilerParams(
            dimension_semantics=("arbitrary",), vmem_limit_bytes=VMEM_BYTES
        ),
        cost_estimate=pl.CostEstimate(flops=flops, bytes_accessed=moved, transcendentals=0),
    )(sc, *ins)


ROW = lambda dt, w=D: (shape_of((IMG, SLOTS, w), dt), per_image(SLOTS, w))


def attn_forward(sc, x, mod, bias, parts, r, fsdp):
    flat = [*parts[0], *parts[1]]
    return image_call(
        partial(attn_forward_body, fsdp, r),
        sc,
        [x, mod, bias, *flat],
        [per_image(SLOTS, D), per_image(6, D), whole(1, 4 * D), *[whole(2, 1, r, D)] * len(flat)],
        [
            ROW(f32),
            ROW(bf16, 3 * D),
            (shape_of((IMG, HEADS, SLOTS, SLOTS), f32), per_image(HEADS, SLOTS, SLOTS)),
            ROW(bf16),
            ROW(f32),
            (shape_of((D, 4 * D), bf16), whole(D, 4 * D)),
        ],
        flops=3 * 10**9,
        moved=16 * 10**6,
    )


def ffn_forward(sc, mid, mod, b1, b2, parts, r, fsdp):
    flat = [*parts[0], *parts[1]]
    return image_call(
        partial(ffn_forward_body, fsdp, r),
        sc,
        [mid, mod, b1, b2, *flat],
        [per_image(SLOTS, D), per_image(6, D), whole(1, FF), whole(1, D), *[whole(2, 2, r, D)] * len(flat)],
        [
            ROW(f32),
            ROW(f32, FF),
            ROW(bf16, FF),
            ROW(f32),
            (shape_of((D, FF), bf16), whole(D, FF)),
            (shape_of((FF, D), bf16), whole(FF, D)),
        ],
        flops=3 * 10**9,
        moved=16 * 10**6,
    )


def grad_outs(fsdp, m, r):
    return [
        (shape_of((fsdp, 2, m, r, D), f32), whole(fsdp, 2, m, r, D)),
        (shape_of((fsdp, 2, m, r, D), bf16), whole(fsdp, 2, m, r, D)),
    ]


def ffn_back_outs(fsdp, r):
    return [
        ROW(f32),
        (shape_of((IMG, 3, D), f32), per_image(3, D)),
        (shape_of((1, FF), f32), whole(1, FF)),
        (shape_of((1, D), f32), whole(1, D)),
        *grad_outs(fsdp, 2, r),
    ]


FFN_ACC = [pltpu.VMEM((D, FF), f32), pltpu.VMEM((FF, D), f32)]


def ffn_last(sc, mid, cot, mod, b1, b2, parts, r, fsdp):
    flat = [*parts[0], *parts[1]]
    return image_call(
        partial(ffn_last_body, fsdp, r),
        sc,
        [mid, cot, mod, b1, b2, *flat],
        [
            per_image(SLOTS, D), per_image(SLOTS, D), per_image(6, D), whole(1, FF), whole(1, D),
            *[whole(2, 2, r, D)] * len(flat),
        ],
        [ROW(bf16), *ffn_back_outs(fsdp, r)],
        scratch=[pltpu.VMEM((D, FF), bf16), pltpu.VMEM((FF, D), bf16), *FFN_ACC],
        flops=8 * 10**9,
        moved=16 * 10**6,
    )


def ffn_back(sc, gy, mid, mod, pre, act, leaving, w1, w2, r, fsdp):
    return image_call(
        partial(ffn_back_body, fsdp, r),
        sc,
        [gy, mid, mod, pre, act, leaving, w1, w2],
        [
            per_image(SLOTS, D), per_image(SLOTS, D), per_image(6, D), per_image(SLOTS, FF),
            per_image(SLOTS, FF), per_image(SLOTS, D), whole(D, FF), whole(FF, D),
        ],
        ffn_back_outs(fsdp, r),
        scratch=FFN_ACC,
        flops=6 * 10**9,
        moved=16 * 10**6,
    )


def attn_back(sc, gmid, x, mod, qkv, probs, att, branch, w, r, fsdp):
    return image_call(
        partial(attn_back_body, fsdp, r),
        sc,
        [gmid, x, mod, qkv, probs, att, branch, w],
        [
            per_image(SLOTS, D), per_image(SLOTS, D), per_image(6, D), per_image(SLOTS, 3 * D),
            per_image(HEADS, SLOTS, SLOTS), per_image(SLOTS, D), per_image(SLOTS, D), whole(D, 4 * D),
        ],
        [
            ROW(f32),
            (shape_of((IMG, 3, D), f32), per_image(3, D)),
            (shape_of((1, 4 * D), f32), whole(1, 4 * D)),
            *grad_outs(fsdp, 1, r),
        ],
        scratch=[pltpu.VMEM((D, 4 * D), f32), pltpu.VMEM((SLOTS, 3 * D), bf16)],
        flops=6 * 10**9,
        moved=16 * 10**6,
    )


def prep_attn_body(r, sc, w_ref, a_ref, b_ref):
    c, y = sc[0], sc[1]
    for kc, out in enumerate((a_ref, b_ref)):
        for ky in range(2):
            out[ky, 0] = w_ref[0, :, at_lane((c ^ kc) * 2 + (y ^ ky))].astype(bf16)


def prep_ffn_body(r, sc, w1_ref, w2_ref, a_ref, b_ref):
    c, y = sc[0], sc[1]
    for kc, out in enumerate((a_ref, b_ref)):
        for cb in range(2):

            @pl.when((c ^ kc) == cb)
            def _(out=out, cb=cb):
                for ky in range(2):
                    for i in range(2):
                        pos = (y ^ ky) * 2 + i
                        if cb == 0:
                            out[ky, i] = w1_ref[0, :, at_lane(pos)].astype(bf16)
                        else:
                            out[ky, i] = w2_ref[0, at_row(pos, r), :].astype(bf16)


def prep_call(body, sc, ins, in_specs, m, r):
    out = shape_of((2, m, r, D), bf16)
    spec = whole(2, m, r, D)
    return pl.pallas_call(
        body,
        out_shape=[out, out],
        grid_spec=pltpu.PrefetchScalarGridSpec(
            num_scalar_prefetch=1, grid=(1,), in_specs=in_specs, out_specs=[spec, spec]
        ),
        compiler_params=pltpu.CompilerParams(
            dimension_semantics=("arbitrary",), vmem_limit_bytes=VMEM_BYTES
        ),
        cost_estimate=pl.CostEstimate(flops=0, bytes_accessed=4 * 10**6, transcendentals=0),
    )(sc, *ins)


def prep_attn(sc, entry, layer, r):
    spec = pl.BlockSpec((1, r, 4 * D), lambda i, s: (layer, 0, 0))
    return prep_call(partial(prep_attn_body, r), sc, [entry], [spec], 1, r)


def prep_ffn(sc, entry, exit_m, layer, r):
    specs = [
        pl.BlockSpec((1, r, FF), lambda i, s: (layer, 0, 1)),
        pl.BlockSpec((1, 4 * r, D), lambda i, s: (layer, 0, 0)),
    ]
    return prep_call(partial(prep_ffn_body, r), sc, [entry, exit_m], specs, 2, r)


def mod_body(w_ref, cond_ref, out_ref):
    out_ref[0] = nn(cond_ref[...], w_ref[0].astype(bf16))


def mod_partial(entry, cond_rows, r):
    rows = cond_rows.shape[0]
    return pl.pallas_call(
        mod_body,
        out_shape=shape_of((LAYERS, rows, ADA), f32),
        grid=(LAYERS, 3),
        in_specs=[
            pl.BlockSpec((1, r, 2 * D), lambda l, k: (l, 0, 4 + k)),
            pl.BlockSpec((rows, r), lambda l, k: (0, 0)),
        ],
        out_specs=pl.BlockSpec((1, rows, 2 * D), lambda l, k: (l, 0, k)),
        compiler_params=pltpu.CompilerParams(vmem_limit_bytes=VMEM_BYTES),
    )(entry, cond_rows)


def cond_back_body(g_ref, w_ref, out_ref):
    val = nt(g_ref[...], w_ref[0].astype(bf16))
    first = jnp.logical_and(pl.program_id(0) == 0, pl.program_id(1) == 0)

    @pl.when(first)
    def _():
        out_ref[...] = val

    @pl.when(jnp.logical_not(first))
    def _():
        out_ref[...] += val


def cond_back(g_rows, entry, r):
    rows = g_rows.shape[0]
    return pl.pallas_call(
        cond_back_body,
        out_shape=shape_of((rows, r), f32),
        grid=(LAYERS, 3),
        in_specs=[
            pl.BlockSpec((rows, 2 * D), lambda l, k: (0, l * 3 + k)),
            pl.BlockSpec((1, r, 2 * D), lambda l, k: (l, 0, 4 + k)),
        ],
        out_specs=pl.BlockSpec((rows, r), lambda l, k: (0, 0)),
        compiler_params=pltpu.CompilerParams(vmem_limit_bytes=VMEM_BYTES),
    )(g_rows, entry)


def adam_math(gradient, master, moment, square):
    new_moment = beta_one * moment + (1.0 - beta_one) * gradient
    new_square = beta_two * square + (1.0 - beta_two) * gradient * gradient
    first_fix = 1.0 - beta_one**STEP
    second_fix = 1.0 - beta_two**STEP
    direction = (
        new_moment / first_fix / (jnp.sqrt(new_square / second_fix) + adam_eps)
        + decay_rate * master
    )
    new_master = master - learn_rate * direction
    return new_moment, new_square, new_master


def adam_store(grad, ins, outs):
    moment, square, master = adam_math(grad, ins[0][0], ins[1][0], ins[2][0])
    outs[0][0] = grad
    outs[1][0] = moment
    outs[2][0] = square
    outs[3][0] = master
    outs[4][0] = master.astype(bf16)


def adam_block_body(pick, scale, n_grad, sc, *refs):
    grads, ins, outs = refs[:n_grad], refs[n_grad : n_grad + 3], refs[-5:]
    kc, ky, i = pick(pl.program_id(0), sc)
    low = jnp.where(ky == 0, grads[0][i], grads[1][i])
    high = jnp.where(ky == 0, grads[2][i], grads[3][i])
    adam_store(jnp.where(kc == 0, low, high).astype(f32) * scale, ins, outs)


def adam_ada_body(scale, *refs):
    cond, gmod, ins, outs = refs[0], refs[1], refs[2:5], refs[-5:]
    adam_store(tn(cond[...], gmod[...]) * scale, ins, outs)


def adam_outs(like):
    return [shape_of(like.shape, f32)] * 4 + [shape_of(like.shape, bf16)]


def adam_unit(sc, grads, states, layer, at, steps, pick, scale, prev, r):
    spec = pl.BlockSpec((1, r, D), lambda b, s: (layer, *at(b)))
    grad_specs = [pl.BlockSpec(g.shape, lambda b, s: (0, 0, 0)) for g in grads]
    extra = [] if prev is None else list(prev)
    return pl.pallas_call(
        partial(adam_block_body, pick, scale, len(grads)),
        out_shape=adam_outs(states[0]),
        grid_spec=pltpu.PrefetchScalarGridSpec(
            num_scalar_prefetch=1,
            grid=(steps,),
            in_specs=[*grad_specs, *[spec] * 3, *[pl.BlockSpec(memory_space=pl.ANY)] * len(extra)],
            out_specs=[spec] * 5,
        ),
        input_output_aliases={1 + len(grads) + 3 + k: k for k in range(len(extra))},
        compiler_params=pltpu.CompilerParams(
            dimension_semantics=("arbitrary",), vmem_limit_bytes=VMEM_BYTES
        ),
        cost_estimate=pl.CostEstimate(flops=0, bytes_accessed=steps * r * D * 30, transcendentals=0),
    )(sc, *grads, *states, *extra)


def adam_ada(cond_own, gmod_all, states, scale, prev, r):
    spec = pl.BlockSpec((1, r, D), lambda l, k: (l, 0, 8 + k))
    rows = cond_own.shape[0]
    extra = [] if prev is None else list(prev)
    return pl.pallas_call(
        partial(adam_ada_body, scale),
        out_shape=adam_outs(states[0]),
        grid=(LAYERS, 6),
        in_specs=[
            pl.BlockSpec((rows, r), lambda l, k: (0, 0)),
            pl.BlockSpec((rows, D), lambda l, k: (0, l * 6 + k)),
            *[spec] * 3,
            *[pl.BlockSpec(memory_space=pl.ANY)] * len(extra),
        ],
        out_specs=[spec] * 5,
        input_output_aliases={5 + k: k for k in range(len(extra))},
        compiler_params=pltpu.CompilerParams(vmem_limit_bytes=VMEM_BYTES),
        cost_estimate=pl.CostEstimate(flops=0, bytes_accessed=12 * r * D * 30, transcendentals=0),
    )(cond_own, gmod_all, *states, *extra)


def swap(v, axis, bit):
    size = lax.axis_size(axis)
    return lax.ppermute(v, axis, [(i, i ^ bit) for i in range(size)])


def spread_fsdp(v, fsdp):
    held = [v]
    bit = 1
    while bit < fsdp:
        held = held + [swap(a, "fsdp", bit) for a in held]
        bit *= 2
    return held


def gather_weights(own, fsdp):
    mine = spread_fsdp(own[0], fsdp)
    other = [own[1]] + [swap(a, "dp", 1) for a in mine[1:]]
    return mine, other


def low_round(v):
    return lax.reduce_precision(v, 8, 7)


def reduce_unit(keep, send, dp, fsdp):
    total = keep + swap(send, "dp", 1).astype(f32)
    half = fsdp // 2
    while half:
        total = total[:half] + swap(total[half:].astype(bf16), "fsdp", half).astype(f32)
        half //= 2
    total = total[0]
    total = total[0] + swap(total[1].astype(bf16), "dp", 2).astype(f32)
    bit = 4
    while bit < dp:
        low = low_round(total)
        total = low + swap(low.astype(bf16), "dp", bit).astype(f32)
        bit *= 2
    low = total.astype(bf16)
    mine = (low, swap(low, "dp", 2))
    return (*mine, *[swap(a, "dp", 1) for a in mine])


def join(v, axis, bit):
    got = swap(v, axis, bit)
    upper = (lax.axis_index(axis) & bit) != 0
    return jnp.stack([jnp.where(upper, got, v), jnp.where(upper, v, got)], axis=0)


def per_device(
    tokens, condition, image_grid, image_counts, cotangent,
    entry_master, exit_master, bias_master,
    entry_moment, exit_moment, bias_moment,
    entry_square, exit_square, bias_square,
):
    dp, fsdp = lax.axis_size("dp"), lax.axis_size("fsdp")
    r = D // fsdp
    dp_at, f_at = lax.axis_index("dp"), lax.axis_index("fsdp")
    counted = jnp.where(
        jnp.arange(IMG) < image_counts[0], image_grid[:, 0] * image_grid[:, 1], 0
    ).astype(jnp.int32)
    sc = jnp.concatenate(
        [jnp.stack([dp_at & 1, (dp_at >> 1) & 1, f_at, f_at]).astype(jnp.int32), counted]
    )
    scale = (IMG * SLOTS * dp * fsdp) ** (-0.5)

    own_attn = [prep_attn(sc, entry_master, layer, r) for layer in range(LAYERS)]
    own_ffn = [prep_ffn(sc, entry_master, exit_master, layer, r) for layer in range(LAYERS)]
    cond_float = condition.astype(f32)
    cond_act = jax.nn.silu(cond_float).astype(bf16)
    cond_rel = spread_fsdp(cond_act, fsdp)
    bias_low = bias_master.astype(bf16)
    bias_all = bias_low[None]
    bit = 1
    while bit < fsdp:
        bias_all = join(bias_all, "fsdp", bit).reshape(-1, *bias_low.shape)
        bit *= 2
    bias_all = jnp.moveaxis(bias_all, 0, 1).reshape(LAYERS, -1).astype(f32)
    cond_rows = jnp.concatenate(
        [lax.dynamic_slice_in_dim(v, f_at * r, r, 1) for v in cond_rel], axis=0
    )
    partial_mod = mod_partial(entry_master, cond_rows, r).reshape(LAYERS, fsdp, IMG, ADA)
    mod = partial_mod[:, 0]
    for j in range(1, fsdp):
        mod = mod + swap(partial_mod[:, j], "fsdp", j)
    hidden_end, ada_end = 4 * D + FF, 10 * D + FF
    mod = mod + bias_all[:, None, hidden_end:ada_end]
    mods = mod.reshape(LAYERS, IMG, 6, D)
    b_attn = [bias_all[l : l + 1, : 4 * D] for l in range(LAYERS)]
    b_one = [bias_all[l : l + 1, 4 * D : hidden_end] for l in range(LAYERS)]
    b_two = [bias_all[l : l + 1, ada_end:] for l in range(LAYERS)]

    w_attn0 = gather_weights(own_attn[0], fsdp)
    w_ffn0 = gather_weights(own_ffn[0], fsdp)
    w_attn1 = gather_weights(own_attn[1], fsdp)
    w_ffn1 = gather_weights(own_ffn[1], fsdp)

    mid0, qkv0, probs0, att0, br0, wa0 = attn_forward(sc, tokens, mods[0], b_attn[0], w_attn0, r, fsdp)
    x1, pre0, act0, lv0, w10, w20 = ffn_forward(sc, mid0, mods[0], b_one[0], b_two[0], w_ffn0, r, fsdp)
    mid1, qkv1, probs1, att1, br1, wa1 = attn_forward(sc, x1, mods[1], b_attn[1], w_attn1, r, fsdp)
    block_output, gmid1, gm1b, bs1_1, bs1_2, keep, send = ffn_last(
        sc, mid1, cotangent, mods[1], b_one[1], b_two[1], w_ffn1, r, fsdp
    )
    g_ffn1 = reduce_unit(keep, send, dp, fsdp)
    gx1, gm1a, bs1_a, keep, send = attn_back(
        sc, gmid1, x1, mods[1], qkv1, probs1, att1, br1, wa1, r, fsdp
    )
    g_attn1 = reduce_unit(keep, send, dp, fsdp)
    gmid0, gm0b, bs0_1, bs0_2, keep, send = ffn_back(
        sc, gx1, mid0, mods[0], pre0, act0, lv0, w10, w20, r, fsdp
    )
    g_ffn0 = reduce_unit(keep, send, dp, fsdp)
    grad_tokens, gm0a, bs0_a, keep, send = attn_back(
        sc, gmid0, tokens, mods[0], qkv0, probs0, att0, br0, wa0, r, fsdp
    )
    g_attn0 = reduce_unit(keep, send, dp, fsdp)

    g_mod = jnp.concatenate([gm0a, gm0b, gm1a, gm1b], axis=1).astype(bf16).reshape(IMG, LAYERS * ADA)
    bias_sum = jnp.concatenate([bs0_a, bs0_1, bs0_2, bs1_a, bs1_1, bs1_2], axis=1)
    rows = g_mod[None]
    conds = cond_act[None]
    bit = 1
    while bit < fsdp:
        rows = join(rows, "fsdp", bit).reshape(-1, IMG, LAYERS * ADA)
        conds = join(conds, "fsdp", bit).reshape(-1, IMG, D)
        bias_sum = bias_sum + swap(bias_sum, "fsdp", bit)
        bit *= 2
    back = cond_back(rows.reshape(-1, LAYERS * ADA), entry_master, r).reshape(fsdp, IMG, r)
    pieces = [lax.dynamic_index_in_dim(back, f_at, 0, keepdims=False)]
    for j in range(1, fsdp):
        pieces.append(swap(lax.dynamic_index_in_dim(back, f_at ^ j, 0, keepdims=False), "fsdp", j))
    g_cond = jnp.zeros((fsdp, IMG, r), f32)
    for j in range(fsdp):
        g_cond = lax.dynamic_update_index_in_dim(g_cond, pieces[j], f_at ^ j, 0)
    g_cond = jnp.moveaxis(g_cond, 0, 1).reshape(IMG, D)
    grad_condition = jax.vjp(jax.nn.silu, cond_float)[1](g_cond)[0]
    bit = dp // 2
    while bit:
        rows = join(rows, "dp", bit).reshape(-1, IMG, LAYERS * ADA)
        conds = join(conds, "dp", bit).reshape(-1, IMG, D)
        bias_sum = bias_sum + swap(bias_sum, "dp", bit)
        bit //= 2
    rows = rows.reshape(-1, LAYERS * ADA)
    cond_own = lax.dynamic_slice_in_dim(conds.reshape(-1, D), f_at * r, r, 1)
    ada_bias = jnp.sum(rows.astype(f32), axis=0).reshape(LAYERS, ADA)
    bias_sum = bias_sum.reshape(LAYERS, -1)
    bias_sum = jnp.concatenate([bias_sum[:, :hidden_end], ada_bias, bias_sum[:, hidden_end:]], axis=1)
    width = bias_master.shape[1]
    bias_grad = lax.dynamic_slice_in_dim(bias_sum, f_at * width, width, 1) * scale
    exit_bias_grad = lax.dynamic_slice_in_dim(bias_sum[:, ada_end:], f_at * r, r, 1) * scale
    bias_moment_new, bias_square_new, bias_master_new = adam_math(
        bias_grad, bias_master, bias_moment, bias_square
    )

    entry = (entry_master, entry_moment, entry_square)
    exits = (exit_master, exit_moment, exit_square)

    def pick_attn(b, s):
        return s[0] ^ (b >> 1), s[1] ^ (b & 1), 0

    def pick_one(b, s):
        return s[0], s[1] ^ (b >> 1), b & 1

    def pick_two(b, s):
        return s[0] ^ 1, s[1] ^ (b >> 1), b & 1

    e = adam_unit(sc, g_ffn1, entry, 1, lambda b: (0, 4 + b), 4, pick_one, scale, None, r)
    x = adam_unit(sc, g_ffn1, exits, 1, lambda b: (b, 0), 4, pick_two, scale, None, r)
    e = adam_unit(sc, g_attn1, entry, 1, lambda b: (0, b), 4, pick_attn, scale, e, r)
    e = adam_ada(cond_own, rows, entry, scale, e, r)
    e = adam_unit(sc, g_ffn0, entry, 0, lambda b: (0, 4 + b), 4, pick_one, scale, e, r)
    x = adam_unit(sc, g_ffn0, exits, 0, lambda b: (b, 0), 4, pick_two, scale, x, r)
    e = adam_unit(sc, g_attn0, entry, 0, lambda b: (0, b), 4, pick_attn, scale, e, r)
    return (
        block_output, grad_tokens, grad_condition,
        *e, *x,
        bias_grad, bias_moment_new, bias_square_new, bias_master_new,
        bias_master_new.astype(bf16), exit_bias_grad,
    )


def solution(mesh):
    rows = P(("dp", "fsdp"), None, None)
    flat = P(("dp", "fsdp"), None)
    mat = P(None, "fsdp", None)
    vec = P(None, "fsdp")
    return jax.shard_map(
        per_device,
        mesh=mesh,
        in_specs=(rows, flat, flat, P(("dp", "fsdp")), rows, mat, mat, vec, mat, mat, vec, mat, mat, vec),
        out_specs=(rows, rows, flat, *[mat] * 10, *[vec] * 6),
        check_vma=False,
    )
```

```python
from functools import partial

import jax
import jax.numpy as jnp
from jax import lax
from jax.experimental import pallas as pl
from jax.experimental.pallas import tpu as pltpu
from jax.sharding import PartitionSpec as P

D = 384
HEADS = 6
HEAD_DIM = 64
FF = 1536
LAYERS = 2
IMG = 4
STEP = 4
SLOTS = 256
ADA = 6 * D

eps_norm = 1e-06
neg_big = -1e30
beta_one = 0.5
beta_two = 0.6
adam_eps = 1e-08
learn_rate = 0.02
decay_rate = 0.1

f32 = jnp.float32
bf16 = jnp.bfloat16
VMEM_BYTES = 56 * 1024 * 1024
VMEM_IMAGE = 30 * 1024 * 1024


def nn(a, b):
    return lax.dot_general(a, b, (((1,), (0,)), ((), ())), preferred_element_type=f32)


def nt(a, b):
    return lax.dot_general(a, b, (((1,), (1,)), ((), ())), preferred_element_type=f32)


def tn(a, b):
    return lax.dot_general(a, b, (((0,), (0,)), ((), ())), preferred_element_type=f32)


def standardize(x):
    mean = jnp.mean(x, axis=-1, keepdims=True)
    cen = x - mean
    var = jnp.mean(cen * cen, axis=-1, keepdims=True)
    rstd = lax.rsqrt(var + eps_norm)
    return cen * rstd, rstd


def norm_back(g, xhat, rstd, scale):
    t = g * (1.0 + scale)
    mean_t = jnp.mean(t, axis=-1, keepdims=True)
    mean_tx = jnp.mean(t * xhat, axis=-1, keepdims=True)
    return (t - mean_t - xhat * mean_tx) * rstd


def colsum(x):
    return jnp.sum(x, axis=0, keepdims=True)


def at_lane(i):
    return pl.ds(pl.multiple_of(i * D, 128), D)


def at_row(i, r):
    return pl.ds(pl.multiple_of(i * r, 16), r)


def place_columns(sc, own, mine, other, w_ref, r, fsdp):
    half = w_ref.shape[1] // 2
    c, f = sc[0], sc[2]
    w_ref[at_row(f, r), :] = own[0].astype(bf16)
    for j in range(1, fsdp):
        for kc, part in ((0, mine), (1, other)):
            w_ref[at_row(f ^ j, r), pl.ds(pl.multiple_of((c ^ kc) * half, 128), half)] = part[j - 1][...]


def place_rows(sc, own, mine, other, w_ref, r, fsdp):
    c, f = sc[0], sc[2]
    w_ref[at_row(f, 4 * r), :] = own[0].astype(bf16)
    for j in range(1, fsdp):
        for kc, part in ((0, mine), (1, other)):
            w_ref[at_row((f ^ j) * 2 + (c ^ kc), 2 * r), :] = part[j - 1][...]


def emit_attn(sc, acc, keep, send, r, fsdp):
    c, y, f = sc[0], sc[1], sc[2]
    for j in range(fsdp):
        for ky in range(2):
            for kc in range(2):
                blk = acc[at_row(f ^ j, r), at_lane((c ^ kc) * 2 + (y ^ ky))]
                if kc == 0:
                    keep[j, ky, 0] = blk
                else:
                    send[j, ky, 0] = blk.astype(bf16)


def emit_ffn(sc, acc1, acc2, keep, send, r, fsdp):
    c, y, f = sc[0], sc[1], sc[2]
    for kc in range(2):
        for cb in range(2):

            @pl.when((c ^ kc) == cb)
            def _(kc=kc, cb=cb):
                for j in range(fsdp):
                    for ky in range(2):
                        for i in range(2):
                            pos = (y ^ ky) * 2 + i
                            if cb == 0:
                                blk = acc1[at_row(f ^ j, r), at_lane(pos)]
                            else:
                                blk = acc2[at_row((f ^ j) * 4 + pos, r), :]
                            if kc == 0:
                                keep[j, ky, i] = blk
                            else:
                                send[j, ky, i] = blk.astype(bf16)


def half_lane():
    return lax.broadcasted_iota(jnp.int32, (1, 2 * HEAD_DIM), 1) < HEAD_DIM


def pair_lanes(qkv, third, p):
    start = third * D + 2 * HEAD_DIM * p
    return qkv[:, start : start + 2 * HEAD_DIM]


def stack_pair(v):
    low_half = half_lane()
    none = jnp.zeros_like(v)
    return jnp.concatenate([jnp.where(low_half, v, none), jnp.where(low_half, none, v)], axis=0)


def pair_probs(qkv, live_slots):
    live = lax.broadcasted_iota(jnp.int32, (1, 2 * SLOTS), 1) & (SLOTS - 1)
    live = live < live_slots
    scores = []
    for p in range(3):
        q = pair_lanes(qkv, 0, p) * jnp.asarray(HEAD_DIM ** (-0.5), bf16)
        scores.append(jnp.where(live, nt(q, stack_pair(pair_lanes(qkv, 1, p))), neg_big))
    out = []
    for s in scores:
        heads = []
        for h in range(2):
            sh = s[:, h * SLOTS : (h + 1) * SLOTS]
            e = jnp.exp(sh - jnp.max(sh, axis=-1, keepdims=True))
            heads.append(e * (1.0 / jnp.sum(e, axis=-1, keepdims=True)))
        out.append(jnp.concatenate(heads, axis=1))
    return out


def flat(v):
    return v.reshape(v.shape[0] * v.shape[1], v.shape[2])


def deep(v):
    return v.reshape(v.shape[0] // SLOTS, SLOTS, v.shape[1])


def slotsum(v):
    return jnp.sum(v, axis=1, keepdims=True)


def mod_part(mod_ref, k, group):
    if group == IMG:
        return mod_ref[0, :, k * D : (k + 1) * D][:, None, :]
    first = pl.program_id(0) * group
    rows = [mod_ref[0, pl.ds(first + i, 1), k * D : (k + 1) * D][None] for i in range(group)]
    return rows[0] if group == 1 else jnp.concatenate(rows, axis=0)


def modulated(x, mod_ref, k):
    xhat, rstd = standardize(x)
    group = x.shape[0]
    normed = (xhat * (1.0 + mod_part(mod_ref, k + 1, group)) + mod_part(mod_ref, k, group)).astype(bf16)
    return xhat, rstd, flat(normed)


def attn_forward_body(group, fsdp, r, *refs):
    sc, x_ref, mod_ref, bias_ref, own = refs[:5]
    n = fsdp - 1
    mine, other = refs[5 : 5 + n], refs[5 + n : 5 + 2 * n]
    mid_ref, qkv_ref, att_ref, w_ref = refs[-4:]
    bias_ref = bias_ref.at[0]
    step = pl.program_id(0)

    @pl.when(step == 0)
    def _():
        place_columns(sc, own, mine, other, w_ref, r, fsdp)

    x = x_ref[...].astype(f32)
    _, _, normed = modulated(x, mod_ref, 0)
    qkv_all = (nn(normed, w_ref[:, : 3 * D]) + bias_ref[:, : 3 * D]).astype(bf16)
    qkv_ref[...] = deep(qkv_all)
    for i in range(group):
        qkv = qkv_all[i * SLOTS : (i + 1) * SLOTS]
        for p, probs in enumerate(pair_probs(qkv, sc[4 + step * group + i])):
            att = nn(probs.astype(bf16), stack_pair(pair_lanes(qkv, 2, p)))
            att_ref[i, :, 2 * HEAD_DIM * p : 2 * HEAD_DIM * (p + 1)] = att.astype(bf16)
    branch = nn(flat(att_ref[...]), w_ref[:, 3 * D :]) + bias_ref[:, 3 * D :]
    mid_ref[...] = x + mod_part(mod_ref, 2, group) * deep(branch)


def gelu(v):
    return v * (0.5 + 0.5 * jnp.tanh(v * (0.7978845608 + (0.7978845608 * 0.044715) * (v * v))))


def gelu_both(v):
    sq = v * v
    half = 0.5 + 0.5 * jnp.tanh(v * (0.7978845608 + (0.7978845608 * 0.044715) * sq))
    slope = 2.0 * 0.7978845608 + (6.0 * 0.044715 * 0.7978845608) * sq
    return v * half, half + v * slope * (half - half * half)


def ffn_forward_body(group, fsdp, r, *refs):
    sc, mid_ref, mod_ref, b1_ref, b2_ref, own1, own2 = refs[:7]
    n = fsdp - 1
    parts = [refs[7 + k * n : 7 + (k + 1) * n] for k in range(4)]
    y_ref, leave_ref, w1_ref, w2_ref = refs[-4:]
    b1_ref, b2_ref = b1_ref.at[0], b2_ref.at[0]

    @pl.when(pl.program_id(0) == 0)
    def _():
        place_columns(sc, own1, parts[0], parts[1], w1_ref, r, fsdp)
        place_rows(sc, own2, parts[2], parts[3], w2_ref, r, fsdp)

    mid = mid_ref[...]
    _, _, normed = modulated(mid, mod_ref, 3)
    act = gelu(nn(normed, w1_ref[...]) + b1_ref[...]).astype(bf16)
    leaving = deep(nn(act, w2_ref[...]) + b2_ref[...])
    leave_ref[...] = leaving
    y_ref[...] = mid + mod_part(mod_ref, 5, group) * leaving


def accumulate(ref, val):
    @pl.when(pl.program_id(0) == 0)
    def _():
        ref[...] = val

    @pl.when(pl.program_id(0) > 0)
    def _():
        ref[...] += val


def ffn_back_core(
    group, g_y, xhat, rstd, normed, slope, act, leaving, mod_ref, w1, w2,
    gmid_ref, gmod_ref, bs1_ref, bs2_ref, held,
):
    normed_all, pre_all, act_all, leave_all = held
    rows = group * SLOTS
    at = pl.ds(pl.multiple_of(pl.program_id(0) * rows, rows), rows)
    g_leave = flat((mod_part(mod_ref, 5, group) * g_y).astype(bf16))
    gmod_ref[:, 2:3] = slotsum(g_y * leaving)
    g_pre = (slope * nt(g_leave, w2[...])).astype(bf16)
    normed_all[at, :] = normed
    act_all[at, :] = act
    leave_all[at, :] = g_leave
    pre_all[at, :] = g_pre
    g_n = deep(nt(g_pre, w1[...]))
    gmod_ref[:, 0:1] = slotsum(g_n)
    gmod_ref[:, 1:2] = slotsum(g_n * xhat)
    gmid_ref[...] = g_y + norm_back(g_n, xhat, rstd, mod_part(mod_ref, 4, group))
    accumulate(bs1_ref, colsum(g_pre.astype(f32)))
    accumulate(bs2_ref, colsum(g_leave.astype(f32)))


def ffn_weight_grads(sc, held, acc1, acc2, keep, send, r, fsdp):
    normed_all, pre_all, act_all, leave_all = held
    acc1[...] = tn(normed_all[...], pre_all[...])
    acc2[...] = tn(act_all[...], leave_all[...])
    emit_ffn(sc, acc1, acc2, keep, send, r, fsdp)


def ffn_last_body(group, fsdp, r, *refs):
    sc, mid_ref, cot_ref, mod_ref, b1_ref, b2_ref, own1, own2 = refs[:8]
    n = fsdp - 1
    parts = [refs[8 + k * n : 8 + (k + 1) * n] for k in range(4)]
    (out_ref, gmid_ref, gmod_ref, bs1_ref, bs2_ref, keep, send, w1_ref, w2_ref, acc1, acc2, *held) = refs[-15:]
    b1_ref, b2_ref = b1_ref.at[0], b2_ref.at[0]
    step = pl.program_id(0)

    @pl.when(step == 0)
    def _():
        place_columns(sc, own1, parts[0], parts[1], w1_ref, r, fsdp)
        place_rows(sc, own2, parts[2], parts[3], w2_ref, r, fsdp)

    mid = mid_ref[...]
    xhat, rstd, normed = modulated(mid, mod_ref, 3)
    act, slope = gelu_both(nn(normed, w1_ref[...]) + b1_ref[...])
    act = act.astype(bf16)
    leaving = deep(nn(act, w2_ref[...]) + b2_ref[...])
    out_ref[...] = (mid + mod_part(mod_ref, 5, group) * leaving).astype(bf16)
    slots = lax.broadcasted_iota(jnp.int32, (1, SLOTS, 1), 1)
    g_y = jnp.concatenate(
        [
            jnp.where(slots < sc[4 + step * group + i], cot_ref[i : i + 1].astype(f32), 0.0)
            for i in range(group)
        ],
        axis=0,
    )
    ffn_back_core(
        group, g_y, xhat, rstd, normed, slope, act, leaving, mod_ref, w1_ref, w2_ref,
        gmid_ref, gmod_ref, bs1_ref, bs2_ref, held,
    )

    @pl.when(step == IMG // group - 1)
    def _():
        ffn_weight_grads(sc, held, acc1, acc2, keep, send, r, fsdp)


def ffn_back_body(group, fsdp, r, *refs):
    sc, gy_ref, mid_ref, mod_ref, b1_ref, leave_ref, w1_ref, w2_ref = refs[:8]
    (gmid_ref, gmod_ref, bs1_ref, bs2_ref, keep, send, acc1, acc2, *held) = refs[-12:]
    xhat, rstd, normed = modulated(mid_ref[...], mod_ref, 3)
    act, slope = gelu_both(nn(normed, w1_ref[...]) + b1_ref[0])
    ffn_back_core(
        group, gy_ref[...], xhat, rstd, normed, slope, act.astype(bf16), leave_ref[...], mod_ref,
        w1_ref, w2_ref, gmid_ref, gmod_ref, bs1_ref, bs2_ref, held,
    )

    @pl.when(pl.program_id(0) == IMG // group - 1)
    def _():
        ffn_weight_grads(sc, held, acc1, acc2, keep, send, r, fsdp)


def attn_back_body(group, fsdp, r, *refs):
    (sc, gmid_ref, x_ref, mod_ref, bias_ref, qkv_ref, att_ref, w_ref) = refs[:8]
    (gx_ref, gmod_ref, bs_ref, keep, send, acc, normed_all, gproj_all, att_all, branch_all) = refs[-10:]
    bias_ref = bias_ref.at[0]
    step = pl.program_id(0)
    rows = group * SLOTS
    at = pl.ds(pl.multiple_of(step * rows, rows), rows)
    gmid = gmid_ref[...]
    att = flat(att_ref[...])
    g_branch = flat((mod_part(mod_ref, 2, group) * gmid).astype(bf16))
    g_att_all = nt(g_branch, w_ref[:, 3 * D :]).astype(bf16)
    low_half = half_lane()
    for i in range(group):
        qkv = qkv_ref[i]
        g_att = g_att_all[i * SLOTS : (i + 1) * SLOTS]
        live_slots = sc[4 + step * group + i]
        g_probs = [nt(pair_lanes(g_att, 0, p), stack_pair(pair_lanes(qkv, 2, p))) for p in range(3)]
        all_probs = pair_probs(qkv, live_slots)
        live = lax.broadcasted_iota(jnp.int32, (1, SLOTS), 1) < live_slots
        for p in range(3):
            q, k, ga = pair_lanes(qkv, 0, p), pair_lanes(qkv, 1, p), pair_lanes(g_att, 0, p)
            g_s = []
            for h in range(2):
                gp = g_probs[p][:, h * SLOTS : (h + 1) * SLOTS]
                probs = all_probs[p][:, h * SLOTS : (h + 1) * SLOTS]
                row = jnp.sum(gp * probs, axis=-1, keepdims=True)
                val = jnp.where(live, probs * (gp - row), 0.0)
                g_s.append(val.astype(bf16) * jnp.asarray(HEAD_DIM ** (-0.5), bf16))
            g_s = jnp.concatenate(g_s, axis=1)
            gq = nn(g_s, stack_pair(k))
            gk = tn(g_s, q)
            gv = tn(all_probs[p].astype(bf16), ga)
            gk = jnp.where(low_half, gk[:SLOTS], gk[SLOTS:])
            gv = jnp.where(low_half, gv[:SLOTS], gv[SLOTS:])
            here = pl.ds(pl.multiple_of(step * rows + i * SLOTS, SLOTS), SLOTS)
            for t, val in enumerate((gq, gk, gv)):
                lanes = slice(t * D + 2 * HEAD_DIM * p, t * D + 2 * HEAD_DIM * (p + 1))
                gproj_all[here, lanes] = val.astype(bf16)
    branch = deep(nn(att, w_ref[:, 3 * D :]) + bias_ref[:, 3 * D :])
    gmod_ref[:, 2:3] = slotsum(gmid * branch)
    xhat, rstd, normed = modulated(x_ref[...].astype(f32), mod_ref, 0)
    normed_all[at, :] = normed
    att_all[at, :] = att
    branch_all[at, :] = g_branch
    gp = gproj_all[at, :]
    g_n = deep(nt(gp, w_ref[:, : 3 * D]))
    gmod_ref[:, 0:1] = slotsum(g_n)
    gmod_ref[:, 1:2] = slotsum(g_n * xhat)
    gx_ref[...] = gmid + norm_back(g_n, xhat, rstd, mod_part(mod_ref, 1, group))
    accumulate(bs_ref, jnp.concatenate([colsum(gp.astype(f32)), colsum(g_branch.astype(f32))], axis=1))

    @pl.when(step == IMG // group - 1)
    def _():
        acc[:, : 3 * D] = tn(normed_all[...], gproj_all[...])
        acc[:, 3 * D :] = tn(att_all[...], branch_all[...])
        emit_attn(sc, acc, keep, send, r, fsdp)


GROUP = {"attn_forward": 1, "ffn_forward": 1, "ffn_last": 1, "ffn_back": 1, "attn_back": 1}


def per_image(g, *tail):
    return pl.BlockSpec((g, *tail), lambda i, s: (i, *([0] * len(tail))))


def whole(*shape):
    return pl.BlockSpec(shape, lambda i, s: (0,) * len(shape))


def shape_of(dims, dt):
    return jax.ShapeDtypeStruct(dims, dt)


ANY = pl.BlockSpec(memory_space=pl.ANY)


def in_hbm(v):
    return pltpu.with_memory_space_constraint(v, pltpu.HBM)


def in_vmem(v):
    return pltpu.with_memory_space_constraint(v, pltpu.VMEM)


def image_call(g, body, sc, ins, in_specs, outs, deps=(), scratch=(), flops=0, moved=0):
    return pl.pallas_call(
        body,
        out_shape=[o[0] for o in outs],
        grid_spec=pltpu.PrefetchScalarGridSpec(
            num_scalar_prefetch=1,
            grid=(IMG // g,),
            in_specs=[*in_specs, *[ANY] * len(deps)],
            out_specs=[o[1] for o in outs],
            scratch_shapes=list(scratch),
        ),
        compiler_params=pltpu.CompilerParams(
            dimension_semantics=("arbitrary",), vmem_limit_bytes=VMEM_IMAGE
        ),
        cost_estimate=pl.CostEstimate(flops=flops, bytes_accessed=moved, transcendentals=0),
    )(sc, *ins, *deps)


def mod_spec(g, layer):
    return pl.BlockSpec((1, IMG, ADA), lambda i, s: (layer, 0, 0))


def bias_spec(layer, width, k):
    return pl.BlockSpec((1, 1, width), lambda i, s: (layer, 0, k))


def own_spec(layer, rows, width, k):
    return pl.BlockSpec((1, rows, width), lambda i, s: (layer, 0, k))


ROW = lambda g, dt, w=D: (shape_of((IMG, SLOTS, w), dt), per_image(g, SLOTS, w))
HELD = lambda g, dt, w=D: (pltpu.VMEM((IMG, SLOTS, w), dt), per_image(g, SLOTS, w))


def attn_forward(sc, layer, x, mods, biases, entry, parts, deps, r, fsdp):
    pieces = [*parts[0], *parts[1]]
    g = GROUP["attn_forward"]
    return image_call(
        g,
        partial(attn_forward_body, g, fsdp, r),
        sc,
        [x, mods, biases, entry, *pieces],
        [
            per_image(g, SLOTS, D), mod_spec(g, layer), bias_spec(layer, 4 * D, 0),
            own_spec(layer, r, 4 * D, 0), *[whole(r, 2 * D)] * len(pieces),
        ],
        [
            HELD(g, f32),
            HELD(g, bf16, 3 * D),
            HELD(g, bf16),
            (pltpu.VMEM((D, 4 * D), bf16), whole(D, 4 * D)),
        ],
        deps,
        flops=3 * 10**9,
        moved=30 * 10**6,
    )


def ffn_part_specs(layer, parts, r):
    pieces = [*parts[0], *parts[1], *parts[2], *parts[3]]
    n = len(parts[0])
    return pieces, [
        bias_spec(layer, FF, 1), bias_spec(layer, D, 14), own_spec(layer, r, FF, 1), own_spec(layer, 4 * r, D, 0),
        *[whole(r, 2 * D)] * (2 * n), *[whole(2 * r, D)] * (2 * n),
    ]


def ffn_forward(sc, layer, mid, mods, biases, entry, exits, parts, deps, r, fsdp):
    pieces, specs = ffn_part_specs(layer, parts, r)
    g = GROUP["ffn_forward"]
    return image_call(
        g,
        partial(ffn_forward_body, g, fsdp, r),
        sc,
        [in_vmem(mid), mods, biases, biases, entry, exits, *pieces],
        [per_image(g, SLOTS, D), mod_spec(g, layer), *specs],
        [
            HELD(g, f32),
            HELD(g, f32),
            (pltpu.VMEM((D, FF), bf16), whole(D, FF)),
            (pltpu.VMEM((FF, D), bf16), whole(FF, D)),
        ],
        deps,
        flops=3 * 10**9,
        moved=30 * 10**6,
    )


def grad_outs(fsdp, m, r):
    return [
        (shape_of((fsdp, 2, m, r, D), f32), whole(fsdp, 2, m, r, D)),
        (shape_of((fsdp, 2, m, r, D), bf16), whole(fsdp, 2, m, r, D)),
    ]


def ffn_back_outs(g, fsdp, r):
    return [
        HELD(g, f32),
        (shape_of((IMG, 3, D), f32), per_image(g, 3, D)),
        (shape_of((1, FF), f32), whole(1, FF)),
        (shape_of((1, D), f32), whole(1, D)),
        *grad_outs(fsdp, 2, r),
    ]


FFN_ACC = [
    pltpu.VMEM((D, FF), f32), pltpu.VMEM((FF, D), f32),
    pltpu.VMEM((IMG * SLOTS, D), bf16), pltpu.VMEM((IMG * SLOTS, FF), bf16),
    pltpu.VMEM((IMG * SLOTS, FF), bf16), pltpu.VMEM((IMG * SLOTS, D), bf16),
]


def ffn_last(sc, layer, mid, cot, mods, biases, entry, exits, parts, deps, r, fsdp):
    pieces, specs = ffn_part_specs(layer, parts, r)
    g = GROUP["ffn_last"]
    return image_call(
        g,
        partial(ffn_last_body, g, fsdp, r),
        sc,
        [in_vmem(mid), cot, mods, biases, biases, entry, exits, *pieces],
        [per_image(g, SLOTS, D), per_image(g, SLOTS, D), mod_spec(g, layer), *specs],
        [ROW(g, bf16), *ffn_back_outs(g, fsdp, r)],
        deps,
        scratch=[pltpu.VMEM((D, FF), bf16), pltpu.VMEM((FF, D), bf16), *FFN_ACC],
        flops=8 * 10**9,
        moved=50 * 10**6,
    )


def ffn_back(sc, layer, gy, mid, mods, biases, leaving, w1, w2, deps, r, fsdp):
    g = GROUP["ffn_back"]
    return image_call(
        g,
        partial(ffn_back_body, g, fsdp, r),
        sc,
        [in_vmem(gy), in_vmem(mid), mods, biases, in_vmem(leaving), in_vmem(w1), in_vmem(w2)],
        [
            per_image(g, SLOTS, D), per_image(g, SLOTS, D), mod_spec(g, layer), bias_spec(layer, FF, 1),
            per_image(g, SLOTS, D), whole(D, FF), whole(FF, D),
        ],
        ffn_back_outs(g, fsdp, r),
        deps,
        scratch=FFN_ACC,
        flops=6 * 10**9,
        moved=50 * 10**6,
    )


def attn_back(out_row, sc, layer, gmid, x, mods, biases, qkv, att, w, deps, r, fsdp):
    g = GROUP["attn_back"]
    return image_call(
        g,
        partial(attn_back_body, g, fsdp, r),
        sc,
        [in_vmem(gmid), x, mods, biases, in_vmem(qkv), in_vmem(att), in_vmem(w)],
        [
            per_image(g, SLOTS, D), per_image(g, SLOTS, D), mod_spec(g, layer), bias_spec(layer, 4 * D, 0),
            per_image(g, SLOTS, 3 * D), per_image(g, SLOTS, D), whole(D, 4 * D),
        ],
        [
            out_row(g, f32),
            (shape_of((IMG, 3, D), f32), per_image(g, 3, D)),
            (shape_of((1, 4 * D), f32), whole(1, 4 * D)),
            *grad_outs(fsdp, 1, r),
        ],
        deps,
        scratch=[
            pltpu.VMEM((D, 4 * D), f32), pltpu.VMEM((IMG * SLOTS, D), bf16),
            pltpu.VMEM((IMG * SLOTS, 3 * D), bf16), pltpu.VMEM((IMG * SLOTS, D), bf16),
            pltpu.VMEM((IMG * SLOTS, D), bf16),
        ],
        flops=6 * 10**9,
        moved=50 * 10**6,
    )


def mod_body(fsdp, *refs):
    ws, conds, outs = refs[:3], refs[3][...], refs[4:]
    for k in range(3):
        val = nn(conds, ws[k][0].astype(bf16))
        for j in range(fsdp):
            outs[j][0, :, 2 * D * k : 2 * D * (k + 1)] = val[j * IMG : (j + 1) * IMG]


def mod_partial(entry, cond_rows, r, fsdp):
    return pl.pallas_call(
        partial(mod_body, fsdp),
        out_shape=[shape_of((LAYERS, IMG, ADA), f32)] * fsdp,
        grid=(LAYERS,),
        in_specs=[
            *[pl.BlockSpec((1, r, 2 * D), lambda l, k=k: (l, 0, 4 + k)) for k in range(3)],
            pl.BlockSpec((fsdp * IMG, r), lambda l: (0, 0)),
        ],
        out_specs=[pl.BlockSpec((1, IMG, ADA), lambda l: (l, 0, 0))] * fsdp,
        compiler_params=pltpu.CompilerParams(vmem_limit_bytes=VMEM_BYTES),
        cost_estimate=pl.CostEstimate(flops=0, bytes_accessed=8 * 10**6, transcendentals=0),
    )(entry, entry, entry, cond_rows)


def cond_back_body(*refs):
    gs, ws, out_ref = refs[:3], refs[3:6], refs[6]
    val = nt(gs[0][...], ws[0][0].astype(bf16))
    for k in range(1, 3):
        val = val + nt(gs[k][...], ws[k][0].astype(bf16))

    @pl.when(pl.program_id(0) == 0)
    def _():
        out_ref[...] = val

    @pl.when(pl.program_id(0) > 0)
    def _():
        out_ref[...] += val


def cond_back(g_rows, entry, r):
    rows = g_rows.shape[0]
    return pl.pallas_call(
        cond_back_body,
        out_shape=shape_of((rows, r), f32),
        grid=(LAYERS,),
        in_specs=[
            *[pl.BlockSpec((rows, 2 * D), lambda l, k=k: (0, l * 3 + k)) for k in range(3)],
            *[pl.BlockSpec((1, r, 2 * D), lambda l, k=k: (l, 0, 4 + k)) for k in range(3)],
        ],
        out_specs=pl.BlockSpec((rows, r), lambda l: (0, 0)),
        compiler_params=pltpu.CompilerParams(vmem_limit_bytes=VMEM_BYTES),
        cost_estimate=pl.CostEstimate(flops=0, bytes_accessed=8 * 10**6, transcendentals=0),
    )(*[g_rows] * 3, *[entry] * 3)


def adam_math(gradient, master, moment, square):
    new_moment = beta_one * moment + (1.0 - beta_one) * gradient
    new_square = beta_two * square + (1.0 - beta_two) * gradient * gradient
    first_fix = 1.0 / (1.0 - beta_one**STEP)
    second_fix = 1.0 / (1.0 - beta_two**STEP)
    direction = (
        new_moment * first_fix / (jnp.sqrt(new_square * second_fix) + adam_eps) + decay_rate * master
    )
    new_master = master - learn_rate * direction
    return new_moment, new_square, new_master


def adam_store(grad, ins, outs):
    moment, square, master = adam_math(grad, ins[0][0], ins[1][0], ins[2][0])
    outs[0][0] = grad
    outs[1][0] = moment
    outs[2][0] = square
    outs[3][0] = master
    outs[4][0] = master.astype(bf16)


def adam_outs(like):
    return [shape_of(like.shape, f32)] * 4 + [shape_of(like.shape, bf16)]


def pick_part(grads, kc, ky, i):
    low = jnp.where(ky == 0, grads[0][i], grads[1][i])
    high = jnp.where(ky == 0, grads[2][i], grads[3][i])
    return jnp.where(kc == 0, low, high).astype(f32)


def adam_attn_body(scale, sc, *refs):
    grads, ins, outs = refs[:4], refs[4:7], refs[-5:]
    kc = sc[0] ^ pl.program_id(0)
    both = [pick_part(grads, kc, sc[1] ^ yb, 0) for yb in range(2)]
    adam_store(jnp.concatenate(both, axis=1) * scale, ins, outs)


def adam_ffn_body(scale, sc, *refs):
    grads, ins_e, ins_x, outs_e, outs_x = refs[:4], refs[4:7], refs[7:10], refs[-10:-5], refs[-5:]
    step = pl.program_id(0)

    @pl.when(step < 2)
    def _():
        both = [pick_part(grads, sc[0], sc[1] ^ step, i) for i in range(2)]
        adam_store(jnp.concatenate(both, axis=1) * scale, ins_e, outs_e)

    @pl.when(step >= 2)
    def _():
        both = [pick_part(grads, sc[0] ^ 1, sc[1] ^ (step - 2), i) for i in range(2)]
        adam_store(jnp.concatenate(both, axis=0) * scale, ins_x, outs_x)


def adam_ada_body(scale, cond, gmod, *refs):
    adam_store(tn(cond[...], gmod[...]) * scale, refs[:3], refs[-5:])


def adam_call(body, sc, grads, groups, steps, r):
    ins, specs, outs, out_specs, aliases, extra = [*grads], [], [], [], {}, []
    specs += [pl.BlockSpec(g.shape, lambda b, s: (0, 0, 0)) for g in grads]
    for states, spec, _ in groups:
        ins += states
        specs += [spec] * 3
    for k, (states, spec, prev) in enumerate(groups):
        outs += adam_outs(states[0])
        out_specs += [spec] * 5
        if prev is not None:
            for t in range(5):
                aliases[1 + len(ins) + len(extra) + t] = 5 * k + t
            extra += prev
    got = pl.pallas_call(
        body,
        out_shape=outs,
        grid_spec=pltpu.PrefetchScalarGridSpec(
            num_scalar_prefetch=1,
            grid=(steps,),
            in_specs=[*specs, *[ANY] * len(extra)],
            out_specs=out_specs,
        ),
        input_output_aliases=aliases,
        compiler_params=pltpu.CompilerParams(
            dimension_semantics=("arbitrary",), vmem_limit_bytes=VMEM_BYTES
        ),
        cost_estimate=pl.CostEstimate(flops=0, bytes_accessed=steps * 2 * r * D * 30, transcendentals=0),
    )(sc, *ins, *extra)
    return [list(got[5 * k : 5 * k + 5]) for k in range(len(groups))]


def adam_attn(sc, grads, states, layer, scale, prev, r):
    spec = pl.BlockSpec((1, r, 2 * D), lambda b, s: (layer, 0, b))
    return adam_call(partial(adam_attn_body, scale), sc, grads, [(states, spec, prev)], 2, r)[0]


def adam_ffn(sc, grads, entry, exits, layer, scale, prev_e, prev_x, r):
    spec_e = pl.BlockSpec((1, r, 2 * D), lambda b, s: (layer, 0, 2 + jnp.minimum(b, 1)))
    spec_x = pl.BlockSpec((1, 2 * r, D), lambda b, s: (layer, jnp.maximum(b - 2, 0), 0))
    return adam_call(
        partial(adam_ffn_body, scale), sc, grads, [(entry, spec_e, prev_e), (exits, spec_x, prev_x)], 4, r
    )


def adam_ada(cond_own, gmod_all, states, scale, prev, r):
    spec = pl.BlockSpec((1, r, 2 * D), lambda l, k: (l, 0, 4 + k))
    rows = cond_own.shape[0]
    extra = [] if prev is None else list(prev)
    return list(pl.pallas_call(
        partial(adam_ada_body, scale),
        out_shape=adam_outs(states[0]),
        grid=(LAYERS, 3),
        in_specs=[
            pl.BlockSpec((rows, r), lambda l, k: (0, 0)),
            pl.BlockSpec((rows, 2 * D), lambda l, k: (0, l * 3 + k)),
            *[spec] * 3,
            *[ANY] * len(extra),
        ],
        out_specs=[spec] * 5,
        input_output_aliases={5 + k: k for k in range(len(extra))},
        compiler_params=pltpu.CompilerParams(vmem_limit_bytes=VMEM_BYTES),
        cost_estimate=pl.CostEstimate(flops=0, bytes_accessed=12 * r * D * 30, transcendentals=0),
    )(cond_own, gmod_all, *states, *extra))


def swap(v, axis, bit):
    size = lax.axis_size(axis)
    return lax.ppermute(v, axis, [(i, i ^ bit) for i in range(size)])


def spread_fsdp(v, fsdp):
    held = [v]
    bit = 1
    while bit < fsdp:
        held = held + [swap(a, "fsdp", bit) for a in held]
        bit *= 2
    return held


def low_round(v):
    return lax.reduce_precision(v, 8, 7)


def swap_both(v, j, bit):
    size = lax.axis_size("dp") * lax.axis_size("fsdp")
    mask = bit * lax.axis_size("fsdp") + j
    return lax.ppermute(v, ("dp", "fsdp"), [(i, i ^ mask) for i in range(size)])


class Unit:
    def __init__(self, keep, send, dp, fsdp):
        self.fsdp = fsdp
        self.total, self.out = keep, send
        self.plan = [("core", 0), ("scatter", 0)]
        bit = 4
        while bit < dp:
            self.plan.append(("sum", bit))
            bit *= 2
        self.plan += [("share", 2), ("pair", 1)]
        self.at = 0
        self.got = None

    def step(self):
        kind, bit = self.plan[self.at]
        self.at += 1
        if kind == "core":
            self.got = swap(self.out, "dp", 1)
            return [self.out]
        if kind == "scatter":
            total = self.total + self.got.astype(f32)
            outs, self.got = [], []
            for j in range(self.fsdp):
                for ky in range(2):
                    if j or ky:
                        outs.append(total[j, ky].astype(bf16))
                        self.got.append(swap_both(outs[-1], j, 2 * ky))
            self.total = total[0, 0]
            return outs
        if kind in ("sum", "share"):
            got = self.got if isinstance(self.got, (list, tuple)) else [self.got]
            for part in got:
                self.total = self.total + part.astype(f32)
        if kind == "sum":
            self.total = low_round(self.total)
            out = self.total.astype(bf16)
            self.got = swap(out, "dp", bit)
        elif kind == "share":
            out = self.total.astype(bf16)
            self.total = out
            self.got = swap(out, "dp", bit)
        else:
            out = self.got
            self.total = (self.total, self.got)
            self.got = tuple(swap(v, "dp", 1) for v in self.total)
        return [out]

    def result(self):
        return (*self.total, *self.got)

    def done(self):
        return self.at == len(self.plan)


def hold(movers, values):
    live = [m for m in movers if m.got is not None]
    tied = lax.optimization_barrier((tuple(values), tuple((m.total, m.got) for m in live)))
    for m, (total, got) in zip(live, tied[1]):
        m.total, m.got = total, got
    return tied[0]


class Chain:
    def __init__(self, rows, sums, hops):
        self.total, self.hops, self.got = (rows, sums), hops, None
        self.at = 0

    def step(self):
        self.settle()
        axis, bit = self.hops[self.at]
        self.at += 1
        self.got = tuple(swap(v, axis, bit) for v in self.total)

    def settle(self):
        if self.got is None:
            return
        axis, bit = self.hops[self.at - 1]
        rows, sums = self.total
        upper = (lax.axis_index(axis) & bit) != 0
        got = self.got[0]
        rows = jnp.concatenate([jnp.where(upper, got, rows), jnp.where(upper, rows, got)], axis=0)
        self.total = (rows, sums + self.got[1])
        self.got = None


def join(v, axis, bit):
    got = swap(v, axis, bit)
    upper = (lax.axis_index(axis) & bit) != 0
    return jnp.stack([jnp.where(upper, got, v), jnp.where(upper, v, got)], axis=0)


def per_device(
    tokens, condition, image_grid, image_counts, cotangent,
    entry_master, exit_master, bias_master,
    entry_moment, exit_moment, bias_moment,
    entry_square, exit_square, bias_square,
):
    dp, fsdp = lax.axis_size("dp"), lax.axis_size("fsdp")
    r = D // fsdp
    dp_at, f_at = lax.axis_index("dp"), lax.axis_index("fsdp")
    counted = jnp.where(
        jnp.arange(IMG) < image_counts[0], image_grid[:, 0] * image_grid[:, 1], 0
    ).astype(jnp.int32)
    sc = jnp.concatenate(
        [jnp.stack([dp_at & 1, (dp_at >> 1) & 1, f_at, f_at]).astype(jnp.int32), counted]
    )
    scale = (IMG * SLOTS * dp * fsdp) ** (-0.5)

    cond_float = condition.astype(f32)
    cond_act = jax.nn.silu(cond_float).astype(bf16)
    cond_rel = spread_fsdp(cond_act, fsdp)
    bias_low = bias_master.astype(bf16)
    bias_all = bias_low[None]
    bit = 1
    while bit < fsdp:
        bias_all = join(bias_all, "fsdp", bit).reshape(-1, *bias_low.shape)
        bit *= 2
    biases = jnp.moveaxis(bias_all, 0, 1).reshape(LAYERS, 1, -1).astype(f32)
    core = dp_at & 1

    def columns(layer, start):
        return lax.dynamic_slice(
            entry_master, (layer, 0, start + core * 2 * D), (1, r, 2 * D)
        )[0].astype(bf16)

    def ffn_halves(layer):
        low = lax.dynamic_slice(exit_master, (layer, core * 2 * r, 0), (1, 2 * r, D))[0].astype(bf16)
        return columns(layer, 4 * D), low

    def send_over(v):
        held = spread_fsdp(v, fsdp)
        return held[1:]

    def to_pair(parts):
        return [swap(v, "dp", 1) for v in parts]

    cond_rows = jnp.concatenate(
        [lax.dynamic_slice_in_dim(v, f_at * r, r, 1) for v in cond_rel], axis=0
    )
    attn0 = send_over(columns(0, 0))
    partial_mod = mod_partial(in_hbm(entry_master), cond_rows, r, fsdp)
    ffn_cols, ffn_rows, partial_mod = lax.optimization_barrier((*ffn_halves(0), partial_mod))
    mod_got = [swap(partial_mod[j], "fsdp", j) for j in range(1, fsdp)]
    ffn0 = send_over(ffn_cols), send_over(ffn_rows)
    attn0, mod_got = lax.optimization_barrier((attn0, mod_got))
    attn0_pair = to_pair(attn0)
    mod = partial_mod[0]
    for got in mod_got:
        mod = mod + got
    hidden_end, ada_end = 4 * D + FF, 10 * D + FF
    mods = mod + biases[:, :, hidden_end:ada_end]
    held_entry, held_exit = in_hbm(entry_master), in_hbm(exit_master)

    mid0, qkv0, att0, wa0 = attn_forward(
        sc, 0, tokens, mods, biases, held_entry, (attn0, attn0_pair), (), r, fsdp
    )
    send = (columns(1, 0), *ffn_halves(1))
    mid0, ffn0, send = lax.optimization_barrier((mid0, ffn0, send))
    ffn0_pair = to_pair(ffn0[0]), to_pair(ffn0[1])
    attn1 = send_over(send[0])
    x1, lv0, w10, w20 = ffn_forward(
        sc, 0, mid0, mods, biases, held_entry, held_exit,
        (ffn0[0], ffn0_pair[0], ffn0[1], ffn0_pair[1]), (), r, fsdp,
    )
    x1, attn1, send = lax.optimization_barrier((x1, attn1, send))
    attn1_pair = to_pair(attn1)
    ffn1 = send_over(send[1]), send_over(send[2])
    mid1, qkv1, att1, wa1 = attn_forward(
        sc, 1, in_vmem(x1), mods, biases, held_entry, (attn1, attn1_pair), (), r, fsdp
    )
    mid1, ffn1 = lax.optimization_barrier((mid1, ffn1))
    ffn1_pair = to_pair(ffn1[0]), to_pair(ffn1[1])
    block_output, gmid1, gm1b, bs1_1, bs1_2, keep, send = ffn_last(
        sc, 1, mid1, cotangent, mods, biases, held_entry, held_exit,
        (ffn1[0], ffn1_pair[0], ffn1[1], ffn1_pair[1]), (), r, fsdp,
    )
    u_a = Unit(keep, send, dp, fsdp)
    u_a.step()
    deps = u_a.step()
    gx1, gm1a, bs1_a, keep, send = attn_back(
        HELD, sc, 1, gmid1, in_vmem(x1), mods, biases, qkv1, att1, wa1, deps, r, fsdp
    )
    gx1, keep, send = hold([u_a], [gx1, keep, send])
    u_b = Unit(keep, send, dp, fsdp)
    u_b.step()
    deps = u_a.step() + u_b.step()
    gmid0, gm0b, bs0_1, bs0_2, keep, send = ffn_back(
        sc, 0, gx1, mid0, mods, biases, lv0, w10, w20, deps, r, fsdp
    )
    gmid0, keep, send = hold([u_a, u_b], [gmid0, keep, send])
    u_c = Unit(keep, send, dp, fsdp)
    u_c.step()
    deps = u_a.step() + u_b.step() + u_c.step()
    grad_tokens, gm0a, bs0_a, keep, send = attn_back(
        ROW, sc, 0, gmid0, tokens, mods, biases, qkv0, att0, wa0, deps, r, fsdp
    )
    g_mods = [gm0a, gm0b, gm1a, gm1b]
    b_sums = [bs0_a, bs0_1, bs0_2, bs1_a, bs1_1, bs1_2]
    grad_tokens, keep, send, *tied = hold(
        [u_a, u_b, u_c], [grad_tokens, keep, send, *g_mods, *b_sums]
    )
    g_mods, b_sums = tied[:4], tied[4:]
    u_d = Unit(keep, send, dp, fsdp)
    u_d.step()
    units = [u_a, u_b, u_c, u_d]
    for unit in (u_d, u_c, u_a, u_b):
        unit.step()
    wide = LAYERS * ADA
    g_mod = jnp.concatenate(g_mods, axis=1).astype(bf16).reshape(IMG, wide)
    hops = []
    bit = 1
    while bit < fsdp:
        hops.append(("fsdp", bit))
        bit *= 2
    group_hops = len(hops)
    bit = dp // 2
    while bit:
        hops.append(("dp", bit))
        bit //= 2
    chain = Chain(jnp.concatenate([g_mod, cond_act], axis=1), jnp.concatenate(b_sums, axis=1), hops)
    for _ in range(group_hops):
        chain.step()
    chain.settle()
    group_rows = chain.total[0]
    hold([chain, *units], [])
    back = cond_back(group_rows, held_entry, r).reshape(fsdp, IMG, r)

    entry = [held_entry, in_hbm(entry_moment), in_hbm(entry_square)]
    exits = [held_exit, in_hbm(exit_moment), in_hbm(exit_square)]
    e = x = None
    updates = [(u_a, 1, True), (u_b, 1, False), (u_c, 0, True), (u_d, 0, False)]
    while True:
        for unit in units:
            if not unit.done():
                unit.step()
        for _ in range(2 if chain.at == group_hops else 1):
            if chain.at < len(hops):
                chain.step()
        for item in [u for u in updates if u[0].done()]:
            unit, layer, ffn = item
            updates.remove(item)
            if unit is u_d:
                chain.settle()
                rows, bias_sum = chain.total
                cond_own = lax.dynamic_slice_in_dim(rows, wide + f_at * r, r, 1)
                e = adam_ada(cond_own, rows, entry, scale, e, r)
            if ffn:
                e, x = adam_ffn(sc, unit.result(), entry, exits, layer, scale, e, x, r)
            else:
                e = adam_attn(sc, unit.result(), entry, layer, scale, e, r)
        if not updates:
            break
        kept = [*(e or []), *(x or []), back]
        tied = hold([chain, *[u for u in units if not u.done()]], kept)
        back = tied[-1]
        e = tied[:5] if e else None
        x = tied[5:10] if x else None

    pieces = [lax.dynamic_index_in_dim(back, f_at, 0, keepdims=False)]
    for j in range(1, fsdp):
        pieces.append(swap(lax.dynamic_index_in_dim(back, f_at ^ j, 0, keepdims=False), "fsdp", j))
    g_cond = jnp.zeros((fsdp, IMG, r), f32)
    for j in range(fsdp):
        g_cond = lax.dynamic_update_index_in_dim(g_cond, pieces[j], f_at ^ j, 0)
    g_cond = jnp.moveaxis(g_cond, 0, 1).reshape(IMG, D)
    grad_condition = jax.vjp(jax.nn.silu, cond_float)[1](g_cond)[0]
    ada_bias = jnp.sum(rows[:, :wide].astype(f32), axis=0).reshape(LAYERS, ADA)
    bias_sum = bias_sum.reshape(LAYERS, -1)
    bias_sum = jnp.concatenate([bias_sum[:, :hidden_end], ada_bias, bias_sum[:, hidden_end:]], axis=1)
    width = bias_master.shape[1]
    bias_grad = lax.dynamic_slice_in_dim(bias_sum, f_at * width, width, 1) * scale
    exit_bias_grad = lax.dynamic_slice_in_dim(bias_sum[:, ada_end:], f_at * r, r, 1) * scale
    bias_moment_new, bias_square_new, bias_master_new = adam_math(
        bias_grad, bias_master, bias_moment, bias_square
    )
    return (
        block_output, grad_tokens, grad_condition,
        *e, *x,
        bias_grad, bias_moment_new, bias_square_new, bias_master_new,
        bias_master_new.astype(bf16), exit_bias_grad,
    )


def solution(mesh):
    rows = P(("dp", "fsdp"), None, None)
    flat = P(("dp", "fsdp"), None)
    mat = P(None, "fsdp", None)
    vec = P(None, "fsdp")
    return jax.shard_map(
        per_device,
        mesh=mesh,
        in_specs=(rows, flat, flat, P(("dp", "fsdp")), rows, mat, mat, vec, mat, mat, vec, mat, mat, vec),
        out_specs=(rows, rows, flat, *[mat] * 10, *[vec] * 6),
        check_vma=False,
    )
```

```python
from functools import partial

import jax
import jax.numpy as jnp
from jax import lax
from jax.experimental import pallas as pl
from jax.experimental.pallas import tpu as pltpu
from jax.sharding import PartitionSpec as P

D = 384
HEADS = 6
HEAD_DIM = 64
FF = 1536
LAYERS = 2
IMG = 4
STEP = 4
SLOTS = 256
ADA = 6 * D

eps_norm = 1e-06
neg_big = -1e30
beta_one = 0.5
beta_two = 0.6
adam_eps = 1e-08
learn_rate = 0.02
decay_rate = 0.1

f32 = jnp.float32
bf16 = jnp.bfloat16
VMEM_BYTES = 24 * 1024 * 1024
VMEM_IMAGE = {"attn_forward": 20, "ffn_forward": 23, "ffn_last": 25, "ffn_back": 21, "attn_back": 17}


def nn(a, b):
    return lax.dot_general(a, b, (((1,), (0,)), ((), ())), preferred_element_type=f32)


def nt(a, b):
    return lax.dot_general(a, b, (((1,), (1,)), ((), ())), preferred_element_type=f32)


def tn(a, b):
    return lax.dot_general(a, b, (((0,), (0,)), ((), ())), preferred_element_type=f32)


def standardize(x):
    mean = jnp.mean(x, axis=-1, keepdims=True)
    cen = x - mean
    var = jnp.mean(cen * cen, axis=-1, keepdims=True)
    rstd = lax.rsqrt(var + eps_norm)
    return cen * rstd, rstd


def norm_back(g, xhat, rstd, scale):
    t = g * (1.0 + scale)
    mean_t = jnp.mean(t, axis=-1, keepdims=True)
    mean_tx = jnp.mean(t * xhat, axis=-1, keepdims=True)
    return (t - mean_t - xhat * mean_tx) * rstd


def colsum(x):
    return jnp.sum(x, axis=0, keepdims=True)


def at_lane(i):
    return pl.ds(pl.multiple_of(i * D, 128), D)


def at_row(i, r):
    return pl.ds(pl.multiple_of(i * r, 16), r)


def place_columns(sc, own, mine, other, w_ref, r, fsdp):
    half = w_ref.shape[1] // 2
    c, f = sc[0], sc[2]
    w_ref[at_row(f, r), :] = own[0].astype(bf16)
    for j in range(1, fsdp):
        for kc, part in ((0, mine), (1, other)):
            w_ref[at_row(f ^ j, r), pl.ds(pl.multiple_of((c ^ kc) * half, 128), half)] = part[j - 1][...]


def place_rows(sc, own, mine, other, w_ref, r, fsdp):
    c, f = sc[0], sc[2]
    w_ref[at_row(f, 4 * r), :] = own[0].astype(bf16)
    for j in range(1, fsdp):
        for kc, part in ((0, mine), (1, other)):
            w_ref[at_row((f ^ j) * 2 + (c ^ kc), 2 * r), :] = part[j - 1][...]


def emit_attn(sc, acc, keep, send, r, fsdp):
    c, y, f = sc[0], sc[1], sc[2]
    for j in range(fsdp):
        for ky in range(2):
            for kc in range(2):
                blk = acc[at_row(f ^ j, r), at_lane((c ^ kc) * 2 + (y ^ ky))]
                if kc == 0:
                    keep[j, ky, 0] = blk
                else:
                    send[j, ky, 0] = blk.astype(bf16)


def emit_ffn(sc, acc1, acc2, keep, send, r, fsdp):
    c, y, f = sc[0], sc[1], sc[2]
    for kc in range(2):
        for cb in range(2):

            @pl.when((c ^ kc) == cb)
            def _(kc=kc, cb=cb):
                for j in range(fsdp):
                    for ky in range(2):
                        for i in range(2):
                            pos = (y ^ ky) * 2 + i
                            if cb == 0:
                                blk = acc1[at_row(f ^ j, r), at_lane(pos)]
                            else:
                                blk = acc2[at_row((f ^ j) * 4 + pos, r), :]
                            if kc == 0:
                                keep[j, ky, i] = blk
                            else:
                                send[j, ky, i] = blk.astype(bf16)


def half_lane():
    return lax.broadcasted_iota(jnp.int32, (1, 2 * HEAD_DIM), 1) < HEAD_DIM


def pair_lanes(qkv, third, p):
    start = third * D + 2 * HEAD_DIM * p
    return qkv[:, start : start + 2 * HEAD_DIM]


def stack_pair(v):
    low_half = half_lane()
    none = jnp.zeros_like(v)
    return jnp.concatenate([jnp.where(low_half, v, none), jnp.where(low_half, none, v)], axis=0)


def pair_probs(qkv, live_slots):
    live = lax.broadcasted_iota(jnp.int32, (1, 2 * SLOTS), 1) & (SLOTS - 1)
    live = live < live_slots
    scores = []
    for p in range(3):
        q = pair_lanes(qkv, 0, p) * jnp.asarray(HEAD_DIM ** (-0.5), bf16)
        scores.append(jnp.where(live, nt(q, stack_pair(pair_lanes(qkv, 1, p))), neg_big))
    out = []
    for s in scores:
        heads = []
        for h in range(2):
            sh = s[:, h * SLOTS : (h + 1) * SLOTS]
            e = jnp.exp(sh - jnp.max(sh, axis=-1, keepdims=True))
            heads.append(e * (1.0 / jnp.sum(e, axis=-1, keepdims=True)))
        out.append(jnp.concatenate(heads, axis=1))
    return out


def flat(v):
    return v.reshape(v.shape[0] * v.shape[1], v.shape[2])


def deep(v):
    return v.reshape(v.shape[0] // SLOTS, SLOTS, v.shape[1])


def slotsum(v):
    return jnp.sum(v, axis=1, keepdims=True)


def mod_part(mod_ref, k, group):
    if group == IMG:
        return mod_ref[0, :, k * D : (k + 1) * D][:, None, :]
    first = pl.program_id(0) * group
    rows = [mod_ref[0, pl.ds(first + i, 1), k * D : (k + 1) * D][None] for i in range(group)]
    return rows[0] if group == 1 else jnp.concatenate(rows, axis=0)


def modulated(x, mod_ref, k):
    xhat, rstd = standardize(x)
    group = x.shape[0]
    normed = (xhat * (1.0 + mod_part(mod_ref, k + 1, group)) + mod_part(mod_ref, k, group)).astype(bf16)
    return xhat, rstd, flat(normed)


def attn_forward_body(group, fsdp, r, *refs):
    sc, x_ref, mod_ref, bias_ref, own = refs[:5]
    n = fsdp - 1
    mine, other = refs[5 : 5 + n], refs[5 + n : 5 + 2 * n]
    mid_ref, qkv_ref, att_ref, w_ref = refs[-4:]
    bias_ref = bias_ref.at[0]
    step = pl.program_id(0)

    @pl.when(step == 0)
    def _():
        place_columns(sc, own, mine, other, w_ref, r, fsdp)

    x = x_ref[...].astype(f32)
    _, _, normed = modulated(x, mod_ref, 0)
    qkv_all = (nn(normed, w_ref[:, : 3 * D]) + bias_ref[:, : 3 * D]).astype(bf16)
    qkv_ref[...] = deep(qkv_all)
    for i in range(group):
        qkv = qkv_all[i * SLOTS : (i + 1) * SLOTS]
        for p, probs in enumerate(pair_probs(qkv, sc[4 + step * group + i])):
            att = nn(probs.astype(bf16), stack_pair(pair_lanes(qkv, 2, p)))
            att_ref[i, :, 2 * HEAD_DIM * p : 2 * HEAD_DIM * (p + 1)] = att.astype(bf16)
    branch = nn(flat(att_ref[...]), w_ref[:, 3 * D :]) + bias_ref[:, 3 * D :]
    mid_ref[...] = x + mod_part(mod_ref, 2, group) * deep(branch)


def gelu(v):
    return v * (0.5 + 0.5 * jnp.tanh(v * (0.7978845608 + (0.7978845608 * 0.044715) * (v * v))))


def gelu_both(v):
    sq = v * v
    half = 0.5 + 0.5 * jnp.tanh(v * (0.7978845608 + (0.7978845608 * 0.044715) * sq))
    slope = 2.0 * 0.7978845608 + (6.0 * 0.044715 * 0.7978845608) * sq
    return v * half, half + v * slope * (half - half * half)


def ffn_forward_body(group, fsdp, r, *refs):
    sc, mid_ref, mod_ref, b1_ref, b2_ref, own1, own2 = refs[:7]
    n = fsdp - 1
    parts = [refs[7 + k * n : 7 + (k + 1) * n] for k in range(4)]
    y_ref, leave_ref, w1_ref, w2_ref = refs[-4:]
    b1_ref, b2_ref = b1_ref.at[0], b2_ref.at[0]

    @pl.when(pl.program_id(0) == 0)
    def _():
        place_columns(sc, own1, parts[0], parts[1], w1_ref, r, fsdp)
        place_rows(sc, own2, parts[2], parts[3], w2_ref, r, fsdp)

    mid = mid_ref[...]
    _, _, normed = modulated(mid, mod_ref, 3)
    act = gelu(nn(normed, w1_ref[...]) + b1_ref[...]).astype(bf16)
    leaving = deep(nn(act, w2_ref[...]) + b2_ref[...])
    leave_ref[...] = leaving
    y_ref[...] = mid + mod_part(mod_ref, 5, group) * leaving


def accumulate(ref, val):
    @pl.when(pl.program_id(0) == 0)
    def _():
        ref[...] = val

    @pl.when(pl.program_id(0) > 0)
    def _():
        ref[...] += val


def ffn_back_core(
    group, g_y, xhat, rstd, normed, slope, act, leaving, mod_ref, w1, w2,
    gmid_ref, gmod_ref, bs1_ref, bs2_ref, held,
):
    normed_all, pre_all, act_all, leave_all = held
    rows = group * SLOTS
    at = pl.ds(pl.multiple_of(pl.program_id(0) * rows, rows), rows)
    g_leave = flat((mod_part(mod_ref, 5, group) * g_y).astype(bf16))
    gmod_ref[:, 2:3] = slotsum(g_y * leaving)
    g_pre = (slope * nt(g_leave, w2[...])).astype(bf16)
    normed_all[at, :] = normed
    act_all[at, :] = act
    leave_all[at, :] = g_leave
    pre_all[at, :] = g_pre
    g_n = deep(nt(g_pre, w1[...]))
    gmod_ref[:, 0:1] = slotsum(g_n)
    gmod_ref[:, 1:2] = slotsum(g_n * xhat)
    gmid_ref[...] = g_y + norm_back(g_n, xhat, rstd, mod_part(mod_ref, 4, group))
    accumulate(bs1_ref, colsum(g_pre.astype(f32)))
    accumulate(bs2_ref, colsum(g_leave.astype(f32)))


def ffn_weight_grads(sc, held, acc1, acc2, keep, send, r, fsdp):
    normed_all, pre_all, act_all, leave_all = held
    acc1[...] = tn(normed_all[...], pre_all[...])
    acc2[...] = tn(act_all[...], leave_all[...])
    emit_ffn(sc, acc1, acc2, keep, send, r, fsdp)


def ffn_last_body(group, fsdp, r, *refs):
    sc, mid_ref, cot_ref, mod_ref, b1_ref, b2_ref, own1, own2 = refs[:8]
    n = fsdp - 1
    parts = [refs[8 + k * n : 8 + (k + 1) * n] for k in range(4)]
    (out_ref, gmid_ref, gmod_ref, bs1_ref, bs2_ref, keep, send, w1_ref, w2_ref, acc1, acc2, *held) = refs[-15:]
    b1_ref, b2_ref = b1_ref.at[0], b2_ref.at[0]
    step = pl.program_id(0)

    @pl.when(step == 0)
    def _():
        place_columns(sc, own1, parts[0], parts[1], w1_ref, r, fsdp)
        place_rows(sc, own2, parts[2], parts[3], w2_ref, r, fsdp)

    mid = mid_ref[...]
    xhat, rstd, normed = modulated(mid, mod_ref, 3)
    act, slope = gelu_both(nn(normed, w1_ref[...]) + b1_ref[...])
    act = act.astype(bf16)
    leaving = deep(nn(act, w2_ref[...]) + b2_ref[...])
    out_ref[...] = (mid + mod_part(mod_ref, 5, group) * leaving).astype(bf16)
    slots = lax.broadcasted_iota(jnp.int32, (1, SLOTS, 1), 1)
    g_y = jnp.concatenate(
        [
            jnp.where(slots < sc[4 + step * group + i], cot_ref[i : i + 1].astype(f32), 0.0)
            for i in range(group)
        ],
        axis=0,
    )
    ffn_back_core(
        group, g_y, xhat, rstd, normed, slope, act, leaving, mod_ref, w1_ref, w2_ref,
        gmid_ref, gmod_ref, bs1_ref, bs2_ref, held,
    )

    @pl.when(step == IMG // group - 1)
    def _():
        ffn_weight_grads(sc, held, acc1, acc2, keep, send, r, fsdp)


def ffn_back_body(group, fsdp, r, *refs):
    sc, gy_ref, mid_ref, mod_ref, b1_ref, leave_ref, w1_ref, w2_ref = refs[:8]
    (gmid_ref, gmod_ref, bs1_ref, bs2_ref, keep, send, acc1, acc2, *held) = refs[-12:]
    xhat, rstd, normed = modulated(mid_ref[...], mod_ref, 3)
    act, slope = gelu_both(nn(normed, w1_ref[...]) + b1_ref[0])
    ffn_back_core(
        group, gy_ref[...], xhat, rstd, normed, slope, act.astype(bf16), leave_ref[...], mod_ref,
        w1_ref, w2_ref, gmid_ref, gmod_ref, bs1_ref, bs2_ref, held,
    )

    @pl.when(pl.program_id(0) == IMG // group - 1)
    def _():
        ffn_weight_grads(sc, held, acc1, acc2, keep, send, r, fsdp)


def attn_back_body(group, fsdp, r, *refs):
    (sc, gmid_ref, x_ref, mod_ref, bias_ref, qkv_ref, att_ref, w_ref) = refs[:8]
    (gx_ref, gmod_ref, bs_ref, keep, send, acc, normed_all, gproj_all, att_all, branch_all) = refs[-10:]
    bias_ref = bias_ref.at[0]
    step = pl.program_id(0)
    rows = group * SLOTS
    at = pl.ds(pl.multiple_of(step * rows, rows), rows)
    gmid = gmid_ref[...]
    att = flat(att_ref[...])
    g_branch = flat((mod_part(mod_ref, 2, group) * gmid).astype(bf16))
    g_att_all = nt(g_branch, w_ref[:, 3 * D :]).astype(bf16)
    low_half = half_lane()
    for i in range(group):
        qkv = qkv_ref[i]
        g_att = g_att_all[i * SLOTS : (i + 1) * SLOTS]
        live_slots = sc[4 + step * group + i]
        g_probs = [nt(pair_lanes(g_att, 0, p), stack_pair(pair_lanes(qkv, 2, p))) for p in range(3)]
        all_probs = pair_probs(qkv, live_slots)
        live = lax.broadcasted_iota(jnp.int32, (1, SLOTS), 1) < live_slots
        for p in range(3):
            q, k, ga = pair_lanes(qkv, 0, p), pair_lanes(qkv, 1, p), pair_lanes(g_att, 0, p)
            g_s = []
            for h in range(2):
                gp = g_probs[p][:, h * SLOTS : (h + 1) * SLOTS]
                probs = all_probs[p][:, h * SLOTS : (h + 1) * SLOTS]
                row = jnp.sum(gp * probs, axis=-1, keepdims=True)
                val = jnp.where(live, probs * (gp - row), 0.0)
                g_s.append(val.astype(bf16) * jnp.asarray(HEAD_DIM ** (-0.5), bf16))
            g_s = jnp.concatenate(g_s, axis=1)
            gq = nn(g_s, stack_pair(k))
            gk = tn(g_s, q)
            gv = tn(all_probs[p].astype(bf16), ga)
            gk = jnp.where(low_half, gk[:SLOTS], gk[SLOTS:])
            gv = jnp.where(low_half, gv[:SLOTS], gv[SLOTS:])
            here = pl.ds(pl.multiple_of(step * rows + i * SLOTS, SLOTS), SLOTS)
            for t, val in enumerate((gq, gk, gv)):
                lanes = slice(t * D + 2 * HEAD_DIM * p, t * D + 2 * HEAD_DIM * (p + 1))
                gproj_all[here, lanes] = val.astype(bf16)
    branch = deep(nn(att, w_ref[:, 3 * D :]) + bias_ref[:, 3 * D :])
    gmod_ref[:, 2:3] = slotsum(gmid * branch)
    xhat, rstd, normed = modulated(x_ref[...].astype(f32), mod_ref, 0)
    normed_all[at, :] = normed
    att_all[at, :] = att
    branch_all[at, :] = g_branch
    gp = gproj_all[at, :]
    g_n = deep(nt(gp, w_ref[:, : 3 * D]))
    gmod_ref[:, 0:1] = slotsum(g_n)
    gmod_ref[:, 1:2] = slotsum(g_n * xhat)
    gx_ref[...] = gmid + norm_back(g_n, xhat, rstd, mod_part(mod_ref, 1, group))
    accumulate(bs_ref, jnp.concatenate([colsum(gp.astype(f32)), colsum(g_branch.astype(f32))], axis=1))

    @pl.when(step == IMG // group - 1)
    def _():
        acc[:, : 3 * D] = tn(normed_all[...], gproj_all[...])
        acc[:, 3 * D :] = tn(att_all[...], branch_all[...])
        emit_attn(sc, acc, keep, send, r, fsdp)


GROUP = {"attn_forward": 2, "ffn_forward": 2, "ffn_last": 1, "ffn_back": 1, "attn_back": 1}


def per_image(g, *tail):
    return pl.BlockSpec((g, *tail), lambda i, s: (i, *([0] * len(tail))))


def whole(*shape):
    return pl.BlockSpec(shape, lambda i, s: (0,) * len(shape))


def shape_of(dims, dt):
    return jax.ShapeDtypeStruct(dims, dt)


ANY = pl.BlockSpec(memory_space=pl.ANY)


def in_hbm(v):
    return pltpu.with_memory_space_constraint(v, pltpu.HBM)


def in_vmem(v):
    return pltpu.with_memory_space_constraint(v, pltpu.VMEM)


def image_call(g, limit, body, sc, ins, in_specs, outs, deps=(), scratch=(), flops=0, moved=0):
    return pl.pallas_call(
        body,
        out_shape=[o[0] for o in outs],
        grid_spec=pltpu.PrefetchScalarGridSpec(
            num_scalar_prefetch=1,
            grid=(IMG // g,),
            in_specs=[*in_specs, *[ANY] * len(deps)],
            out_specs=[o[1] for o in outs],
            scratch_shapes=list(scratch),
        ),
        compiler_params=pltpu.CompilerParams(
            dimension_semantics=("arbitrary",), vmem_limit_bytes=limit * 1024 * 1024
        ),
        cost_estimate=pl.CostEstimate(flops=flops, bytes_accessed=moved, transcendentals=0),
    )(sc, *ins, *deps)


def mod_spec(g, layer):
    return pl.BlockSpec((1, IMG, ADA), lambda i, s: (layer, 0, 0))


def bias_spec(layer, width, k):
    return pl.BlockSpec((1, 1, width), lambda i, s: (layer, 0, k))


def own_spec(layer, rows, width, k):
    return pl.BlockSpec((1, rows, width), lambda i, s: (layer, 0, k))


ROW = lambda g, dt, w=D: (shape_of((IMG, SLOTS, w), dt), per_image(g, SLOTS, w))
FAR = lambda g, dt, w=D: (pltpu.HBM((IMG, SLOTS, w), dt), per_image(g, SLOTS, w))
HELD = lambda g, dt, w=D: (pltpu.VMEM((IMG, SLOTS, w), dt), per_image(g, SLOTS, w))


def attn_forward(far, sc, layer, x, mods, biases, entry, parts, deps, r, fsdp):
    pieces = [*parts[0], *parts[1]]
    g = GROUP["attn_forward"]
    return image_call(
        g,
        VMEM_IMAGE["attn_forward"],
        partial(attn_forward_body, g, fsdp, r),
        sc,
        [x, mods, biases, entry, *pieces],
        [
            per_image(g, SLOTS, D), mod_spec(g, layer), bias_spec(layer, 4 * D, 0),
            own_spec(layer, r, 4 * D, 0), *[whole(r, 2 * D)] * len(pieces),
        ],
        [
            HELD(g, f32),
            far(g, bf16, 3 * D),
            far(g, bf16),
            ((pltpu.HBM if far is FAR else pltpu.VMEM)((D, 4 * D), bf16), whole(D, 4 * D)),
        ],
        deps,
        flops=3 * 10**9,
        moved=30 * 10**6,
    )


def ffn_part_specs(layer, parts, r):
    pieces = [*parts[0], *parts[1], *parts[2], *parts[3]]
    n = len(parts[0])
    return pieces, [
        bias_spec(layer, FF, 1), bias_spec(layer, D, 14), own_spec(layer, r, FF, 1), own_spec(layer, 4 * r, D, 0),
        *[whole(r, 2 * D)] * (2 * n), *[whole(2 * r, D)] * (2 * n),
    ]


def ffn_forward(sc, layer, mid, mods, biases, entry, exits, parts, deps, r, fsdp):
    pieces, specs = ffn_part_specs(layer, parts, r)
    g = GROUP["ffn_forward"]
    return image_call(
        g,
        VMEM_IMAGE["ffn_forward"],
        partial(ffn_forward_body, g, fsdp, r),
        sc,
        [in_vmem(mid), mods, biases, biases, entry, exits, *pieces],
        [per_image(g, SLOTS, D), mod_spec(g, layer), *specs],
        [
            HELD(g, f32),
            HELD(g, f32),
            (pltpu.VMEM((D, FF), bf16), whole(D, FF)),
            (pltpu.VMEM((FF, D), bf16), whole(FF, D)),
        ],
        deps,
        flops=3 * 10**9,
        moved=30 * 10**6,
    )


def grad_outs(fsdp, m, r):
    return [
        (shape_of((fsdp, 2, m, r, D), f32), whole(fsdp, 2, m, r, D)),
        (shape_of((fsdp, 2, m, r, D), bf16), whole(fsdp, 2, m, r, D)),
    ]


def ffn_back_outs(place, g, fsdp, r):
    return [
        place(g, f32),
        (shape_of((IMG, 3, D), f32), per_image(g, 3, D)),
        (shape_of((1, FF), f32), whole(1, FF)),
        (shape_of((1, D), f32), whole(1, D)),
        *grad_outs(fsdp, 2, r),
    ]


FFN_ACC = [
    pltpu.VMEM((D, FF), f32), pltpu.VMEM((FF, D), f32),
    pltpu.VMEM((IMG * SLOTS, D), bf16), pltpu.VMEM((IMG * SLOTS, FF), bf16),
    pltpu.VMEM((IMG * SLOTS, FF), bf16), pltpu.VMEM((IMG * SLOTS, D), bf16),
]


def ffn_last(sc, layer, mid, cot, mods, biases, entry, exits, parts, deps, r, fsdp):
    pieces, specs = ffn_part_specs(layer, parts, r)
    g = GROUP["ffn_last"]
    return image_call(
        g,
        VMEM_IMAGE["ffn_last"],
        partial(ffn_last_body, g, fsdp, r),
        sc,
        [in_vmem(mid), cot, mods, biases, biases, entry, exits, *pieces],
        [per_image(g, SLOTS, D), per_image(g, SLOTS, D), mod_spec(g, layer), *specs],
        [ROW(g, bf16), *ffn_back_outs(HELD, g, fsdp, r)],
        deps,
        scratch=[pltpu.VMEM((D, FF), bf16), pltpu.VMEM((FF, D), bf16), *FFN_ACC],
        flops=8 * 10**9,
        moved=50 * 10**6,
    )


def ffn_back(sc, layer, gy, mid, mods, biases, leaving, w1, w2, deps, r, fsdp):
    g = GROUP["ffn_back"]
    return image_call(
        g,
        VMEM_IMAGE["ffn_back"],
        partial(ffn_back_body, g, fsdp, r),
        sc,
        [in_vmem(gy), in_vmem(mid), mods, biases, in_vmem(leaving), in_vmem(w1), in_vmem(w2)],
        [
            per_image(g, SLOTS, D), per_image(g, SLOTS, D), mod_spec(g, layer), bias_spec(layer, FF, 1),
            per_image(g, SLOTS, D), whole(D, FF), whole(FF, D),
        ],
        ffn_back_outs(HELD, g, fsdp, r),
        deps,
        scratch=FFN_ACC,
        flops=6 * 10**9,
        moved=50 * 10**6,
    )


def attn_back(out_row, near, sc, layer, gmid, x, mods, biases, qkv, att, w, deps, r, fsdp):
    g = GROUP["attn_back"]
    return image_call(
        g,
        VMEM_IMAGE["attn_back"],
        partial(attn_back_body, g, fsdp, r),
        sc,
        [near(gmid), x, mods, biases, near(qkv), near(att), near(w)],
        [
            per_image(g, SLOTS, D), per_image(g, SLOTS, D), mod_spec(g, layer), bias_spec(layer, 4 * D, 0),
            per_image(g, SLOTS, 3 * D), per_image(g, SLOTS, D), whole(D, 4 * D),
        ],
        [
            out_row(g, f32),
            (shape_of((IMG, 3, D), f32), per_image(g, 3, D)),
            (shape_of((1, 4 * D), f32), whole(1, 4 * D)),
            *grad_outs(fsdp, 1, r),
        ],
        deps,
        scratch=[
            pltpu.VMEM((D, 4 * D), f32), pltpu.VMEM((IMG * SLOTS, D), bf16),
            pltpu.VMEM((IMG * SLOTS, 3 * D), bf16), pltpu.VMEM((IMG * SLOTS, D), bf16),
            pltpu.VMEM((IMG * SLOTS, D), bf16),
        ],
        flops=6 * 10**9,
        moved=50 * 10**6,
    )


def mod_body(fsdp, *refs):
    ws, conds, outs = refs[:3], refs[3][...], refs[4:]
    for k in range(3):
        val = nn(conds, ws[k][0].astype(bf16))
        for j in range(fsdp):
            outs[j][0, :, 2 * D * k : 2 * D * (k + 1)] = val[j * IMG : (j + 1) * IMG]


def mod_partial(entry, cond_rows, r, fsdp):
    return pl.pallas_call(
        partial(mod_body, fsdp),
        out_shape=[shape_of((LAYERS, IMG, ADA), f32)] * fsdp,
        grid=(LAYERS,),
        in_specs=[
            *[pl.BlockSpec((1, r, 2 * D), lambda l, k=k: (l, 0, 4 + k)) for k in range(3)],
            pl.BlockSpec((fsdp * IMG, r), lambda l: (0, 0)),
        ],
        out_specs=[pl.BlockSpec((1, IMG, ADA), lambda l: (l, 0, 0))] * fsdp,
        compiler_params=pltpu.CompilerParams(vmem_limit_bytes=VMEM_BYTES),
        cost_estimate=pl.CostEstimate(flops=0, bytes_accessed=8 * 10**6, transcendentals=0),
    )(entry, entry, entry, cond_rows)


def cond_back_body(*refs):
    gs, ws, out_ref = refs[:3], refs[3:6], refs[6]
    val = nt(gs[0][...], ws[0][0].astype(bf16))
    for k in range(1, 3):
        val = val + nt(gs[k][...], ws[k][0].astype(bf16))

    @pl.when(pl.program_id(0) == 0)
    def _():
        out_ref[...] = val

    @pl.when(pl.program_id(0) > 0)
    def _():
        out_ref[...] += val


def cond_back(g_rows, entry, r):
    rows = g_rows.shape[0]
    return pl.pallas_call(
        cond_back_body,
        out_shape=shape_of((rows, r), f32),
        grid=(LAYERS,),
        in_specs=[
            *[pl.BlockSpec((rows, 2 * D), lambda l, k=k: (0, l * 3 + k)) for k in range(3)],
            *[pl.BlockSpec((1, r, 2 * D), lambda l, k=k: (l, 0, 4 + k)) for k in range(3)],
        ],
        out_specs=pl.BlockSpec((rows, r), lambda l: (0, 0)),
        compiler_params=pltpu.CompilerParams(vmem_limit_bytes=VMEM_BYTES),
        cost_estimate=pl.CostEstimate(flops=0, bytes_accessed=8 * 10**6, transcendentals=0),
    )(*[g_rows] * 3, *[entry] * 3)


def adam_math(gradient, master, moment, square):
    new_moment = beta_one * moment + (1.0 - beta_one) * gradient
    new_square = beta_two * square + (1.0 - beta_two) * gradient * gradient
    first_fix = 1.0 / (1.0 - beta_one**STEP)
    second_fix = 1.0 / (1.0 - beta_two**STEP)
    direction = (
        new_moment * first_fix / (jnp.sqrt(new_square * second_fix) + adam_eps) + decay_rate * master
    )
    new_master = master - learn_rate * direction
    return new_moment, new_square, new_master


def adam_store(grad, ins, outs):
    moment, square, master = adam_math(grad, ins[0][0], ins[1][0], ins[2][0])
    outs[0][0] = grad
    outs[1][0] = moment
    outs[2][0] = square
    outs[3][0] = master
    outs[4][0] = master.astype(bf16)


def adam_outs(like):
    return [shape_of(like.shape, f32)] * 4 + [shape_of(like.shape, bf16)]


def pick_part(grads, kc, ky, i):
    low = jnp.where(ky == 0, grads[0][i], grads[1][i])
    high = jnp.where(ky == 0, grads[2][i], grads[3][i])
    return jnp.where(kc == 0, low, high).astype(f32)


def adam_attn_body(scale, sc, *refs):
    grads, ins, outs = refs[:4], refs[4:7], refs[-5:]
    kc = sc[0] ^ pl.program_id(0)
    both = [pick_part(grads, kc, sc[1] ^ yb, 0) for yb in range(2)]
    adam_store(jnp.concatenate(both, axis=1) * scale, ins, outs)


def adam_ffn_body(scale, sc, *refs):
    grads, ins_e, ins_x, outs_e, outs_x = refs[:4], refs[4:7], refs[7:10], refs[-10:-5], refs[-5:]
    step = pl.program_id(0)

    @pl.when(step < 2)
    def _():
        both = [pick_part(grads, sc[0], sc[1] ^ step, i) for i in range(2)]
        adam_store(jnp.concatenate(both, axis=1) * scale, ins_e, outs_e)

    @pl.when(step >= 2)
    def _():
        both = [pick_part(grads, sc[0] ^ 1, sc[1] ^ (step - 2), i) for i in range(2)]
        adam_store(jnp.concatenate(both, axis=0) * scale, ins_x, outs_x)


def adam_ada_body(scale, cond, gmod, *refs):
    adam_store(tn(cond[...], gmod[...]) * scale, refs[:3], refs[-5:])


def adam_call(body, sc, grads, groups, steps, r):
    ins, specs, outs, out_specs, aliases, extra = [*grads], [], [], [], {}, []
    specs += [pl.BlockSpec(g.shape, lambda b, s: (0, 0, 0)) for g in grads]
    for states, spec, _ in groups:
        ins += states
        specs += [spec] * 3
    for k, (states, spec, prev) in enumerate(groups):
        outs += adam_outs(states[0])
        out_specs += [spec] * 5
        if prev is not None:
            for t in range(5):
                aliases[1 + len(ins) + len(extra) + t] = 5 * k + t
            extra += prev
    got = pl.pallas_call(
        body,
        out_shape=outs,
        grid_spec=pltpu.PrefetchScalarGridSpec(
            num_scalar_prefetch=1,
            grid=(steps,),
            in_specs=[*specs, *[ANY] * len(extra)],
            out_specs=out_specs,
        ),
        input_output_aliases=aliases,
        compiler_params=pltpu.CompilerParams(
            dimension_semantics=("arbitrary",), vmem_limit_bytes=VMEM_BYTES
        ),
        cost_estimate=pl.CostEstimate(flops=0, bytes_accessed=steps * 2 * r * D * 30, transcendentals=0),
    )(sc, *ins, *extra)
    return [list(got[5 * k : 5 * k + 5]) for k in range(len(groups))]


def adam_attn(sc, grads, states, layer, scale, prev, r):
    spec = pl.BlockSpec((1, r, 2 * D), lambda b, s: (layer, 0, b))
    return adam_call(partial(adam_attn_body, scale), sc, grads, [(states, spec, prev)], 2, r)[0]


def adam_ffn(sc, grads, entry, exits, layer, scale, prev_e, prev_x, r):
    spec_e = pl.BlockSpec((1, r, 2 * D), lambda b, s: (layer, 0, 2 + jnp.minimum(b, 1)))
    spec_x = pl.BlockSpec((1, 2 * r, D), lambda b, s: (layer, jnp.maximum(b - 2, 0), 0))
    return adam_call(
        partial(adam_ffn_body, scale), sc, grads, [(entry, spec_e, prev_e), (exits, spec_x, prev_x)], 4, r
    )


def adam_ada(cond_own, gmod_all, states, scale, prev, r):
    spec = pl.BlockSpec((1, r, 2 * D), lambda l, k: (l, 0, 4 + k))
    rows = cond_own.shape[0]
    extra = [] if prev is None else list(prev)
    return list(pl.pallas_call(
        partial(adam_ada_body, scale),
        out_shape=adam_outs(states[0]),
        grid=(LAYERS, 3),
        in_specs=[
            pl.BlockSpec((rows, r), lambda l, k: (0, 0)),
            pl.BlockSpec((rows, 2 * D), lambda l, k: (0, l * 3 + k)),
            *[spec] * 3,
            *[ANY] * len(extra),
        ],
        out_specs=[spec] * 5,
        input_output_aliases={5 + k: k for k in range(len(extra))},
        compiler_params=pltpu.CompilerParams(vmem_limit_bytes=VMEM_BYTES),
        cost_estimate=pl.CostEstimate(flops=0, bytes_accessed=12 * r * D * 30, transcendentals=0),
    )(cond_own, gmod_all, *states, *extra))


def swap(v, axis, bit):
    size = lax.axis_size(axis)
    return lax.ppermute(v, axis, [(i, i ^ bit) for i in range(size)])


def spread_fsdp(v, fsdp):
    held = [v]
    bit = 1
    while bit < fsdp:
        held = held + [swap(a, "fsdp", bit) for a in held]
        bit *= 2
    return held


def low_round(v):
    return lax.reduce_precision(v, 8, 7)


def swap_both(v, j, bit):
    size = lax.axis_size("dp") * lax.axis_size("fsdp")
    mask = bit * lax.axis_size("fsdp") + j
    return lax.ppermute(v, ("dp", "fsdp"), [(i, i ^ mask) for i in range(size)])


class Unit:
    def __init__(self, keep, send, dp, fsdp):
        self.fsdp = fsdp
        self.total, self.out = keep, send
        self.plan = [("core", 0), ("scatter", 0)]
        bit = 4
        while bit < dp:
            self.plan.append(("sum", bit))
            bit *= 2
        self.plan += [("share", 2), ("pair", 1)]
        self.at = 0
        self.got = None

    def step(self):
        kind, bit = self.plan[self.at]
        self.at += 1
        if kind == "core":
            self.got = swap(self.out, "dp", 1)
            return [self.out]
        if kind == "scatter":
            total = self.total + self.got.astype(f32)
            outs, self.got = [], []
            for j in range(self.fsdp):
                for ky in range(2):
                    if j or ky:
                        outs.append(total[j, ky].astype(bf16))
                        self.got.append(swap_both(outs[-1], j, 2 * ky))
            self.total = total[0, 0]
            return outs
        if kind in ("sum", "share"):
            got = self.got if isinstance(self.got, (list, tuple)) else [self.got]
            for part in got:
                self.total = self.total + part.astype(f32)
        if kind == "sum":
            self.total = low_round(self.total)
            out = self.total.astype(bf16)
            self.got = swap(out, "dp", bit)
        elif kind == "share":
            out = self.total.astype(bf16)
            self.total = out
            self.got = swap(out, "dp", bit)
        else:
            out = self.got
            self.total = (self.total, self.got)
            self.got = tuple(swap(v, "dp", 1) for v in self.total)
        return [out]

    def result(self):
        return (*self.total, *self.got)

    def done(self):
        return self.at == len(self.plan)


def hold(movers, values):
    tied = lax.optimization_barrier((tuple(values), tuple((m.total, m.got) for m in movers)))
    for m, (total, got) in zip(movers, tied[1]):
        m.total, m.got = total, got
    return tied[0]


class Chain:
    def __init__(self, rows, sums, hops):
        self.total, self.hops, self.got = (rows, sums), hops, None
        self.at = 0

    def step(self):
        self.settle()
        axis, bit = self.hops[self.at]
        self.at += 1
        self.got = tuple(swap(v, axis, bit) for v in self.total)

    def settle(self):
        if self.got is None:
            return
        axis, bit = self.hops[self.at - 1]
        rows, sums = self.total
        upper = (lax.axis_index(axis) & bit) != 0
        got = self.got[0]
        rows = jnp.concatenate([jnp.where(upper, got, rows), jnp.where(upper, rows, got)], axis=0)
        self.total = (rows, sums + self.got[1])
        self.got = None


def join(v, axis, bit):
    got = swap(v, axis, bit)
    upper = (lax.axis_index(axis) & bit) != 0
    return jnp.stack([jnp.where(upper, got, v), jnp.where(upper, v, got)], axis=0)


def per_device(
    tokens, condition, image_grid, image_counts, cotangent,
    entry_master, exit_master, bias_master,
    entry_moment, exit_moment, bias_moment,
    entry_square, exit_square, bias_square,
):
    dp, fsdp = lax.axis_size("dp"), lax.axis_size("fsdp")
    r = D // fsdp
    dp_at, f_at = lax.axis_index("dp"), lax.axis_index("fsdp")
    counted = jnp.where(
        jnp.arange(IMG) < image_counts[0], image_grid[:, 0] * image_grid[:, 1], 0
    ).astype(jnp.int32)
    sc = jnp.concatenate(
        [jnp.stack([dp_at & 1, (dp_at >> 1) & 1, f_at, f_at]).astype(jnp.int32), counted]
    )
    scale = (IMG * SLOTS * dp * fsdp) ** (-0.5)

    cond_float = condition.astype(f32)
    cond_act = jax.nn.silu(cond_float).astype(bf16)
    cond_rel = spread_fsdp(cond_act, fsdp)
    bias_low = bias_master.astype(bf16)
    bias_all = bias_low[None]
    bit = 1
    while bit < fsdp:
        bias_all = join(bias_all, "fsdp", bit).reshape(-1, *bias_low.shape)
        bit *= 2
    biases = jnp.moveaxis(bias_all, 0, 1).reshape(LAYERS, 1, -1).astype(f32)
    core = dp_at & 1

    def columns(layer, start, core):
        return lax.dynamic_slice(
            entry_master, (layer, 0, start + core * 2 * D), (1, r, 2 * D)
        )[0].astype(bf16)

    def ffn_halves(layer, core):
        low = lax.dynamic_slice(exit_master, (layer, core * 2 * r, 0), (1, 2 * r, D))[0].astype(bf16)
        return columns(layer, 4 * D, core), low

    def send_over(v):
        held = spread_fsdp(v, fsdp)
        return held[1:]

    def to_pair(parts):
        return [swap(v, "dp", 1) for v in parts]

    cond_rows = jnp.concatenate(
        [lax.dynamic_slice_in_dim(v, f_at * r, r, 1) for v in cond_rel], axis=0
    )
    attn0 = send_over(columns(0, 0, core))
    partial_mod = mod_partial(in_hbm(entry_master), cond_rows, r, fsdp)
    core_one, partial_mod, ffn_cols, ffn_rows = lax.optimization_barrier(
        (core, partial_mod, *ffn_halves(0, core))
    )
    mod_got = [swap(partial_mod[j], "fsdp", j) for j in range(1, fsdp)]
    ffn0 = send_over(ffn_cols), send_over(ffn_rows)
    core_two, attn0, mod_got = lax.optimization_barrier((core_one, attn0, mod_got))
    attn0_pair = to_pair(attn0)
    mod = partial_mod[0]
    for got in mod_got:
        mod = mod + got
    hidden_end, ada_end = 4 * D + FF, 10 * D + FF
    mods = mod + biases[:, :, hidden_end:ada_end]
    held_entry, held_exit = in_hbm(entry_master), in_hbm(exit_master)

    mid0, qkv0, att0, wa0 = attn_forward(
        HELD, sc, 0, tokens, mods, biases, held_entry, (attn0, attn0_pair), (), r, fsdp
    )
    send = (columns(1, 0, core_two), *ffn_halves(1, core_two))
    mid0, ffn0, send = lax.optimization_barrier((mid0, ffn0, send))
    ffn0_pair = to_pair(ffn0[0]), to_pair(ffn0[1])
    attn1 = send_over(send[0])
    ffn1 = send_over(send[1]), send_over(send[2])
    x1, lv0, w10, w20 = ffn_forward(
        sc, 0, mid0, mods, biases, held_entry, held_exit,
        (ffn0[0], ffn0_pair[0], ffn0[1], ffn0_pair[1]), (), r, fsdp,
    )
    x1, attn1 = lax.optimization_barrier((x1, attn1))
    attn1_pair = to_pair(attn1)
    mid1, qkv1, att1, wa1 = attn_forward(
        HELD, sc, 1, in_vmem(x1), mods, biases, held_entry, (attn1, attn1_pair), (), r, fsdp
    )
    mid1, ffn1 = lax.optimization_barrier((mid1, ffn1))
    ffn1_pair = to_pair(ffn1[0]), to_pair(ffn1[1])
    block_output, gmid1, gm1b, bs1_1, bs1_2, keep, send = ffn_last(
        sc, 1, mid1, cotangent, mods, biases, held_entry, held_exit,
        (ffn1[0], ffn1_pair[0], ffn1[1], ffn1_pair[1]), (), r, fsdp,
    )
    u_a = Unit(keep, send, dp, fsdp)
    u_a.step()
    deps = u_a.step()
    gx1, gm1a, bs1_a, keep, send = attn_back(
        HELD, in_vmem, sc, 1, gmid1, in_vmem(x1), mods, biases, qkv1, att1, wa1, deps, r, fsdp
    )
    gx1, keep, send = hold([u_a], [gx1, keep, send])
    u_b = Unit(keep, send, dp, fsdp)
    u_b.step()
    deps = u_a.step() + u_b.step()
    gmid0, gm0b, bs0_1, bs0_2, keep, send = ffn_back(
        sc, 0, gx1, mid0, mods, biases, lv0, w10, w20, deps, r, fsdp
    )
    gmid0, keep, send = hold([u_a, u_b], [gmid0, keep, send])
    u_c = Unit(keep, send, dp, fsdp)
    u_c.step()
    deps = u_a.step() + u_b.step() + u_c.step()
    grad_tokens, gm0a, bs0_a, keep, send = attn_back(
        ROW, in_vmem, sc, 0, gmid0, tokens, mods, biases, qkv0, att0, wa0, deps, r, fsdp
    )
    g_mods = [gm0a, gm0b, gm1a, gm1b]
    b_sums = [bs0_a, bs0_1, bs0_2, bs1_a, bs1_1, bs1_2]
    grad_tokens, keep, send, *tied = hold(
        [u_a, u_b, u_c], [grad_tokens, keep, send, *g_mods, *b_sums]
    )
    g_mods, b_sums = tied[:4], tied[4:]
    u_d = Unit(keep, send, dp, fsdp)
    u_d.step()
    units = [u_a, u_b, u_c, u_d]
    outs = u_d.step()
    for unit in (u_c, u_a, u_b):
        unit.step()
    wide = LAYERS * ADA
    g_mod = jnp.concatenate(g_mods, axis=1).astype(bf16).reshape(IMG, wide)
    hops = []
    bit = 1
    while bit < fsdp:
        hops.append(("fsdp", bit))
        bit *= 2
    group_hops = len(hops)
    bit = dp // 2
    while bit:
        hops.append(("dp", bit))
        bit //= 2
    packed, sums, _ = lax.optimization_barrier(
        (jnp.concatenate([g_mod, cond_act], axis=1), jnp.concatenate(b_sums, axis=1), outs)
    )
    chain = Chain(packed, sums, hops)
    for _ in range(group_hops):
        chain.step()
    hold([chain, *units], [])
    chain.settle()
    group_rows = chain.total[0]
    back = cond_back(group_rows, held_entry, r).reshape(fsdp, IMG, r)

    entry = [held_entry, in_hbm(entry_moment), in_hbm(entry_square)]
    exits = [held_exit, in_hbm(exit_moment), in_hbm(exit_square)]
    e = x = None
    updates = [(u_a, 1, True), (u_b, 1, False), (u_c, 0, True), (u_d, 0, False)]
    while True:
        for unit in units:
            if not unit.done():
                unit.step()
        for _ in range(1):
            if chain.at < len(hops):
                chain.step()
        for item in [u for u in updates if u[0].done()]:
            unit, layer, ffn = item
            updates.remove(item)
            if unit is u_d:
                chain.settle()
                rows, bias_sum = chain.total
                cond_own = lax.dynamic_slice_in_dim(rows, wide + f_at * r, r, 1)
                e = adam_ada(cond_own, rows, entry, scale, e, r)
            if ffn:
                e, x = adam_ffn(sc, unit.result(), entry, exits, layer, scale, e, x, r)
            else:
                e = adam_attn(sc, unit.result(), entry, layer, scale, e, r)
        if not updates:
            break
        kept = [*(e or []), *(x or []), back]
        tied = hold([chain, *[u for u in units if not u.done()]], kept)
        back = tied[-1]
        e = tied[:5] if e else None
        x = tied[5:10] if x else None

    pieces = [lax.dynamic_index_in_dim(back, f_at, 0, keepdims=False)]
    for j in range(1, fsdp):
        pieces.append(swap(lax.dynamic_index_in_dim(back, f_at ^ j, 0, keepdims=False), "fsdp", j))
    g_cond = jnp.zeros((fsdp, IMG, r), f32)
    for j in range(fsdp):
        g_cond = lax.dynamic_update_index_in_dim(g_cond, pieces[j], f_at ^ j, 0)
    g_cond = jnp.moveaxis(g_cond, 0, 1).reshape(IMG, D)
    grad_condition = jax.vjp(jax.nn.silu, cond_float)[1](g_cond)[0]
    ada_bias = jnp.sum(rows[:, :wide].astype(f32), axis=0).reshape(LAYERS, ADA)
    bias_sum = bias_sum.reshape(LAYERS, -1)
    bias_sum = jnp.concatenate([bias_sum[:, :hidden_end], ada_bias, bias_sum[:, hidden_end:]], axis=1)
    width = bias_master.shape[1]
    bias_grad = lax.dynamic_slice_in_dim(bias_sum, f_at * width, width, 1) * scale
    exit_bias_grad = lax.dynamic_slice_in_dim(bias_sum[:, ada_end:], f_at * r, r, 1) * scale
    bias_moment_new, bias_square_new, bias_master_new = adam_math(
        bias_grad, bias_master, bias_moment, bias_square
    )
    return (
        block_output, grad_tokens, grad_condition,
        *e, *x,
        bias_grad, bias_moment_new, bias_square_new, bias_master_new,
        bias_master_new.astype(bf16), exit_bias_grad,
    )


def solution(mesh):
    rows = P(("dp", "fsdp"), None, None)
    flat = P(("dp", "fsdp"), None)
    mat = P(None, "fsdp", None)
    vec = P(None, "fsdp")
    return jax.shard_map(
        per_device,
        mesh=mesh,
        in_specs=(rows, flat, flat, P(("dp", "fsdp")), rows, mat, mat, vec, mat, mat, vec, mat, mat, vec),
        out_specs=(rows, rows, flat, *[mat] * 10, *[vec] * 6),
        check_vma=False,
    )
```

```python
from functools import partial

import jax
import jax.numpy as jnp
from jax import lax
from jax.experimental import pallas as pl
from jax.experimental.pallas import tpu as pltpu
from jax.sharding import PartitionSpec as P

D = 384
HEADS = 6
HEAD_DIM = 64
FF = 1536
LAYERS = 2
IMG = 4
STEP = 4
SLOTS = 256
ADA = 6 * D

eps_norm = 1e-06
neg_big = -1e30
beta_one = 0.5
beta_two = 0.6
adam_eps = 1e-08
learn_rate = 0.02
decay_rate = 0.1

f32 = jnp.float32
bf16 = jnp.bfloat16
VMEM_BYTES = 24 * 1024 * 1024
VMEM_IMAGE = {"attn_forward": 20, "ffn_forward": 23, "ffn_last": 25, "ffn_back": 21, "attn_back": 17}


def nn(a, b):
    return lax.dot_general(a, b, (((1,), (0,)), ((), ())), preferred_element_type=f32)


def nt(a, b):
    return lax.dot_general(a, b, (((1,), (1,)), ((), ())), preferred_element_type=f32)


def tn(a, b):
    return lax.dot_general(a, b, (((0,), (0,)), ((), ())), preferred_element_type=f32)


def standardize(x):
    mean = jnp.mean(x, axis=-1, keepdims=True)
    cen = x - mean
    var = jnp.mean(cen * cen, axis=-1, keepdims=True)
    rstd = lax.rsqrt(var + eps_norm)
    return cen * rstd, rstd


def norm_back(g, xhat, rstd, scale):
    t = g * (1.0 + scale)
    mean_t = jnp.mean(t, axis=-1, keepdims=True)
    mean_tx = jnp.mean(t * xhat, axis=-1, keepdims=True)
    return (t - mean_t - xhat * mean_tx) * rstd


def colsum(x):
    return jnp.sum(x, axis=0, keepdims=True)


def at_lane(i):
    return pl.ds(pl.multiple_of(i * D, 128), D)


def at_row(i, r):
    return pl.ds(pl.multiple_of(i * r, 16), r)


def place_columns(sc, own, mine, other, w_ref, r, fsdp):
    half = w_ref.shape[1] // 2
    c, f = sc[0], sc[2]
    w_ref[at_row(f, r), :] = own[0].astype(bf16)
    for j in range(1, fsdp):
        for kc, part in ((0, mine), (1, other)):
            w_ref[at_row(f ^ j, r), pl.ds(pl.multiple_of((c ^ kc) * half, 128), half)] = part[j - 1][...]


def place_rows(sc, own, mine, other, w_ref, r, fsdp):
    c, f = sc[0], sc[2]
    w_ref[at_row(f, 4 * r), :] = own[0].astype(bf16)
    for j in range(1, fsdp):
        for kc, part in ((0, mine), (1, other)):
            w_ref[at_row((f ^ j) * 2 + (c ^ kc), 2 * r), :] = part[j - 1][...]


def emit_attn(sc, acc, keep, send, r, fsdp):
    c, y, f = sc[0], sc[1], sc[2]
    for j in range(fsdp):
        for ky in range(2):
            for kc in range(2):
                blk = acc[at_row(f ^ j, r), at_lane((c ^ kc) * 2 + (y ^ ky))]
                if kc == 0:
                    keep[j, ky, 0] = blk
                else:
                    send[j, ky, 0] = blk.astype(bf16)


def emit_ffn(sc, acc1, acc2, keep, send, r, fsdp):
    c, y, f = sc[0], sc[1], sc[2]
    for kc in range(2):
        for cb in range(2):

            @pl.when((c ^ kc) == cb)
            def _(kc=kc, cb=cb):
                for j in range(fsdp):
                    for ky in range(2):
                        for i in range(2):
                            pos = (y ^ ky) * 2 + i
                            if cb == 0:
                                blk = acc1[at_row(f ^ j, r), at_lane(pos)]
                            else:
                                blk = acc2[at_row((f ^ j) * 4 + pos, r), :]
                            if kc == 0:
                                keep[j, ky, i] = blk
                            else:
                                send[j, ky, i] = blk.astype(bf16)


def half_lane():
    return lax.broadcasted_iota(jnp.int32, (1, 2 * HEAD_DIM), 1) < HEAD_DIM


def pair_lanes(qkv, third, p):
    start = third * D + 2 * HEAD_DIM * p
    return qkv[:, start : start + 2 * HEAD_DIM]


def stack_pair(v):
    low_half = half_lane()
    none = jnp.zeros_like(v)
    return jnp.concatenate([jnp.where(low_half, v, none), jnp.where(low_half, none, v)], axis=0)


def pair_probs(qkv, live_slots):
    live = lax.broadcasted_iota(jnp.int32, (1, 2 * SLOTS), 1) & (SLOTS - 1)
    live = live < live_slots
    scores = []
    for p in range(3):
        q = pair_lanes(qkv, 0, p) * jnp.asarray(HEAD_DIM ** (-0.5), bf16)
        scores.append(jnp.where(live, nt(q, stack_pair(pair_lanes(qkv, 1, p))), neg_big))
    out = []
    for s in scores:
        heads = []
        for h in range(2):
            sh = s[:, h * SLOTS : (h + 1) * SLOTS]
            e = jnp.exp(sh - jnp.max(sh, axis=-1, keepdims=True))
            heads.append(e * (1.0 / jnp.sum(e, axis=-1, keepdims=True)))
        out.append(jnp.concatenate(heads, axis=1))
    return out


def flat(v):
    return v.reshape(v.shape[0] * v.shape[1], v.shape[2])


def deep(v):
    return v.reshape(v.shape[0] // SLOTS, SLOTS, v.shape[1])


def slotsum(v):
    return jnp.sum(v, axis=1, keepdims=True)


def mod_part(mod_ref, k, group):
    if group == IMG:
        return mod_ref[0, :, k * D : (k + 1) * D][:, None, :]
    first = pl.program_id(0) * group
    rows = [mod_ref[0, pl.ds(first + i, 1), k * D : (k + 1) * D][None] for i in range(group)]
    return rows[0] if group == 1 else jnp.concatenate(rows, axis=0)


def modulated(x, mod_ref, k):
    xhat, rstd = standardize(x)
    group = x.shape[0]
    normed = (xhat * (1.0 + mod_part(mod_ref, k + 1, group)) + mod_part(mod_ref, k, group)).astype(bf16)
    return xhat, rstd, flat(normed)


def attn_forward_body(group, fsdp, r, *refs):
    sc, x_ref, mod_ref, bias_ref, own = refs[:5]
    n = fsdp - 1
    mine, other = refs[5 : 5 + n], refs[5 + n : 5 + 2 * n]
    mid_ref, qkv_ref, att_ref, w_ref = refs[-4:]
    bias_ref = bias_ref.at[0]
    step = pl.program_id(0)

    @pl.when(step == 0)
    def _():
        place_columns(sc, own, mine, other, w_ref, r, fsdp)

    x = x_ref[...].astype(f32)
    _, _, normed = modulated(x, mod_ref, 0)
    qkv_all = (nn(normed, w_ref[:, : 3 * D]) + bias_ref[:, : 3 * D]).astype(bf16)
    qkv_ref[...] = deep(qkv_all)
    for i in range(group):
        qkv = qkv_all[i * SLOTS : (i + 1) * SLOTS]
        for p, probs in enumerate(pair_probs(qkv, sc[4 + step * group + i])):
            att = nn(probs.astype(bf16), stack_pair(pair_lanes(qkv, 2, p)))
            att_ref[i, :, 2 * HEAD_DIM * p : 2 * HEAD_DIM * (p + 1)] = att.astype(bf16)
    branch = nn(flat(att_ref[...]), w_ref[:, 3 * D :]) + bias_ref[:, 3 * D :]
    mid_ref[...] = x + mod_part(mod_ref, 2, group) * deep(branch)


def gelu(v):
    return v * (0.5 + 0.5 * jnp.tanh(v * (0.7978845608 + (0.7978845608 * 0.044715) * (v * v))))


def gelu_both(v):
    sq = v * v
    half = 0.5 + 0.5 * jnp.tanh(v * (0.7978845608 + (0.7978845608 * 0.044715) * sq))
    slope = 2.0 * 0.7978845608 + (6.0 * 0.044715 * 0.7978845608) * sq
    return v * half, half + v * slope * (half - half * half)


def ffn_forward_body(group, fsdp, r, *refs):
    sc, mid_ref, mod_ref, b1_ref, b2_ref, own1, own2 = refs[:7]
    n = fsdp - 1
    parts = [refs[7 + k * n : 7 + (k + 1) * n] for k in range(4)]
    y_ref, leave_ref, w1_ref, w2_ref = refs[-4:]
    b1_ref, b2_ref = b1_ref.at[0], b2_ref.at[0]

    @pl.when(pl.program_id(0) == 0)
    def _():
        place_columns(sc, own1, parts[0], parts[1], w1_ref, r, fsdp)
        place_rows(sc, own2, parts[2], parts[3], w2_ref, r, fsdp)

    mid = mid_ref[...]
    _, _, normed = modulated(mid, mod_ref, 3)
    act = gelu(nn(normed, w1_ref[...]) + b1_ref[...]).astype(bf16)
    leaving = deep(nn(act, w2_ref[...]) + b2_ref[...])
    leave_ref[...] = leaving
    y_ref[...] = mid + mod_part(mod_ref, 5, group) * leaving


def accumulate(ref, val):
    @pl.when(pl.program_id(0) == 0)
    def _():
        ref[...] = val

    @pl.when(pl.program_id(0) > 0)
    def _():
        ref[...] += val


def ffn_back_core(
    group, g_y, xhat, rstd, normed, slope, act, leaving, mod_ref, w1, w2,
    gmid_ref, gmod_ref, bs1_ref, bs2_ref, held,
):
    normed_all, pre_all, act_all, leave_all = held
    rows = group * SLOTS
    at = pl.ds(pl.multiple_of(pl.program_id(0) * rows, rows), rows)
    g_leave = flat((mod_part(mod_ref, 5, group) * g_y).astype(bf16))
    gmod_ref[:, 2:3] = slotsum(g_y * leaving)
    g_pre = (slope * nt(g_leave, w2[...])).astype(bf16)
    normed_all[at, :] = normed
    act_all[at, :] = act
    leave_all[at, :] = g_leave
    pre_all[at, :] = g_pre
    g_n = deep(nt(g_pre, w1[...]))
    gmod_ref[:, 0:1] = slotsum(g_n)
    gmod_ref[:, 1:2] = slotsum(g_n * xhat)
    gmid_ref[...] = g_y + norm_back(g_n, xhat, rstd, mod_part(mod_ref, 4, group))
    accumulate(bs1_ref, colsum(g_pre.astype(f32)))
    accumulate(bs2_ref, colsum(g_leave.astype(f32)))


def ffn_weight_grads(sc, held, acc1, acc2, keep, send, r, fsdp):
    normed_all, pre_all, act_all, leave_all = held
    acc1[...] = tn(normed_all[...], pre_all[...])
    acc2[...] = tn(act_all[...], leave_all[...])
    emit_ffn(sc, acc1, acc2, keep, send, r, fsdp)


def ffn_last_body(group, fsdp, r, *refs):
    sc, mid_ref, cot_ref, mod_ref, b1_ref, b2_ref, own1, own2 = refs[:8]
    n = fsdp - 1
    parts = [refs[8 + k * n : 8 + (k + 1) * n] for k in range(4)]
    (out_ref, gmid_ref, gmod_ref, bs1_ref, bs2_ref, keep, send, w1_ref, w2_ref, acc1, acc2, *held) = refs[-15:]
    b1_ref, b2_ref = b1_ref.at[0], b2_ref.at[0]
    step = pl.program_id(0)

    @pl.when(step == 0)
    def _():
        place_columns(sc, own1, parts[0], parts[1], w1_ref, r, fsdp)
        place_rows(sc, own2, parts[2], parts[3], w2_ref, r, fsdp)

    mid = mid_ref[...]
    xhat, rstd, normed = modulated(mid, mod_ref, 3)
    act, slope = gelu_both(nn(normed, w1_ref[...]) + b1_ref[...])
    act = act.astype(bf16)
    leaving = deep(nn(act, w2_ref[...]) + b2_ref[...])
    out_ref[...] = (mid + mod_part(mod_ref, 5, group) * leaving).astype(bf16)
    slots = lax.broadcasted_iota(jnp.int32, (1, SLOTS, 1), 1)
    g_y = jnp.concatenate(
        [
            jnp.where(slots < sc[4 + step * group + i], cot_ref[i : i + 1].astype(f32), 0.0)
            for i in range(group)
        ],
        axis=0,
    )
    ffn_back_core(
        group, g_y, xhat, rstd, normed, slope, act, leaving, mod_ref, w1_ref, w2_ref,
        gmid_ref, gmod_ref, bs1_ref, bs2_ref, held,
    )

    @pl.when(step == IMG // group - 1)
    def _():
        ffn_weight_grads(sc, held, acc1, acc2, keep, send, r, fsdp)


def ffn_back_body(group, fsdp, r, *refs):
    sc, gy_ref, mid_ref, mod_ref, b1_ref, leave_ref, w1_ref, w2_ref = refs[:8]
    (gmid_ref, gmod_ref, bs1_ref, bs2_ref, keep, send, acc1, acc2, *held) = refs[-12:]
    xhat, rstd, normed = modulated(mid_ref[...], mod_ref, 3)
    act, slope = gelu_both(nn(normed, w1_ref[...]) + b1_ref[0])
    ffn_back_core(
        group, gy_ref[...], xhat, rstd, normed, slope, act.astype(bf16), leave_ref[...], mod_ref,
        w1_ref, w2_ref, gmid_ref, gmod_ref, bs1_ref, bs2_ref, held,
    )

    @pl.when(pl.program_id(0) == IMG // group - 1)
    def _():
        ffn_weight_grads(sc, held, acc1, acc2, keep, send, r, fsdp)


def attn_back_body(group, fsdp, r, *refs):
    (sc, gmid_ref, x_ref, mod_ref, bias_ref, qkv_ref, att_ref, w_ref) = refs[:8]
    (gx_ref, gmod_ref, bs_ref, keep, send, acc, normed_all, gproj_all, att_all, branch_all) = refs[-10:]
    bias_ref = bias_ref.at[0]
    step = pl.program_id(0)
    rows = group * SLOTS
    at = pl.ds(pl.multiple_of(step * rows, rows), rows)
    gmid = gmid_ref[...]
    att = flat(att_ref[...])
    g_branch = flat((mod_part(mod_ref, 2, group) * gmid).astype(bf16))
    g_att_all = nt(g_branch, w_ref[:, 3 * D :]).astype(bf16)
    low_half = half_lane()
    for i in range(group):
        qkv = qkv_ref[i]
        g_att = g_att_all[i * SLOTS : (i + 1) * SLOTS]
        live_slots = sc[4 + step * group + i]
        g_probs = [nt(pair_lanes(g_att, 0, p), stack_pair(pair_lanes(qkv, 2, p))) for p in range(3)]
        all_probs = pair_probs(qkv, live_slots)
        live = lax.broadcasted_iota(jnp.int32, (1, SLOTS), 1) < live_slots
        for p in range(3):
            q, k, ga = pair_lanes(qkv, 0, p), pair_lanes(qkv, 1, p), pair_lanes(g_att, 0, p)
            g_s = []
            for h in range(2):
                gp = g_probs[p][:, h * SLOTS : (h + 1) * SLOTS]
                probs = all_probs[p][:, h * SLOTS : (h + 1) * SLOTS]
                row = jnp.sum(gp * probs, axis=-1, keepdims=True)
                val = jnp.where(live, probs * (gp - row), 0.0)
                g_s.append(val.astype(bf16))
            g_s = jnp.concatenate(g_s, axis=1)
            part = jnp.asarray(HEAD_DIM ** (-0.5), bf16)
            gq = nn(g_s, stack_pair(k * part))
            gk = tn(g_s, q * part)
            gv = tn(all_probs[p].astype(bf16), ga)
            gk = jnp.where(low_half, gk[:SLOTS], gk[SLOTS:])
            gv = jnp.where(low_half, gv[:SLOTS], gv[SLOTS:])
            here = pl.ds(pl.multiple_of(step * rows + i * SLOTS, SLOTS), SLOTS)
            for t, val in enumerate((gq, gk, gv)):
                lanes = slice(t * D + 2 * HEAD_DIM * p, t * D + 2 * HEAD_DIM * (p + 1))
                gproj_all[here, lanes] = val.astype(bf16)
    branch = deep(nn(att, w_ref[:, 3 * D :]) + bias_ref[:, 3 * D :])
    gmod_ref[:, 2:3] = slotsum(gmid * branch)
    xhat, rstd, normed = modulated(x_ref[...].astype(f32), mod_ref, 0)
    normed_all[at, :] = normed
    att_all[at, :] = att
    branch_all[at, :] = g_branch
    gp = gproj_all[at, :]
    g_n = deep(nt(gp, w_ref[:, : 3 * D]))
    gmod_ref[:, 0:1] = slotsum(g_n)
    gmod_ref[:, 1:2] = slotsum(g_n * xhat)
    gx_ref[...] = gmid + norm_back(g_n, xhat, rstd, mod_part(mod_ref, 1, group))
    accumulate(bs_ref, jnp.concatenate([colsum(gp.astype(f32)), colsum(g_branch.astype(f32))], axis=1))

    @pl.when(step == IMG // group - 1)
    def _():
        acc[:, : 3 * D] = tn(normed_all[...], gproj_all[...])
        acc[:, 3 * D :] = tn(att_all[...], branch_all[...])
        emit_attn(sc, acc, keep, send, r, fsdp)


GROUP = {"attn_forward": 2, "ffn_forward": 2, "ffn_last": 1, "ffn_back": 1, "attn_back": 1}


def per_image(g, *tail):
    return pl.BlockSpec((g, *tail), lambda i, s: (i, *([0] * len(tail))))


def whole(*shape):
    return pl.BlockSpec(shape, lambda i, s: (0,) * len(shape))


def shape_of(dims, dt):
    return jax.ShapeDtypeStruct(dims, dt)


ANY = pl.BlockSpec(memory_space=pl.ANY)


def in_hbm(v):
    return pltpu.with_memory_space_constraint(v, pltpu.HBM)


def in_vmem(v):
    return pltpu.with_memory_space_constraint(v, pltpu.VMEM)


def image_call(g, limit, body, sc, ins, in_specs, outs, deps=(), scratch=(), flops=0, moved=0):
    return pl.pallas_call(
        body,
        out_shape=[o[0] for o in outs],
        grid_spec=pltpu.PrefetchScalarGridSpec(
            num_scalar_prefetch=1,
            grid=(IMG // g,),
            in_specs=[*in_specs, *[ANY] * len(deps)],
            out_specs=[o[1] for o in outs],
            scratch_shapes=list(scratch),
        ),
        compiler_params=pltpu.CompilerParams(
            dimension_semantics=("arbitrary",), vmem_limit_bytes=limit * 1024 * 1024
        ),
        cost_estimate=pl.CostEstimate(flops=flops, bytes_accessed=moved, transcendentals=0),
    )(sc, *ins, *deps)


def mod_spec(g, layer):
    return pl.BlockSpec((1, IMG, ADA), lambda i, s: (layer, 0, 0))


def bias_spec(layer, width, k):
    return pl.BlockSpec((1, 1, width), lambda i, s: (layer, 0, k))


def own_spec(layer, rows, width, k):
    return pl.BlockSpec((1, rows, width), lambda i, s: (layer, 0, k))


ROW = lambda g, dt, w=D: (shape_of((IMG, SLOTS, w), dt), per_image(g, SLOTS, w))
FAR = lambda g, dt, w=D: (pltpu.HBM((IMG, SLOTS, w), dt), per_image(g, SLOTS, w))
HELD = lambda g, dt, w=D: (pltpu.VMEM((IMG, SLOTS, w), dt), per_image(g, SLOTS, w))


def attn_forward(far, sc, layer, x, mods, biases, entry, parts, deps, r, fsdp):
    pieces = [*parts[0], *parts[1]]
    g = GROUP["attn_forward"]
    return image_call(
        g,
        VMEM_IMAGE["attn_forward"],
        partial(attn_forward_body, g, fsdp, r),
        sc,
        [x, mods, biases, entry, *pieces],
        [
            per_image(g, SLOTS, D), mod_spec(g, layer), bias_spec(layer, 4 * D, 0),
            own_spec(layer, r, 4 * D, 0), *[whole(r, 2 * D)] * len(pieces),
        ],
        [
            HELD(g, f32),
            far(g, bf16, 3 * D),
            far(g, bf16),
            ((pltpu.HBM if far is FAR else pltpu.VMEM)((D, 4 * D), bf16), whole(D, 4 * D)),
        ],
        deps,
        flops=3 * 10**9,
        moved=30 * 10**6,
    )


def ffn_part_specs(layer, parts, r):
    pieces = [*parts[0], *parts[1], *parts[2], *parts[3]]
    n = len(parts[0])
    return pieces, [
        bias_spec(layer, FF, 1), bias_spec(layer, D, 14), own_spec(layer, r, FF, 1), own_spec(layer, 4 * r, D, 0),
        *[whole(r, 2 * D)] * (2 * n), *[whole(2 * r, D)] * (2 * n),
    ]


def ffn_forward(sc, layer, mid, mods, biases, entry, exits, parts, deps, r, fsdp):
    pieces, specs = ffn_part_specs(layer, parts, r)
    g = GROUP["ffn_forward"]
    return image_call(
        g,
        VMEM_IMAGE["ffn_forward"],
        partial(ffn_forward_body, g, fsdp, r),
        sc,
        [in_vmem(mid), mods, biases, biases, entry, exits, *pieces],
        [per_image(g, SLOTS, D), mod_spec(g, layer), *specs],
        [
            HELD(g, f32),
            HELD(g, f32),
            (pltpu.VMEM((D, FF), bf16), whole(D, FF)),
            (pltpu.VMEM((FF, D), bf16), whole(FF, D)),
        ],
        deps,
        flops=3 * 10**9,
        moved=30 * 10**6,
    )


def grad_outs(fsdp, m, r):
    return [
        (shape_of((fsdp, 2, m, r, D), f32), whole(fsdp, 2, m, r, D)),
        (shape_of((fsdp, 2, m, r, D), bf16), whole(fsdp, 2, m, r, D)),
    ]


def ffn_back_outs(place, g, fsdp, r):
    return [
        place(g, f32),
        (shape_of((IMG, 3, D), f32), per_image(g, 3, D)),
        (shape_of((1, FF), f32), whole(1, FF)),
        (shape_of((1, D), f32), whole(1, D)),
        *grad_outs(fsdp, 2, r),
    ]


FFN_ACC = [
    pltpu.VMEM((D, FF), f32), pltpu.VMEM((FF, D), f32),
    pltpu.VMEM((IMG * SLOTS, D), bf16), pltpu.VMEM((IMG * SLOTS, FF), bf16),
    pltpu.VMEM((IMG * SLOTS, FF), bf16), pltpu.VMEM((IMG * SLOTS, D), bf16),
]


def ffn_last(sc, layer, mid, cot, mods, biases, entry, exits, parts, deps, r, fsdp):
    pieces, specs = ffn_part_specs(layer, parts, r)
    g = GROUP["ffn_last"]
    return image_call(
        g,
        VMEM_IMAGE["ffn_last"],
        partial(ffn_last_body, g, fsdp, r),
        sc,
        [in_vmem(mid), cot, mods, biases, biases, entry, exits, *pieces],
        [per_image(g, SLOTS, D), per_image(g, SLOTS, D), mod_spec(g, layer), *specs],
        [ROW(g, bf16), *ffn_back_outs(HELD, g, fsdp, r)],
        deps,
        scratch=[pltpu.VMEM((D, FF), bf16), pltpu.VMEM((FF, D), bf16), *FFN_ACC],
        flops=8 * 10**9,
        moved=50 * 10**6,
    )


def ffn_back(sc, layer, gy, mid, mods, biases, leaving, w1, w2, deps, r, fsdp):
    g = GROUP["ffn_back"]
    return image_call(
        g,
        VMEM_IMAGE["ffn_back"],
        partial(ffn_back_body, g, fsdp, r),
        sc,
        [in_vmem(gy), in_vmem(mid), mods, biases, in_vmem(leaving), in_vmem(w1), in_vmem(w2)],
        [
            per_image(g, SLOTS, D), per_image(g, SLOTS, D), mod_spec(g, layer), bias_spec(layer, FF, 1),
            per_image(g, SLOTS, D), whole(D, FF), whole(FF, D),
        ],
        ffn_back_outs(HELD, g, fsdp, r),
        deps,
        scratch=FFN_ACC,
        flops=6 * 10**9,
        moved=50 * 10**6,
    )


def attn_back(out_row, near, sc, layer, gmid, x, mods, biases, qkv, att, w, deps, r, fsdp):
    g = GROUP["attn_back"]
    return image_call(
        g,
        VMEM_IMAGE["attn_back"],
        partial(attn_back_body, g, fsdp, r),
        sc,
        [near(gmid), x, mods, biases, near(qkv), near(att), near(w)],
        [
            per_image(g, SLOTS, D), per_image(g, SLOTS, D), mod_spec(g, layer), bias_spec(layer, 4 * D, 0),
            per_image(g, SLOTS, 3 * D), per_image(g, SLOTS, D), whole(D, 4 * D),
        ],
        [
            out_row(g, f32),
            (shape_of((IMG, 3, D), f32), per_image(g, 3, D)),
            (shape_of((1, 4 * D), f32), whole(1, 4 * D)),
            *grad_outs(fsdp, 1, r),
        ],
        deps,
        scratch=[
            pltpu.VMEM((D, 4 * D), f32), pltpu.VMEM((IMG * SLOTS, D), bf16),
            pltpu.VMEM((IMG * SLOTS, 3 * D), bf16), pltpu.VMEM((IMG * SLOTS, D), bf16),
            pltpu.VMEM((IMG * SLOTS, D), bf16),
        ],
        flops=6 * 10**9,
        moved=50 * 10**6,
    )


def mod_body(fsdp, *refs):
    ws, conds, outs = refs[:3], refs[3][...], refs[4:]
    for k in range(3):
        val = nn(conds, ws[k][0].astype(bf16))
        for j in range(fsdp):
            outs[j][0, :, 2 * D * k : 2 * D * (k + 1)] = val[j * IMG : (j + 1) * IMG]


def mod_partial(entry, cond_rows, r, fsdp):
    return pl.pallas_call(
        partial(mod_body, fsdp),
        out_shape=[shape_of((LAYERS, IMG, ADA), f32)] * fsdp,
        grid=(LAYERS,),
        in_specs=[
            *[pl.BlockSpec((1, r, 2 * D), lambda l, k=k: (l, 0, 4 + k)) for k in range(3)],
            pl.BlockSpec((fsdp * IMG, r), lambda l: (0, 0)),
        ],
        out_specs=[pl.BlockSpec((1, IMG, ADA), lambda l: (l, 0, 0))] * fsdp,
        compiler_params=pltpu.CompilerParams(vmem_limit_bytes=VMEM_BYTES),
        cost_estimate=pl.CostEstimate(flops=0, bytes_accessed=8 * 10**6, transcendentals=0),
    )(entry, entry, entry, cond_rows)


def cond_back_body(*refs):
    gs, ws, out_ref = refs[:3], refs[3:6], refs[6]
    val = nt(gs[0][...], ws[0][0].astype(bf16))
    for k in range(1, 3):
        val = val + nt(gs[k][...], ws[k][0].astype(bf16))

    @pl.when(pl.program_id(0) == 0)
    def _():
        out_ref[...] = val

    @pl.when(pl.program_id(0) > 0)
    def _():
        out_ref[...] += val


def cond_back(g_rows, entry, r):
    rows = g_rows.shape[0]
    return pl.pallas_call(
        cond_back_body,
        out_shape=shape_of((rows, r), f32),
        grid=(LAYERS,),
        in_specs=[
            *[pl.BlockSpec((rows, 2 * D), lambda l, k=k: (0, l * 3 + k)) for k in range(3)],
            *[pl.BlockSpec((1, r, 2 * D), lambda l, k=k: (l, 0, 4 + k)) for k in range(3)],
        ],
        out_specs=pl.BlockSpec((rows, r), lambda l: (0, 0)),
        compiler_params=pltpu.CompilerParams(vmem_limit_bytes=VMEM_BYTES),
        cost_estimate=pl.CostEstimate(flops=0, bytes_accessed=8 * 10**6, transcendentals=0),
    )(*[g_rows] * 3, *[entry] * 3)


def adam_math(gradient, master, moment, square):
    new_moment = beta_one * moment + (1.0 - beta_one) * gradient
    new_square = beta_two * square + (1.0 - beta_two) * gradient * gradient
    first_fix = 1.0 / (1.0 - beta_one**STEP)
    second_fix = 1.0 / (1.0 - beta_two**STEP)
    direction = (
        new_moment * first_fix / (jnp.sqrt(new_square * second_fix) + adam_eps) + decay_rate * master
    )
    new_master = master - learn_rate * direction
    return new_moment, new_square, new_master


def pick_part(grads, kc, ky, i):
    low = jnp.where(ky == 0, grads[0][i], grads[1][i])
    high = jnp.where(ky == 0, grads[2][i], grads[3][i])
    return jnp.where(kc == 0, low, high).astype(f32)


def attn_gradient(sc, grads, cb):
    both = [pick_part(grads, sc[0] ^ cb, sc[1] ^ yb, 0) for yb in range(2)]
    return jnp.concatenate(both, axis=1)


def ffn_gradient(sc, grads, cb, yb):
    both = [pick_part(grads, sc[0] ^ cb, sc[1] ^ yb, i) for i in range(2)]
    return jnp.concatenate(both, axis=1 - cb)


def ada_gradient(sc, grads, layer, k):
    cond, gmod = grads
    at = slice((layer * 3 + k) * 2 * D, (layer * 3 + k + 1) * 2 * D)
    return tn(cond[...], gmod[:, at])


def adam_body(pieces, n_grad, n_group, n_prev, scale, sc, *refs):
    grads = refs[:n_grad]
    states = [refs[n_grad + 3 * k : n_grad + 3 * k + 3] for k in range(n_group)]
    at = n_grad + 3 * n_group + n_prev
    outs = [refs[at + 5 * k : at + 5 * k + 5] for k in range(n_group)]
    scratch = refs[at + 5 * n_group :]
    sem_in, sem_out = scratch[-2:]
    held = [scratch[5 * p : 5 * p + 5] for p in range(len(pieces))]
    fetches = []
    for p, (group, place, _) in enumerate(pieces):
        mine = [
            pltpu.make_async_copy(states[group][t].at[place], held[p][t], sem_in.at[p, t]) for t in range(3)
        ]
        for copy in mine:
            copy.start()
        fetches.append(mine)
    writes = []
    for p, (group, place, gradient) in enumerate(pieces):
        for copy in fetches[p]:
            copy.wait()
        master_ref, moment_ref, square_ref, grad_ref, weight_ref = held[p]
        grad = gradient(sc, grads) * scale
        moment, square, master = adam_math(grad, master_ref[...], moment_ref[...], square_ref[...])
        grad_ref[...] = grad
        moment_ref[...] = moment
        square_ref[...] = square
        master_ref[...] = master
        weight_ref[...] = master.astype(bf16)
        order = (grad_ref, moment_ref, square_ref, master_ref, weight_ref)
        for t in range(5):
            copy = pltpu.make_async_copy(order[t], outs[group][t].at[place], sem_out.at[p, t])
            copy.start()
            writes.append(copy)
    for copy in writes:
        copy.wait()


def adam_call(sc, pieces, shapes, grads, groups, scale):
    ins = [*grads]
    for states, _ in groups:
        ins += states
    prev, aliases = [], {}
    for k, (_, done) in enumerate(groups):
        if done is not None:
            for t in range(5):
                aliases[1 + len(ins) + len(prev) + t] = 5 * k + t
            prev += [in_hbm(v) for v in done]
    outs, scratch = [], []
    for states, _ in groups:
        outs += [pltpu.HBM(states[0].shape, f32)] * 4 + [pltpu.HBM(states[0].shape, bf16)]
    for shape in shapes:
        scratch += [pltpu.VMEM(shape, f32)] * 4 + [pltpu.VMEM(shape, bf16)]
    scratch += [pltpu.SemaphoreType.DMA((len(pieces), 3)), pltpu.SemaphoreType.DMA((len(pieces), 5))]
    got = pl.pallas_call(
        partial(adam_body, pieces, len(grads), len(groups), len(prev), scale),
        out_shape=outs,
        grid_spec=pltpu.PrefetchScalarGridSpec(
            num_scalar_prefetch=1,
            grid=(1,),
            in_specs=[
                *[pl.BlockSpec(g.shape, lambda i, s, n=len(g.shape): (0,) * n) for g in grads],
                *[ANY] * (len(ins) - len(grads) + len(prev)),
            ],
            out_specs=[ANY] * len(outs),
            scratch_shapes=scratch,
        ),
        input_output_aliases=aliases,
        compiler_params=pltpu.CompilerParams(
            dimension_semantics=("arbitrary",), vmem_limit_bytes=VMEM_BYTES
        ),
        cost_estimate=pl.CostEstimate(flops=0, bytes_accessed=10**7, transcendentals=0),
    )(sc, *ins, *prev)
    return [list(got[5 * k : 5 * k + 5]) for k in range(len(groups))]


def adam_attn(sc, grads, states, layer, scale, prev, r):
    pieces = [
        (0, (layer, slice(None), slice(cb * 2 * D, (cb + 1) * 2 * D)), partial(attn_gradient, cb=cb))
        for cb in range(2)
    ]
    return adam_call(sc, pieces, [(r, 2 * D)] * 2, grads, [(states, prev)], scale)[0]


def adam_ffn(sc, grads, entry, exits, layer, scale, prev_e, prev_x, r):
    pieces = [
        (0, (layer, slice(None), slice((2 + yb) * 2 * D, (3 + yb) * 2 * D)), partial(ffn_gradient, cb=0, yb=yb))
        for yb in range(2)
    ]
    pieces += [
        (1, (layer, slice(yb * 2 * r, (yb + 1) * 2 * r), slice(None)), partial(ffn_gradient, cb=1, yb=yb))
        for yb in range(2)
    ]
    shapes = [(r, 2 * D)] * 2 + [(2 * r, D)] * 2
    return adam_call(sc, pieces, shapes, grads, [(entry, prev_e), (exits, prev_x)], scale)


def adam_ada(sc, cond_own, gmod_all, states, scale, prev, r):
    pieces = [
        (0, (layer, slice(None), slice((4 + k) * 2 * D, (5 + k) * 2 * D)), partial(ada_gradient, layer=layer, k=k))
        for layer in range(LAYERS)
        for k in range(3)
    ]
    return adam_call(sc, pieces, [(r, 2 * D)] * 6, [cond_own, gmod_all], [(states, prev)], scale)[0]


def swap(v, axis, bit):
    size = lax.axis_size(axis)
    return lax.ppermute(v, axis, [(i, i ^ bit) for i in range(size)])


def spread_fsdp(v, fsdp):
    held = [v]
    bit = 1
    while bit < fsdp:
        held = held + [swap(a, "fsdp", bit) for a in held]
        bit *= 2
    return held


def low_round(v):
    return lax.reduce_precision(v, 8, 7)


def swap_both(v, j, bit):
    size = lax.axis_size("dp") * lax.axis_size("fsdp")
    mask = bit * lax.axis_size("fsdp") + j
    return lax.ppermute(v, ("dp", "fsdp"), [(i, i ^ mask) for i in range(size)])


class Unit:
    def __init__(self, keep, send, dp, fsdp):
        self.fsdp = fsdp
        self.total, self.out = keep, send
        self.plan = [("core", 0), ("scatter", 0)]
        bit = 4
        while bit < dp:
            self.plan.append(("sum", bit))
            bit *= 2
        self.plan += [("share", 2), ("pair", 1)]
        self.at = 0
        self.got = None

    def step(self):
        kind, bit = self.plan[self.at]
        self.at += 1
        if kind == "core":
            self.got = swap(self.out, "dp", 1)
            return [self.out]
        if kind == "scatter":
            total = self.total + self.got.astype(f32)
            outs, self.got = [], []
            for j in range(self.fsdp):
                for ky in range(2):
                    if j or ky:
                        outs.append(total[j, ky].astype(bf16))
                        self.got.append(swap_both(outs[-1], j, 2 * ky))
            self.total = total[0, 0]
            return outs
        if kind in ("sum", "share"):
            got = self.got if isinstance(self.got, (list, tuple)) else [self.got]
            for part in got:
                self.total = self.total + part.astype(f32)
        if kind == "sum":
            self.total = low_round(self.total)
            out = self.total.astype(bf16)
            self.got = swap(out, "dp", bit)
        elif kind == "share":
            out = self.total.astype(bf16)
            self.total = out
            self.got = swap(out, "dp", bit)
        else:
            out = self.got
            self.total = (self.total, self.got)
            self.got = tuple(swap(v, "dp", 1) for v in self.total)
        return [out]

    def result(self):
        return (*self.total, *self.got)

    def done(self):
        return self.at == len(self.plan)


def hold(movers, values):
    tied = lax.optimization_barrier((tuple(values), tuple((m.total, m.got) for m in movers)))
    for m, (total, got) in zip(movers, tied[1]):
        m.total, m.got = total, got
    return tied[0]


class Chain:
    def __init__(self, rows, sums, hops):
        self.total, self.hops, self.got = (rows, sums), hops, None
        self.at = 0

    def step(self):
        self.settle()
        axis, bit = self.hops[self.at]
        self.at += 1
        self.got = tuple(swap(v, axis, bit) for v in self.total)

    def settle(self):
        if self.got is None:
            return
        axis, bit = self.hops[self.at - 1]
        rows, sums = self.total
        upper = (lax.axis_index(axis) & bit) != 0
        got = self.got[0]
        rows = jnp.concatenate([jnp.where(upper, got, rows), jnp.where(upper, rows, got)], axis=0)
        self.total = (rows, sums + self.got[1])
        self.got = None


def join(v, axis, bit):
    got = swap(v, axis, bit)
    upper = (lax.axis_index(axis) & bit) != 0
    return jnp.stack([jnp.where(upper, got, v), jnp.where(upper, v, got)], axis=0)


def per_device(
    tokens, condition, image_grid, image_counts, cotangent,
    entry_master, exit_master, bias_master,
    entry_moment, exit_moment, bias_moment,
    entry_square, exit_square, bias_square,
):
    dp, fsdp = lax.axis_size("dp"), lax.axis_size("fsdp")
    r = D // fsdp
    dp_at, f_at = lax.axis_index("dp"), lax.axis_index("fsdp")
    counted = jnp.where(
        jnp.arange(IMG) < image_counts[0], image_grid[:, 0] * image_grid[:, 1], 0
    ).astype(jnp.int32)
    sc = jnp.concatenate(
        [jnp.stack([dp_at & 1, (dp_at >> 1) & 1, f_at, f_at]).astype(jnp.int32), counted]
    )
    scale = (IMG * SLOTS * dp * fsdp) ** (-0.5)

    cond_float = condition.astype(f32)
    cond_act = jax.nn.silu(cond_float).astype(bf16)
    cond_rel = spread_fsdp(cond_act, fsdp)
    bias_low = bias_master.astype(bf16)
    bias_all = bias_low[None]
    bit = 1
    while bit < fsdp:
        bias_all = join(bias_all, "fsdp", bit).reshape(-1, *bias_low.shape)
        bit *= 2
    biases = jnp.moveaxis(bias_all, 0, 1).reshape(LAYERS, 1, -1).astype(f32)
    core = dp_at & 1

    def columns(layer, start, core):
        return lax.dynamic_slice(
            entry_master, (layer, 0, start + core * 2 * D), (1, r, 2 * D)
        )[0].astype(bf16)

    def ffn_halves(layer, core):
        low = lax.dynamic_slice(exit_master, (layer, core * 2 * r, 0), (1, 2 * r, D))[0].astype(bf16)
        return columns(layer, 4 * D, core), low

    def send_over(v):
        held = spread_fsdp(v, fsdp)
        return held[1:]

    def to_pair(parts):
        return [swap(v, "dp", 1) for v in parts]

    cond_rows = jnp.concatenate(
        [lax.dynamic_slice_in_dim(v, f_at * r, r, 1) for v in cond_rel], axis=0
    )
    attn0 = send_over(columns(0, 0, core))
    partial_mod = mod_partial(in_hbm(entry_master), cond_rows, r, fsdp)
    core_one, partial_mod, ffn_cols, ffn_rows = lax.optimization_barrier(
        (core, partial_mod, *ffn_halves(0, core))
    )
    mod_got = [swap(partial_mod[j], "fsdp", j) for j in range(1, fsdp)]
    ffn0 = send_over(ffn_cols), send_over(ffn_rows)
    core_two, attn0, mod_got = lax.optimization_barrier((core_one, attn0, mod_got))
    attn0_pair = to_pair(attn0)
    mod = partial_mod[0]
    for got in mod_got:
        mod = mod + got
    hidden_end, ada_end = 4 * D + FF, 10 * D + FF
    mods = mod + biases[:, :, hidden_end:ada_end]
    held_entry, held_exit = in_hbm(entry_master), in_hbm(exit_master)

    mid0, qkv0, att0, wa0 = attn_forward(
        HELD, sc, 0, tokens, mods, biases, held_entry, (attn0, attn0_pair), (), r, fsdp
    )
    send = (columns(1, 0, core_two), *ffn_halves(1, core_two))
    mid0, ffn0, send = lax.optimization_barrier((mid0, ffn0, send))
    ffn0_pair = to_pair(ffn0[0]), to_pair(ffn0[1])
    attn1 = send_over(send[0])
    ffn1 = send_over(send[1]), send_over(send[2])
    x1, lv0, w10, w20 = ffn_forward(
        sc, 0, mid0, mods, biases, held_entry, held_exit,
        (ffn0[0], ffn0_pair[0], ffn0[1], ffn0_pair[1]), (), r, fsdp,
    )
    x1, attn1 = lax.optimization_barrier((x1, attn1))
    attn1_pair = to_pair(attn1)
    mid1, qkv1, att1, wa1 = attn_forward(
        HELD, sc, 1, in_vmem(x1), mods, biases, held_entry, (attn1, attn1_pair), (), r, fsdp
    )
    mid1, ffn1 = lax.optimization_barrier((mid1, ffn1))
    ffn1_pair = to_pair(ffn1[0]), to_pair(ffn1[1])
    block_output, gmid1, gm1b, bs1_1, bs1_2, keep, send = ffn_last(
        sc, 1, mid1, cotangent, mods, biases, held_entry, held_exit,
        (ffn1[0], ffn1_pair[0], ffn1[1], ffn1_pair[1]), (), r, fsdp,
    )
    u_a = Unit(keep, send, dp, fsdp)
    u_a.step()
    deps = u_a.step()
    gx1, gm1a, bs1_a, keep, send = attn_back(
        HELD, in_vmem, sc, 1, gmid1, in_vmem(x1), mods, biases, qkv1, att1, wa1, deps, r, fsdp
    )
    gx1, keep, send = hold([u_a], [gx1, keep, send])
    u_b = Unit(keep, send, dp, fsdp)
    u_b.step()
    deps = u_a.step() + u_b.step()
    gmid0, gm0b, bs0_1, bs0_2, keep, send = ffn_back(
        sc, 0, gx1, mid0, mods, biases, lv0, w10, w20, deps, r, fsdp
    )
    gmid0, keep, send = hold([u_a, u_b], [gmid0, keep, send])
    u_c = Unit(keep, send, dp, fsdp)
    u_c.step()
    deps = u_a.step() + u_b.step() + u_c.step()
    grad_tokens, gm0a, bs0_a, keep, send = attn_back(
        ROW, in_vmem, sc, 0, gmid0, tokens, mods, biases, qkv0, att0, wa0, deps, r, fsdp
    )
    g_mods = [gm0a, gm0b, gm1a, gm1b]
    b_sums = [bs0_a, bs0_1, bs0_2, bs1_a, bs1_1, bs1_2]
    grad_tokens, keep, send, *tied = hold(
        [u_a, u_b, u_c], [grad_tokens, keep, send, *g_mods, *b_sums]
    )
    g_mods, b_sums = tied[:4], tied[4:]
    u_d = Unit(keep, send, dp, fsdp)
    u_d.step()
    units = [u_a, u_b, u_c, u_d]
    outs = u_d.step()
    for unit in (u_c, u_a, u_b):
        unit.step()
    wide = LAYERS * ADA
    g_mod = jnp.concatenate(g_mods, axis=1).astype(bf16).reshape(IMG, wide)
    hops = []
    bit = 1
    while bit < fsdp:
        hops.append(("fsdp", bit))
        bit *= 2
    group_hops = len(hops)
    bit = 2
    while bit < dp:
        hops.append(("dp", bit))
        bit *= 2
    hops.append(("dp", 1))
    packed, sums, _ = lax.optimization_barrier(
        (jnp.concatenate([g_mod, cond_act], axis=1), jnp.concatenate(b_sums, axis=1), outs)
    )
    chain = Chain(packed, sums, hops)
    for _ in range(group_hops):
        chain.step()
    hold([chain, *units], [])
    chain.settle()
    group_rows = chain.total[0]
    back = cond_back(group_rows, held_entry, r).reshape(fsdp, IMG, r)

    entry = [held_entry, in_hbm(entry_moment), in_hbm(entry_square)]
    exits = [held_exit, in_hbm(exit_moment), in_hbm(exit_square)]
    e = x = None
    updates = [(u_a, 1, True), (u_b, 1, False), (u_c, 0, True), (u_d, 0, False)]
    while True:
        for unit in units:
            if not unit.done():
                unit.step()
        if chain.at < len(hops) - 1:
            chain.step()
        for item in [u for u in updates if u[0].done()]:
            unit, layer, ffn = item
            updates.remove(item)
            if ffn:
                e, x = adam_ffn(sc, unit.result(), entry, exits, layer, scale, e, x, r)
            else:
                e = adam_attn(sc, unit.result(), entry, layer, scale, e, r)
        if not updates:
            break
        kept = [*(e or []), *(x or []), back]
        slow = [] if chain.at == len(hops) - 1 else [chain]
        tied = hold([*slow, *[u for u in units if not u.done()]], kept)
        back = tied[-1]
        e = tied[:5] if e else None
        x = tied[5:10] if x else None

    pieces = [lax.dynamic_index_in_dim(back, f_at, 0, keepdims=False)]
    for j in range(1, fsdp):
        pieces.append(swap(lax.dynamic_index_in_dim(back, f_at ^ j, 0, keepdims=False), "fsdp", j))
    tied = hold([chain], [*pieces, *e])
    pieces, e = tied[:fsdp], list(tied[fsdp:])
    while chain.at < len(hops):
        chain.step()
    chain.settle()
    rows, bias_sum = chain.total
    cond_own = lax.dynamic_slice_in_dim(rows, wide + f_at * r, r, 1)
    e = adam_ada(sc, cond_own, rows, entry, scale, e, r)
    g_cond = jnp.zeros((fsdp, IMG, r), f32)
    for j in range(fsdp):
        g_cond = lax.dynamic_update_index_in_dim(g_cond, pieces[j], f_at ^ j, 0)
    g_cond = jnp.moveaxis(g_cond, 0, 1).reshape(IMG, D)
    grad_condition = jax.vjp(jax.nn.silu, cond_float)[1](g_cond)[0]
    ada_bias = jnp.sum(rows[:, :wide].astype(f32), axis=0).reshape(LAYERS, ADA)
    bias_sum = bias_sum.reshape(LAYERS, -1)
    bias_sum = jnp.concatenate([bias_sum[:, :hidden_end], ada_bias, bias_sum[:, hidden_end:]], axis=1)
    width = bias_master.shape[1]
    bias_grad = lax.dynamic_slice_in_dim(bias_sum, f_at * width, width, 1) * scale
    exit_bias_grad = lax.dynamic_slice_in_dim(bias_sum[:, ada_end:], f_at * r, r, 1) * scale
    bias_moment_new, bias_square_new, bias_master_new = adam_math(
        bias_grad, bias_master, bias_moment, bias_square
    )
    return (
        block_output, grad_tokens, grad_condition,
        *e, *x,
        bias_grad, bias_moment_new, bias_square_new, bias_master_new,
        bias_master_new.astype(bf16), exit_bias_grad,
    )


def solution(mesh):
    rows = P(("dp", "fsdp"), None, None)
    flat = P(("dp", "fsdp"), None)
    mat = P(None, "fsdp", None)
    vec = P(None, "fsdp")
    return jax.shard_map(
        per_device,
        mesh=mesh,
        in_specs=(rows, flat, flat, P(("dp", "fsdp")), rows, mat, mat, vec, mat, mat, vec, mat, mat, vec),
        out_specs=(rows, rows, flat, *[mat] * 10, *[vec] * 6),
        check_vma=False,
    )
```

```python
from functools import partial

import jax
import jax.numpy as jnp
from jax import lax
from jax.experimental import pallas as pl
from jax.experimental.pallas import tpu as pltpu
from jax.sharding import PartitionSpec as P

D = 384
HEADS = 6
HEAD_DIM = 64
FF = 1536
LAYERS = 2
IMG = 4
STEP = 4
SLOTS = 256
ADA = 6 * D

eps_norm = 1e-06
neg_big = -1e30
beta_one = 0.5
beta_two = 0.6
adam_eps = 1e-08
learn_rate = 0.02
decay_rate = 0.1

f32 = jnp.float32
bf16 = jnp.bfloat16
VMEM_BYTES = 24 * 1024 * 1024
VMEM_IMAGE = {"attn_forward": 20, "ffn_forward": 23, "ffn_last": 25, "ffn_back": 21, "attn_back": 17}


def nn(a, b):
    return lax.dot_general(a, b, (((1,), (0,)), ((), ())), preferred_element_type=f32)


def nt(a, b):
    return lax.dot_general(a, b, (((1,), (1,)), ((), ())), preferred_element_type=f32)


def tn(a, b):
    return lax.dot_general(a, b, (((0,), (0,)), ((), ())), preferred_element_type=f32)


def standardize(x):
    mean = jnp.mean(x, axis=-1, keepdims=True)
    cen = x - mean
    var = jnp.mean(cen * cen, axis=-1, keepdims=True)
    rstd = lax.rsqrt(var + eps_norm)
    return cen * rstd, rstd


def norm_back(g, xhat, rstd, scale):
    t = g * (1.0 + scale)
    mean_t = jnp.mean(t, axis=-1, keepdims=True)
    mean_tx = jnp.mean(t * xhat, axis=-1, keepdims=True)
    return (t - mean_t - xhat * mean_tx) * rstd


def colsum(x):
    return jnp.sum(x, axis=0, keepdims=True)


def at_lane(i):
    return pl.ds(pl.multiple_of(i * D, 128), D)


def at_row(i, r):
    return pl.ds(pl.multiple_of(i * r, 16), r)


def place_columns(sc, own, mine, other, w_ref, r, fsdp):
    half = w_ref.shape[1] // 2
    c, f = sc[0], sc[2]
    w_ref[at_row(f, r), :] = own[0].astype(bf16)
    for j in range(1, fsdp):
        for kc, part in ((0, mine), (1, other)):
            w_ref[at_row(f ^ j, r), pl.ds(pl.multiple_of((c ^ kc) * half, 128), half)] = part[j - 1][...]


def place_rows(sc, own, mine, other, w_ref, r, fsdp):
    c, f = sc[0], sc[2]
    w_ref[at_row(f, 4 * r), :] = own[0].astype(bf16)
    for j in range(1, fsdp):
        for kc, part in ((0, mine), (1, other)):
            w_ref[at_row((f ^ j) * 2 + (c ^ kc), 2 * r), :] = part[j - 1][...]


def emit_attn(sc, acc, keep, send, r, fsdp):
    c, y, f = sc[0], sc[1], sc[2]
    for j in range(fsdp):
        for ky in range(2):
            for kc in range(2):
                blk = acc[at_row(f ^ j, r), at_lane((c ^ kc) * 2 + (y ^ ky))]
                if kc == 0:
                    keep[j, ky, 0] = blk
                else:
                    send[j, ky, 0] = blk.astype(bf16)


def emit_ffn(sc, acc1, acc2, keep, send, r, fsdp):
    c, y, f = sc[0], sc[1], sc[2]
    for kc in range(2):
        for cb in range(2):

            @pl.when((c ^ kc) == cb)
            def _(kc=kc, cb=cb):
                for j in range(fsdp):
                    for ky in range(2):
                        for i in range(2):
                            pos = (y ^ ky) * 2 + i
                            if cb == 0:
                                blk = acc1[at_row(f ^ j, r), at_lane(pos)]
                            else:
                                blk = acc2[at_row((f ^ j) * 4 + pos, r), :]
                            if kc == 0:
                                keep[j, ky, i] = blk
                            else:
                                send[j, ky, i] = blk.astype(bf16)


def half_lane():
    return lax.broadcasted_iota(jnp.int32, (1, 2 * HEAD_DIM), 1) < HEAD_DIM


def pair_lanes(qkv, third, p):
    start = third * D + 2 * HEAD_DIM * p
    return qkv[:, start : start + 2 * HEAD_DIM]


def stack_pair(v):
    low_half = half_lane()
    none = jnp.zeros_like(v)
    return jnp.concatenate([jnp.where(low_half, v, none), jnp.where(low_half, none, v)], axis=0)


def pair_probs(qkv, live_slots):
    live = lax.broadcasted_iota(jnp.int32, (1, 2 * SLOTS), 1) & (SLOTS - 1)
    live = live < live_slots
    scores = []
    for p in range(3):
        q = pair_lanes(qkv, 0, p) * jnp.asarray(HEAD_DIM ** (-0.5), bf16)
        scores.append(jnp.where(live, nt(q, stack_pair(pair_lanes(qkv, 1, p))), neg_big))
    out = []
    for s in scores:
        heads = []
        for h in range(2):
            sh = s[:, h * SLOTS : (h + 1) * SLOTS]
            e = jnp.exp(sh - jnp.max(sh, axis=-1, keepdims=True))
            heads.append(e * (1.0 / jnp.sum(e, axis=-1, keepdims=True)))
        out.append(jnp.concatenate(heads, axis=1))
    return out


def flat(v):
    return v.reshape(v.shape[0] * v.shape[1], v.shape[2])


def deep(v):
    return v.reshape(v.shape[0] // SLOTS, SLOTS, v.shape[1])


def slotsum(v):
    return jnp.sum(v, axis=1, keepdims=True)


def mod_part(mod_ref, k, group):
    if group == IMG:
        return mod_ref[0, :, k * D : (k + 1) * D][:, None, :]
    first = pl.program_id(0) * group
    rows = [mod_ref[0, pl.ds(first + i, 1), k * D : (k + 1) * D][None] for i in range(group)]
    return rows[0] if group == 1 else jnp.concatenate(rows, axis=0)


def modulated(x, mod_ref, k):
    xhat, rstd = standardize(x)
    group = x.shape[0]
    normed = (xhat * (1.0 + mod_part(mod_ref, k + 1, group)) + mod_part(mod_ref, k, group)).astype(bf16)
    return xhat, rstd, flat(normed)


def attn_forward_body(group, fsdp, r, *refs):
    sc, x_ref, mod_ref, bias_ref, own = refs[:5]
    n = fsdp - 1
    mine, other = refs[5 : 5 + n], refs[5 + n : 5 + 2 * n]
    mid_ref, qkv_ref, att_ref, w_ref = refs[-4:]
    bias_ref = bias_ref.at[0]
    step = pl.program_id(0)

    @pl.when(step == 0)
    def _():
        place_columns(sc, own, mine, other, w_ref, r, fsdp)

    x = x_ref[...].astype(f32)
    _, _, normed = modulated(x, mod_ref, 0)
    qkv_all = (nn(normed, w_ref[:, : 3 * D]) + bias_ref[:, : 3 * D]).astype(bf16)
    qkv_ref[...] = deep(qkv_all)
    for i in range(group):
        qkv = qkv_all[i * SLOTS : (i + 1) * SLOTS]
        for p, probs in enumerate(pair_probs(qkv, sc[4 + step * group + i])):
            att = nn(probs.astype(bf16), stack_pair(pair_lanes(qkv, 2, p)))
            att_ref[i, :, 2 * HEAD_DIM * p : 2 * HEAD_DIM * (p + 1)] = att.astype(bf16)
    branch = nn(flat(att_ref[...]), w_ref[:, 3 * D :]) + bias_ref[:, 3 * D :]
    mid_ref[...] = x + mod_part(mod_ref, 2, group) * deep(branch)


def gelu(v):
    return v * (0.5 + 0.5 * jnp.tanh(v * (0.7978845608 + (0.7978845608 * 0.044715) * (v * v))))


def gelu_both(v):
    sq = v * v
    half = 0.5 + 0.5 * jnp.tanh(v * (0.7978845608 + (0.7978845608 * 0.044715) * sq))
    slope = 2.0 * 0.7978845608 + (6.0 * 0.044715 * 0.7978845608) * sq
    return v * half, half + v * slope * (half - half * half)


def ffn_forward_body(group, fsdp, r, *refs):
    sc, mid_ref, mod_ref, b1_ref, b2_ref, own1, own2 = refs[:7]
    n = fsdp - 1
    parts = [refs[7 + k * n : 7 + (k + 1) * n] for k in range(4)]
    y_ref, leave_ref, w1_ref, w2_ref = refs[-4:]
    b1_ref, b2_ref = b1_ref.at[0], b2_ref.at[0]

    @pl.when(pl.program_id(0) == 0)
    def _():
        place_columns(sc, own1, parts[0], parts[1], w1_ref, r, fsdp)
        place_rows(sc, own2, parts[2], parts[3], w2_ref, r, fsdp)

    mid = mid_ref[...]
    _, _, normed = modulated(mid, mod_ref, 3)
    act = gelu(nn(normed, w1_ref[...]) + b1_ref[...]).astype(bf16)
    leaving = deep(nn(act, w2_ref[...]) + b2_ref[...])
    leave_ref[...] = leaving
    y_ref[...] = mid + mod_part(mod_ref, 5, group) * leaving


def accumulate(ref, val):
    @pl.when(pl.program_id(0) == 0)
    def _():
        ref[...] = val

    @pl.when(pl.program_id(0) > 0)
    def _():
        ref[...] += val


def ffn_back_core(
    group, g_y, xhat, rstd, normed, slope, act, leaving, mod_ref, w1, w2,
    gmid_ref, gmod_ref, bs1_ref, bs2_ref, held,
):
    normed_all, pre_all, act_all, leave_all = held
    rows = group * SLOTS
    at = pl.ds(pl.multiple_of(pl.program_id(0) * rows, rows), rows)
    g_leave = flat((mod_part(mod_ref, 5, group) * g_y).astype(bf16))
    gmod_ref[:, 2:3] = slotsum(g_y * leaving)
    g_pre = (slope * nt(g_leave, w2[...])).astype(bf16)
    normed_all[at, :] = normed
    act_all[at, :] = act
    leave_all[at, :] = g_leave
    pre_all[at, :] = g_pre
    g_n = deep(nt(g_pre, w1[...]))
    gmod_ref[:, 0:1] = slotsum(g_n)
    gmod_ref[:, 1:2] = slotsum(g_n * xhat)
    gmid_ref[...] = g_y + norm_back(g_n, xhat, rstd, mod_part(mod_ref, 4, group))
    accumulate(bs1_ref, colsum(g_pre.astype(f32)))
    accumulate(bs2_ref, colsum(g_leave.astype(f32)))


def ffn_weight_grads(sc, held, acc1, acc2, keep, send, r, fsdp):
    normed_all, pre_all, act_all, leave_all = held
    acc1[...] = tn(normed_all[...], pre_all[...])
    acc2[...] = tn(act_all[...], leave_all[...])
    emit_ffn(sc, acc1, acc2, keep, send, r, fsdp)


def ffn_last_body(group, fsdp, r, *refs):
    sc, mid_ref, cot_ref, mod_ref, b1_ref, b2_ref, own1, own2 = refs[:8]
    n = fsdp - 1
    parts = [refs[8 + k * n : 8 + (k + 1) * n] for k in range(4)]
    (out_ref, gmid_ref, gmod_ref, bs1_ref, bs2_ref, keep, send, w1_ref, w2_ref, acc1, acc2, *held) = refs[-15:]
    b1_ref, b2_ref = b1_ref.at[0], b2_ref.at[0]
    step = pl.program_id(0)

    @pl.when(step == 0)
    def _():
        place_columns(sc, own1, parts[0], parts[1], w1_ref, r, fsdp)
        place_rows(sc, own2, parts[2], parts[3], w2_ref, r, fsdp)

    mid = mid_ref[...]
    xhat, rstd, normed = modulated(mid, mod_ref, 3)
    act, slope = gelu_both(nn(normed, w1_ref[...]) + b1_ref[...])
    act = act.astype(bf16)
    leaving = deep(nn(act, w2_ref[...]) + b2_ref[...])
    out_ref[...] = (mid + mod_part(mod_ref, 5, group) * leaving).astype(bf16)
    slots = lax.broadcasted_iota(jnp.int32, (1, SLOTS, 1), 1)
    g_y = jnp.concatenate(
        [
            jnp.where(slots < sc[4 + step * group + i], cot_ref[i : i + 1].astype(f32), 0.0)
            for i in range(group)
        ],
        axis=0,
    )
    ffn_back_core(
        group, g_y, xhat, rstd, normed, slope, act, leaving, mod_ref, w1_ref, w2_ref,
        gmid_ref, gmod_ref, bs1_ref, bs2_ref, held,
    )

    @pl.when(step == IMG // group - 1)
    def _():
        ffn_weight_grads(sc, held, acc1, acc2, keep, send, r, fsdp)


def ffn_back_body(group, fsdp, r, *refs):
    sc, gy_ref, mid_ref, mod_ref, b1_ref, leave_ref, w1_ref, w2_ref = refs[:8]
    (gmid_ref, gmod_ref, bs1_ref, bs2_ref, keep, send, acc1, acc2, *held) = refs[-12:]
    xhat, rstd, normed = modulated(mid_ref[...], mod_ref, 3)
    act, slope = gelu_both(nn(normed, w1_ref[...]) + b1_ref[0])
    ffn_back_core(
        group, gy_ref[...], xhat, rstd, normed, slope, act.astype(bf16), leave_ref[...], mod_ref,
        w1_ref, w2_ref, gmid_ref, gmod_ref, bs1_ref, bs2_ref, held,
    )

    @pl.when(pl.program_id(0) == IMG // group - 1)
    def _():
        ffn_weight_grads(sc, held, acc1, acc2, keep, send, r, fsdp)


def attn_back_body(group, fsdp, r, *refs):
    (sc, gmid_ref, x_ref, mod_ref, bias_ref, qkv_ref, att_ref, w_ref) = refs[:8]
    (gx_ref, gmod_ref, bs_ref, keep, send, acc, normed_all, gproj_all, att_all, branch_all) = refs[-10:]
    bias_ref = bias_ref.at[0]
    step = pl.program_id(0)
    rows = group * SLOTS
    at = pl.ds(pl.multiple_of(step * rows, rows), rows)
    gmid = gmid_ref[...]
    att = flat(att_ref[...])
    g_branch = flat((mod_part(mod_ref, 2, group) * gmid).astype(bf16))
    g_att_all = nt(g_branch, w_ref[:, 3 * D :]).astype(bf16)
    low_half = half_lane()
    for i in range(group):
        qkv = qkv_ref[i]
        g_att = g_att_all[i * SLOTS : (i + 1) * SLOTS]
        live_slots = sc[4 + step * group + i]
        g_probs = [nt(pair_lanes(g_att, 0, p), stack_pair(pair_lanes(qkv, 2, p))) for p in range(3)]
        all_probs = pair_probs(qkv, live_slots)
        live = lax.broadcasted_iota(jnp.int32, (1, SLOTS), 1) < live_slots
        for p in range(3):
            q, k, ga = pair_lanes(qkv, 0, p), pair_lanes(qkv, 1, p), pair_lanes(g_att, 0, p)
            g_s = []
            for h in range(2):
                gp = g_probs[p][:, h * SLOTS : (h + 1) * SLOTS]
                probs = all_probs[p][:, h * SLOTS : (h + 1) * SLOTS]
                row = jnp.sum(gp * probs, axis=-1, keepdims=True)
                val = jnp.where(live, probs * (gp - row), 0.0)
                g_s.append(val.astype(bf16))
            g_s = jnp.concatenate(g_s, axis=1)
            part = jnp.asarray(HEAD_DIM ** (-0.5), bf16)
            gq = nn(g_s, stack_pair(k * part))
            gk = tn(g_s, q * part)
            gv = tn(all_probs[p].astype(bf16), ga)
            gk = jnp.where(low_half, gk[:SLOTS], gk[SLOTS:])
            gv = jnp.where(low_half, gv[:SLOTS], gv[SLOTS:])
            here = pl.ds(pl.multiple_of(step * rows + i * SLOTS, SLOTS), SLOTS)
            for t, val in enumerate((gq, gk, gv)):
                lanes = slice(t * D + 2 * HEAD_DIM * p, t * D + 2 * HEAD_DIM * (p + 1))
                gproj_all[here, lanes] = val.astype(bf16)
    branch = deep(nn(att, w_ref[:, 3 * D :]) + bias_ref[:, 3 * D :])
    gmod_ref[:, 2:3] = slotsum(gmid * branch)
    xhat, rstd, normed = modulated(x_ref[...].astype(f32), mod_ref, 0)
    normed_all[at, :] = normed
    att_all[at, :] = att
    branch_all[at, :] = g_branch
    gp = gproj_all[at, :]
    g_n = deep(nt(gp, w_ref[:, : 3 * D]))
    gmod_ref[:, 0:1] = slotsum(g_n)
    gmod_ref[:, 1:2] = slotsum(g_n * xhat)
    gx_ref[...] = gmid + norm_back(g_n, xhat, rstd, mod_part(mod_ref, 1, group))
    accumulate(bs_ref, jnp.concatenate([colsum(gp.astype(f32)), colsum(g_branch.astype(f32))], axis=1))

    @pl.when(step == IMG // group - 1)
    def _():
        acc[:, : 3 * D] = tn(normed_all[...], gproj_all[...])
        acc[:, 3 * D :] = tn(att_all[...], branch_all[...])
        emit_attn(sc, acc, keep, send, r, fsdp)


GROUP = {"attn_forward": 2, "ffn_forward": 2, "ffn_last": 1, "ffn_back": 1, "attn_back": 1}


def per_image(g, *tail):
    return pl.BlockSpec((g, *tail), lambda i, s: (i, *([0] * len(tail))))


def whole(*shape):
    return pl.BlockSpec(shape, lambda i, s: (0,) * len(shape))


def shape_of(dims, dt):
    return jax.ShapeDtypeStruct(dims, dt)


ANY = pl.BlockSpec(memory_space=pl.ANY)


def in_hbm(v):
    return pltpu.with_memory_space_constraint(v, pltpu.HBM)


def in_vmem(v):
    return pltpu.with_memory_space_constraint(v, pltpu.VMEM)


def image_call(g, limit, body, sc, ins, in_specs, outs, deps=(), scratch=(), flops=0, moved=0):
    return pl.pallas_call(
        body,
        out_shape=[o[0] for o in outs],
        grid_spec=pltpu.PrefetchScalarGridSpec(
            num_scalar_prefetch=1,
            grid=(IMG // g,),
            in_specs=[*in_specs, *[ANY] * len(deps)],
            out_specs=[o[1] for o in outs],
            scratch_shapes=list(scratch),
        ),
        compiler_params=pltpu.CompilerParams(
            dimension_semantics=("arbitrary",), vmem_limit_bytes=limit * 1024 * 1024
        ),
        cost_estimate=pl.CostEstimate(flops=flops, bytes_accessed=moved, transcendentals=0),
    )(sc, *ins, *deps)


def mod_spec(g, layer):
    return pl.BlockSpec((1, IMG, ADA), lambda i, s: (layer, 0, 0))


def bias_spec(layer, width, k):
    return pl.BlockSpec((1, 1, width), lambda i, s: (layer, 0, k))


def own_spec(layer, rows, width, k):
    return pl.BlockSpec((1, rows, width), lambda i, s: (layer, 0, k))


ROW = lambda g, dt, w=D: (shape_of((IMG, SLOTS, w), dt), per_image(g, SLOTS, w))
FAR = lambda g, dt, w=D: (pltpu.HBM((IMG, SLOTS, w), dt), per_image(g, SLOTS, w))
HELD = lambda g, dt, w=D: (pltpu.VMEM((IMG, SLOTS, w), dt), per_image(g, SLOTS, w))


def attn_forward(far, sc, layer, x, mods, biases, entry, parts, deps, r, fsdp):
    pieces = [*parts[0], *parts[1]]
    g = GROUP["attn_forward"]
    return image_call(
        g,
        VMEM_IMAGE["attn_forward"],
        partial(attn_forward_body, g, fsdp, r),
        sc,
        [x, mods, biases, entry, *pieces],
        [
            per_image(g, SLOTS, D), mod_spec(g, layer), bias_spec(layer, 4 * D, 0),
            own_spec(layer, r, 4 * D, 0), *[whole(r, 2 * D)] * len(pieces),
        ],
        [
            HELD(g, f32),
            far(g, bf16, 3 * D),
            far(g, bf16),
            ((pltpu.HBM if far is FAR else pltpu.VMEM)((D, 4 * D), bf16), whole(D, 4 * D)),
        ],
        deps,
        flops=3 * 10**9,
        moved=30 * 10**6,
    )


def ffn_part_specs(layer, parts, r):
    pieces = [*parts[0], *parts[1], *parts[2], *parts[3]]
    n = len(parts[0])
    return pieces, [
        bias_spec(layer, FF, 1), bias_spec(layer, D, 14), own_spec(layer, r, FF, 1), own_spec(layer, 4 * r, D, 0),
        *[whole(r, 2 * D)] * (2 * n), *[whole(2 * r, D)] * (2 * n),
    ]


def ffn_forward(sc, layer, mid, mods, biases, entry, exits, parts, deps, r, fsdp):
    pieces, specs = ffn_part_specs(layer, parts, r)
    g = GROUP["ffn_forward"]
    return image_call(
        g,
        VMEM_IMAGE["ffn_forward"],
        partial(ffn_forward_body, g, fsdp, r),
        sc,
        [in_vmem(mid), mods, biases, biases, entry, exits, *pieces],
        [per_image(g, SLOTS, D), mod_spec(g, layer), *specs],
        [
            HELD(g, f32),
            HELD(g, f32),
            (pltpu.VMEM((D, FF), bf16), whole(D, FF)),
            (pltpu.VMEM((FF, D), bf16), whole(FF, D)),
        ],
        deps,
        flops=3 * 10**9,
        moved=30 * 10**6,
    )


def grad_outs(fsdp, m, r):
    return [
        (shape_of((fsdp, 2, m, r, D), f32), whole(fsdp, 2, m, r, D)),
        (shape_of((fsdp, 2, m, r, D), bf16), whole(fsdp, 2, m, r, D)),
    ]


def ffn_back_outs(place, g, fsdp, r):
    return [
        place(g, f32),
        (shape_of((IMG, 3, D), f32), per_image(g, 3, D)),
        (shape_of((1, FF), f32), whole(1, FF)),
        (shape_of((1, D), f32), whole(1, D)),
        *grad_outs(fsdp, 2, r),
    ]


FFN_ACC = [
    pltpu.VMEM((D, FF), f32), pltpu.VMEM((FF, D), f32),
    pltpu.VMEM((IMG * SLOTS, D), bf16), pltpu.VMEM((IMG * SLOTS, FF), bf16),
    pltpu.VMEM((IMG * SLOTS, FF), bf16), pltpu.VMEM((IMG * SLOTS, D), bf16),
]


def ffn_last(sc, layer, mid, cot, mods, biases, entry, exits, parts, deps, r, fsdp):
    pieces, specs = ffn_part_specs(layer, parts, r)
    g = GROUP["ffn_last"]
    return image_call(
        g,
        VMEM_IMAGE["ffn_last"],
        partial(ffn_last_body, g, fsdp, r),
        sc,
        [in_vmem(mid), cot, mods, biases, biases, entry, exits, *pieces],
        [per_image(g, SLOTS, D), per_image(g, SLOTS, D), mod_spec(g, layer), *specs],
        [ROW(g, bf16), *ffn_back_outs(HELD, g, fsdp, r)],
        deps,
        scratch=[pltpu.VMEM((D, FF), bf16), pltpu.VMEM((FF, D), bf16), *FFN_ACC],
        flops=8 * 10**9,
        moved=50 * 10**6,
    )


def ffn_back(sc, layer, gy, mid, mods, biases, leaving, w1, w2, deps, r, fsdp):
    g = GROUP["ffn_back"]
    return image_call(
        g,
        VMEM_IMAGE["ffn_back"],
        partial(ffn_back_body, g, fsdp, r),
        sc,
        [in_vmem(gy), in_vmem(mid), mods, biases, in_vmem(leaving), in_vmem(w1), in_vmem(w2)],
        [
            per_image(g, SLOTS, D), per_image(g, SLOTS, D), mod_spec(g, layer), bias_spec(layer, FF, 1),
            per_image(g, SLOTS, D), whole(D, FF), whole(FF, D),
        ],
        ffn_back_outs(HELD, g, fsdp, r),
        deps,
        scratch=FFN_ACC,
        flops=6 * 10**9,
        moved=50 * 10**6,
    )


def attn_back(out_row, near, sc, layer, gmid, x, mods, biases, qkv, att, w, deps, r, fsdp):
    g = GROUP["attn_back"]
    return image_call(
        g,
        VMEM_IMAGE["attn_back"],
        partial(attn_back_body, g, fsdp, r),
        sc,
        [near(gmid), x, mods, biases, near(qkv), near(att), near(w)],
        [
            per_image(g, SLOTS, D), per_image(g, SLOTS, D), mod_spec(g, layer), bias_spec(layer, 4 * D, 0),
            per_image(g, SLOTS, 3 * D), per_image(g, SLOTS, D), whole(D, 4 * D),
        ],
        [
            out_row(g, f32),
            (shape_of((IMG, 3, D), f32), per_image(g, 3, D)),
            (shape_of((1, 4 * D), f32), whole(1, 4 * D)),
            *grad_outs(fsdp, 1, r),
        ],
        deps,
        scratch=[
            pltpu.VMEM((D, 4 * D), f32), pltpu.VMEM((IMG * SLOTS, D), bf16),
            pltpu.VMEM((IMG * SLOTS, 3 * D), bf16), pltpu.VMEM((IMG * SLOTS, D), bf16),
            pltpu.VMEM((IMG * SLOTS, D), bf16),
        ],
        flops=6 * 10**9,
        moved=50 * 10**6,
    )


def mod_body(fsdp, *refs):
    ws, conds, outs = refs[:3], refs[3][...], refs[4:]
    for k in range(3):
        val = nn(conds, ws[k][0].astype(bf16))
        for j in range(fsdp):
            outs[j][0, :, 2 * D * k : 2 * D * (k + 1)] = val[j * IMG : (j + 1) * IMG]


def mod_partial(entry, cond_rows, r, fsdp):
    return pl.pallas_call(
        partial(mod_body, fsdp),
        out_shape=[shape_of((LAYERS, IMG, ADA), f32)] * fsdp,
        grid=(LAYERS,),
        in_specs=[
            *[pl.BlockSpec((1, r, 2 * D), lambda l, k=k: (l, 0, 4 + k)) for k in range(3)],
            pl.BlockSpec((fsdp * IMG, r), lambda l: (0, 0)),
        ],
        out_specs=[pl.BlockSpec((1, IMG, ADA), lambda l: (l, 0, 0))] * fsdp,
        compiler_params=pltpu.CompilerParams(vmem_limit_bytes=VMEM_BYTES),
        cost_estimate=pl.CostEstimate(flops=0, bytes_accessed=8 * 10**6, transcendentals=0),
    )(entry, entry, entry, cond_rows)


def cond_back_body(*refs):
    gs, ws, out_ref = refs[:3], refs[3:6], refs[6]
    val = nt(gs[0][...], ws[0][0].astype(bf16))
    for k in range(1, 3):
        val = val + nt(gs[k][...], ws[k][0].astype(bf16))

    @pl.when(pl.program_id(0) == 0)
    def _():
        out_ref[...] = val

    @pl.when(pl.program_id(0) > 0)
    def _():
        out_ref[...] += val


def cond_back(g_rows, entry, r):
    rows = g_rows.shape[0]
    return pl.pallas_call(
        cond_back_body,
        out_shape=shape_of((rows, r), f32),
        grid=(LAYERS,),
        in_specs=[
            *[pl.BlockSpec((rows, 2 * D), lambda l, k=k: (0, l * 3 + k)) for k in range(3)],
            *[pl.BlockSpec((1, r, 2 * D), lambda l, k=k: (l, 0, 4 + k)) for k in range(3)],
        ],
        out_specs=pl.BlockSpec((rows, r), lambda l: (0, 0)),
        compiler_params=pltpu.CompilerParams(vmem_limit_bytes=VMEM_BYTES),
        cost_estimate=pl.CostEstimate(flops=0, bytes_accessed=8 * 10**6, transcendentals=0),
    )(*[g_rows] * 3, *[entry] * 3)


def adam_math(gradient, master, moment, square):
    new_moment = beta_one * moment + (1.0 - beta_one) * gradient
    new_square = beta_two * square + (1.0 - beta_two) * gradient * gradient
    first_fix = 1.0 / (1.0 - beta_one**STEP)
    second_fix = 1.0 / (1.0 - beta_two**STEP)
    direction = (
        new_moment * first_fix / (jnp.sqrt(new_square * second_fix) + adam_eps) + decay_rate * master
    )
    new_master = master - learn_rate * direction
    return new_moment, new_square, new_master


def pick_part(grads, kc, ky, i):
    low = jnp.where(ky == 0, grads[0][i], grads[1][i])
    high = jnp.where(ky == 0, grads[2][i], grads[3][i])
    return jnp.where(kc == 0, low, high).astype(f32)


def attn_gradient(sc, grads, cb):
    both = [pick_part(grads, sc[0] ^ cb, sc[1] ^ yb, 0) for yb in range(2)]
    return jnp.concatenate(both, axis=1)


def ffn_gradient(sc, grads, cb, yb):
    both = [pick_part(grads, sc[0] ^ cb, sc[1] ^ yb, i) for i in range(2)]
    return jnp.concatenate(both, axis=1 - cb)


def ada_gradient(sc, grads, layer, k):
    cond, gmod = grads
    at = slice((layer * 3 + k) * 2 * D, (layer * 3 + k + 1) * 2 * D)
    return tn(cond[...], gmod[:, at])


def adam_body(pieces, n_grad, n_group, n_prev, scale, sc, *refs):
    grads = refs[:n_grad]
    states = [refs[n_grad + 3 * k : n_grad + 3 * k + 3] for k in range(n_group)]
    at = n_grad + 3 * n_group + n_prev
    outs = [refs[at + 5 * k : at + 5 * k + 5] for k in range(n_group)]
    scratch = refs[at + 5 * n_group :]
    sem_in, sem_out = scratch[-2:]
    held = [scratch[5 * p : 5 * p + 5] for p in range(len(pieces))]
    fetches = []
    for p, (group, place, _) in enumerate(pieces):
        mine = [
            pltpu.make_async_copy(states[group][t].at[place], held[p][t], sem_in.at[p, t]) for t in range(3)
        ]
        for copy in mine:
            copy.start()
        fetches.append(mine)
    writes = []
    for p, (group, place, gradient) in enumerate(pieces):
        for copy in fetches[p]:
            copy.wait()
        master_ref, moment_ref, square_ref, grad_ref, weight_ref = held[p]
        grad = gradient(sc, grads) * scale
        moment, square, master = adam_math(grad, master_ref[...], moment_ref[...], square_ref[...])
        grad_ref[...] = grad
        moment_ref[...] = moment
        square_ref[...] = square
        master_ref[...] = master
        weight_ref[...] = master.astype(bf16)
        order = (grad_ref, moment_ref, square_ref, master_ref, weight_ref)
        for t in range(5):
            copy = pltpu.make_async_copy(order[t], outs[group][t].at[place], sem_out.at[p, t])
            copy.start()
            writes.append(copy)
    for copy in writes:
        copy.wait()


def adam_call(sc, pieces, shapes, grads, groups, scale):
    ins = [*grads]
    for states, _ in groups:
        ins += states
    prev, aliases = [], {}
    for k, (_, done) in enumerate(groups):
        if done is not None:
            for t in range(5):
                aliases[1 + len(ins) + len(prev) + t] = 5 * k + t
            prev += [in_hbm(v) for v in done]
    outs, scratch = [], []
    for states, _ in groups:
        outs += [pltpu.HBM(states[0].shape, f32)] * 4 + [pltpu.HBM(states[0].shape, bf16)]
    for shape in shapes:
        scratch += [pltpu.VMEM(shape, f32)] * 4 + [pltpu.VMEM(shape, bf16)]
    scratch += [pltpu.SemaphoreType.DMA((len(pieces), 3)), pltpu.SemaphoreType.DMA((len(pieces), 5))]
    got = pl.pallas_call(
        partial(adam_body, pieces, len(grads), len(groups), len(prev), scale),
        out_shape=outs,
        grid_spec=pltpu.PrefetchScalarGridSpec(
            num_scalar_prefetch=1,
            grid=(1,),
            in_specs=[
                *[pl.BlockSpec(g.shape, lambda i, s, n=len(g.shape): (0,) * n) for g in grads],
                *[ANY] * (len(ins) - len(grads) + len(prev)),
            ],
            out_specs=[ANY] * len(outs),
            scratch_shapes=scratch,
        ),
        input_output_aliases=aliases,
        compiler_params=pltpu.CompilerParams(
            dimension_semantics=("arbitrary",), vmem_limit_bytes=VMEM_BYTES
        ),
        cost_estimate=pl.CostEstimate(flops=0, bytes_accessed=10**7, transcendentals=0),
    )(sc, *ins, *prev)
    return [list(got[5 * k : 5 * k + 5]) for k in range(len(groups))]


def adam_attn(sc, grads, states, layer, scale, prev, r):
    pieces = [
        (0, (layer, slice(None), slice(cb * 2 * D, (cb + 1) * 2 * D)), partial(attn_gradient, cb=cb))
        for cb in range(2)
    ]
    return adam_call(sc, pieces, [(r, 2 * D)] * 2, grads, [(states, prev)], scale)[0]


def adam_ffn(sc, grads, entry, exits, layer, scale, prev_e, prev_x, r):
    pieces = [
        (0, (layer, slice(None), slice((2 + yb) * 2 * D, (3 + yb) * 2 * D)), partial(ffn_gradient, cb=0, yb=yb))
        for yb in range(2)
    ]
    pieces += [
        (1, (layer, slice(yb * 2 * r, (yb + 1) * 2 * r), slice(None)), partial(ffn_gradient, cb=1, yb=yb))
        for yb in range(2)
    ]
    shapes = [(r, 2 * D)] * 2 + [(2 * r, D)] * 2
    return adam_call(sc, pieces, shapes, grads, [(entry, prev_e), (exits, prev_x)], scale)


def adam_ada(sc, cond_own, gmod_all, states, scale, prev, r):
    pieces = [
        (0, (layer, slice(None), slice((4 + k) * 2 * D, (5 + k) * 2 * D)), partial(ada_gradient, layer=layer, k=k))
        for layer in range(LAYERS)
        for k in range(3)
    ]
    return adam_call(sc, pieces, [(r, 2 * D)] * 6, [cond_own, gmod_all], [(states, prev)], scale)[0]


def swap(v, axis, bit):
    size = lax.axis_size(axis)
    return lax.ppermute(v, axis, [(i, i ^ bit) for i in range(size)])


def spread_fsdp(v, fsdp):
    held = [v]
    bit = 1
    while bit < fsdp:
        held = held + [swap(a, "fsdp", bit) for a in held]
        bit *= 2
    return held


def low_round(v):
    return lax.reduce_precision(v, 8, 7)


def swap_both(v, j, bit):
    size = lax.axis_size("dp") * lax.axis_size("fsdp")
    mask = bit * lax.axis_size("fsdp") + j
    return lax.ppermute(v, ("dp", "fsdp"), [(i, i ^ mask) for i in range(size)])


class Unit:
    def __init__(self, keep, send, dp, fsdp):
        self.fsdp = fsdp
        self.total, self.out = keep, send
        self.plan = [("core", 0), ("scatter", 0)]
        bit = 4
        while bit < dp:
            self.plan.append(("sum", bit))
            bit *= 2
        self.plan += [("share", 2), ("pair", 1)]
        self.at = 0
        self.got = None

    def step(self):
        kind, bit = self.plan[self.at]
        self.at += 1
        if kind == "core":
            self.got = swap(self.out, "dp", 1)
            return [self.out]
        if kind == "scatter":
            total = self.total + self.got.astype(f32)
            outs, self.got = [], []
            for j in range(self.fsdp):
                for ky in range(2):
                    if j or ky:
                        outs.append(total[j, ky].astype(bf16))
                        self.got.append(swap_both(outs[-1], j, 2 * ky))
            self.total = total[0, 0]
            return outs
        if kind in ("sum", "share"):
            got = self.got if isinstance(self.got, (list, tuple)) else [self.got]
            for part in got:
                self.total = self.total + part.astype(f32)
        if kind == "sum":
            self.total = low_round(self.total)
            out = self.total.astype(bf16)
            self.got = swap(out, "dp", bit)
        elif kind == "share":
            out = self.total.astype(bf16)
            self.total = out
            self.got = swap(out, "dp", bit)
        else:
            out = self.got
            self.total = (self.total, self.got)
            self.got = tuple(swap(v, "dp", 1) for v in self.total)
        return [out]

    def result(self):
        return (*self.total, *self.got)

    def done(self):
        return self.at == len(self.plan)


def hold(movers, values):
    tied = lax.optimization_barrier((tuple(values), tuple((m.total, m.got) for m in movers)))
    for m, (total, got) in zip(movers, tied[1]):
        m.total, m.got = total, got
    return tied[0]


class Chain:
    def __init__(self, rows, sums, hops):
        self.total, self.hops, self.got = (rows, sums), hops, None
        self.at = 0

    def step(self):
        self.settle()
        axis, bit = self.hops[self.at]
        self.at += 1
        self.got = tuple(swap(v, axis, bit) for v in self.total)

    def settle(self):
        if self.got is None:
            return
        axis, bit = self.hops[self.at - 1]
        rows, sums = self.total
        upper = (lax.axis_index(axis) & bit) != 0
        got = self.got[0]
        rows = jnp.concatenate([jnp.where(upper, got, rows), jnp.where(upper, rows, got)], axis=0)
        self.total = (rows, sums + self.got[1])
        self.got = None


def join(v, axis, bit):
    got = swap(v, axis, bit)
    upper = (lax.axis_index(axis) & bit) != 0
    return jnp.stack([jnp.where(upper, got, v), jnp.where(upper, v, got)], axis=0)


def per_device(
    tokens, condition, image_grid, image_counts, cotangent,
    entry_master, exit_master, bias_master,
    entry_moment, exit_moment, bias_moment,
    entry_square, exit_square, bias_square,
):
    dp, fsdp = lax.axis_size("dp"), lax.axis_size("fsdp")
    r = D // fsdp
    dp_at, f_at = lax.axis_index("dp"), lax.axis_index("fsdp")
    scale = (IMG * SLOTS * dp * fsdp) ** (-0.5)

    cond_float = condition.astype(f32)
    cond_act = jax.nn.silu(cond_float).astype(bf16)
    cond_rel = spread_fsdp(cond_act, fsdp)
    core = dp_at & 1

    def columns(layer, start, core):
        return lax.dynamic_slice(
            entry_master, (layer, 0, start + core * 2 * D), (1, r, 2 * D)
        )[0].astype(bf16)

    def ffn_halves(layer, core):
        low = lax.dynamic_slice(exit_master, (layer, core * 2 * r, 0), (1, 2 * r, D))[0].astype(bf16)
        return columns(layer, 4 * D, core), low

    def send_over(v):
        held = spread_fsdp(v, fsdp)
        return held[1:]

    def to_pair(parts):
        return [swap(v, "dp", 1) for v in parts]

    cond_rows = jnp.concatenate(
        [lax.dynamic_slice_in_dim(v, f_at * r, r, 1) for v in cond_rel], axis=0
    )
    first_send, held_bias = lax.optimization_barrier((columns(0, 0, core), bias_master))
    attn0 = send_over(first_send)
    bias_low = held_bias.astype(bf16)
    bias_all = bias_low[None]
    bit = 1
    while bit < fsdp:
        bias_all = join(bias_all, "fsdp", bit).reshape(-1, *bias_low.shape)
        bit *= 2
    biases = jnp.moveaxis(bias_all, 0, 1).reshape(LAYERS, 1, -1).astype(f32)
    partial_mod = mod_partial(in_hbm(entry_master), cond_rows, r, fsdp)
    core_one, partial_mod, ffn_cols, ffn_rows, counts, grid = lax.optimization_barrier(
        (core, partial_mod, *ffn_halves(0, core), image_counts, image_grid)
    )
    counted = jnp.where(
        jnp.arange(IMG) < counts[0], grid[:, 0] * grid[:, 1], 0
    ).astype(jnp.int32)
    sc = jnp.concatenate(
        [jnp.stack([dp_at & 1, (dp_at >> 1) & 1, f_at, f_at]).astype(jnp.int32), counted]
    )
    mod_got = [swap(partial_mod[j], "fsdp", j) for j in range(1, fsdp)]
    ffn0 = send_over(ffn_cols), send_over(ffn_rows)
    core_two, attn0, mod_got, sc = lax.optimization_barrier((core_one, attn0, mod_got, sc))
    attn0_pair = to_pair(attn0)
    mod = partial_mod[0]
    for got in mod_got:
        mod = mod + got
    hidden_end, ada_end = 4 * D + FF, 10 * D + FF
    mods = mod + biases[:, :, hidden_end:ada_end]
    held_entry, held_exit = in_hbm(entry_master), in_hbm(exit_master)

    mid0, qkv0, att0, wa0 = attn_forward(
        HELD, sc, 0, tokens, mods, biases, held_entry, (attn0, attn0_pair), (), r, fsdp
    )
    send = (columns(1, 0, core_two), *ffn_halves(1, core_two))
    mid0, ffn0, send = lax.optimization_barrier((mid0, ffn0, send))
    ffn0_pair = to_pair(ffn0[0]), to_pair(ffn0[1])
    attn1 = send_over(send[0])
    ffn1 = send_over(send[1]), send_over(send[2])
    x1, lv0, w10, w20 = ffn_forward(
        sc, 0, mid0, mods, biases, held_entry, held_exit,
        (ffn0[0], ffn0_pair[0], ffn0[1], ffn0_pair[1]), (), r, fsdp,
    )
    x1, attn1 = lax.optimization_barrier((x1, attn1))
    attn1_pair = to_pair(attn1)
    mid1, qkv1, att1, wa1 = attn_forward(
        HELD, sc, 1, in_vmem(x1), mods, biases, held_entry, (attn1, attn1_pair), (), r, fsdp
    )
    mid1, ffn1 = lax.optimization_barrier((mid1, ffn1))
    ffn1_pair = to_pair(ffn1[0]), to_pair(ffn1[1])
    block_output, gmid1, gm1b, bs1_1, bs1_2, keep, send = ffn_last(
        sc, 1, mid1, cotangent, mods, biases, held_entry, held_exit,
        (ffn1[0], ffn1_pair[0], ffn1[1], ffn1_pair[1]), (), r, fsdp,
    )
    u_a = Unit(keep, send, dp, fsdp)
    u_a.step()
    deps = u_a.step()
    gx1, gm1a, bs1_a, keep, send = attn_back(
        HELD, in_vmem, sc, 1, gmid1, in_vmem(x1), mods, biases, qkv1, att1, wa1, deps, r, fsdp
    )
    gx1, keep, send = hold([u_a], [gx1, keep, send])
    u_b = Unit(keep, send, dp, fsdp)
    u_b.step()
    deps = u_a.step() + u_b.step()
    gmid0, gm0b, bs0_1, bs0_2, keep, send = ffn_back(
        sc, 0, gx1, mid0, mods, biases, lv0, w10, w20, deps, r, fsdp
    )
    gmid0, keep, send = hold([u_a, u_b], [gmid0, keep, send])
    u_c = Unit(keep, send, dp, fsdp)
    u_c.step()
    deps = u_a.step() + u_b.step() + u_c.step()
    grad_tokens, gm0a, bs0_a, keep, send = attn_back(
        ROW, in_vmem, sc, 0, gmid0, tokens, mods, biases, qkv0, att0, wa0, deps, r, fsdp
    )
    g_mods = [gm0a, gm0b, gm1a, gm1b]
    b_sums = [bs0_a, bs0_1, bs0_2, bs1_a, bs1_1, bs1_2]
    grad_tokens, keep, send, *tied = hold(
        [u_a, u_b, u_c], [grad_tokens, keep, send, *g_mods, *b_sums]
    )
    g_mods, b_sums = tied[:4], tied[4:]
    u_d = Unit(keep, send, dp, fsdp)
    u_d.step()
    units = [u_a, u_b, u_c, u_d]
    outs = u_d.step()
    for unit in (u_c, u_a, u_b):
        unit.step()
    wide = LAYERS * ADA
    g_mod = jnp.concatenate(g_mods, axis=1).astype(bf16).reshape(IMG, wide)
    hops = []
    bit = 1
    while bit < fsdp:
        hops.append(("fsdp", bit))
        bit *= 2
    group_hops = len(hops)
    bit = 2
    while bit < dp:
        hops.append(("dp", bit))
        bit *= 2
    hops.append(("dp", 1))
    chain = Chain(jnp.concatenate([g_mod, cond_act], axis=1), jnp.concatenate(b_sums, axis=1), hops)
    for _ in range(group_hops):
        chain.step()
    chain.settle()
    group_rows, _ = lax.optimization_barrier((chain.total[0], outs))
    back = cond_back(group_rows, held_entry, r)
    (back,) = hold([chain, *units], [back])
    back = back.reshape(fsdp, IMG, r)

    entry = [held_entry, in_hbm(entry_moment), in_hbm(entry_square)]
    exits = [held_exit, in_hbm(exit_moment), in_hbm(exit_square)]
    e = x = None
    updates = [(u_a, 1, True), (u_b, 1, False), (u_c, 0, True), (u_d, 0, False)]
    while True:
        for unit in units:
            if not unit.done():
                unit.step()
        if chain.at < len(hops) - 1:
            chain.step()
        for item in [u for u in updates if u[0].done()]:
            unit, layer, ffn = item
            updates.remove(item)
            if ffn:
                e, x = adam_ffn(sc, unit.result(), entry, exits, layer, scale, e, x, r)
            else:
                e = adam_attn(sc, unit.result(), entry, layer, scale, e, r)
        if not updates:
            break
        kept = [*(e or []), *(x or []), back]
        slow = [] if chain.at == len(hops) - 1 else [chain]
        tied = hold([*slow, *[u for u in units if not u.done()]], kept)
        back = tied[-1]
        e = tied[:5] if e else None
        x = tied[5:10] if x else None

    pieces = [lax.dynamic_index_in_dim(back, f_at, 0, keepdims=False)]
    for j in range(1, fsdp):
        pieces.append(swap(lax.dynamic_index_in_dim(back, f_at ^ j, 0, keepdims=False), "fsdp", j))
    tied = hold([chain], [*pieces, *e])
    pieces, e = tied[:fsdp], list(tied[fsdp:])
    while chain.at < len(hops):
        chain.step()
    chain.settle()
    rows, bias_sum = chain.total
    cond_own = lax.dynamic_slice_in_dim(rows, wide + f_at * r, r, 1)
    e = adam_ada(sc, cond_own, rows, entry, scale, e, r)
    g_cond = jnp.zeros((fsdp, IMG, r), f32)
    for j in range(fsdp):
        g_cond = lax.dynamic_update_index_in_dim(g_cond, pieces[j], f_at ^ j, 0)
    g_cond = jnp.moveaxis(g_cond, 0, 1).reshape(IMG, D)
    grad_condition = jax.vjp(jax.nn.silu, cond_float)[1](g_cond)[0]
    ada_bias = jnp.sum(rows[:, :wide].astype(f32), axis=0).reshape(LAYERS, ADA)
    bias_sum = bias_sum.reshape(LAYERS, -1)
    bias_sum = jnp.concatenate([bias_sum[:, :hidden_end], ada_bias, bias_sum[:, hidden_end:]], axis=1)
    width = bias_master.shape[1]
    bias_grad = lax.dynamic_slice_in_dim(bias_sum, f_at * width, width, 1) * scale
    exit_bias_grad = lax.dynamic_slice_in_dim(bias_sum[:, ada_end:], f_at * r, r, 1) * scale
    bias_moment_new, bias_square_new, bias_master_new = adam_math(
        bias_grad, bias_master, bias_moment, bias_square
    )
    return (
        block_output, grad_tokens, grad_condition,
        *e, *x,
        bias_grad, bias_moment_new, bias_square_new, bias_master_new,
        bias_master_new.astype(bf16), exit_bias_grad,
    )


def solution(mesh):
    rows = P(("dp", "fsdp"), None, None)
    flat = P(("dp", "fsdp"), None)
    mat = P(None, "fsdp", None)
    vec = P(None, "fsdp")
    return jax.shard_map(
        per_device,
        mesh=mesh,
        in_specs=(rows, flat, flat, P(("dp", "fsdp")), rows, mat, mat, vec, mat, mat, vec, mat, mat, vec),
        out_specs=(rows, rows, flat, *[mat] * 10, *[vec] * 6),
        check_vma=False,
    )
```

```python
from functools import partial

import jax
import jax.numpy as jnp
from jax import lax
from jax.experimental import pallas as pl
from jax.experimental.pallas import tpu as pltpu
from jax.sharding import PartitionSpec as P

D = 384
HEADS = 6
HEAD_DIM = 64
FF = 1536
LAYERS = 2
IMG = 4
STEP = 4
SLOTS = 256
ADA = 6 * D

eps_norm = 1e-06
neg_big = -1e30
beta_one = 0.5
beta_two = 0.6
adam_eps = 1e-08
learn_rate = 0.02
decay_rate = 0.1

f32 = jnp.float32
bf16 = jnp.bfloat16
VMEM_BYTES = 24 * 1024 * 1024
VMEM_IMAGE = {"attn_forward": 20, "ffn_forward": 23, "ffn_last": 25, "ffn_back": 21, "attn_back": 17}


def nn(a, b):
    return lax.dot_general(a, b, (((1,), (0,)), ((), ())), preferred_element_type=f32)


def nt(a, b):
    return lax.dot_general(a, b, (((1,), (1,)), ((), ())), preferred_element_type=f32)


def tn(a, b):
    return lax.dot_general(a, b, (((0,), (0,)), ((), ())), preferred_element_type=f32)


def standardize(x):
    mean = jnp.mean(x, axis=-1, keepdims=True)
    cen = x - mean
    var = jnp.mean(cen * cen, axis=-1, keepdims=True)
    rstd = lax.rsqrt(var + eps_norm)
    return cen * rstd, rstd


def norm_back(g, xhat, rstd, scale):
    t = g * (1.0 + scale)
    mean_t = jnp.mean(t, axis=-1, keepdims=True)
    mean_tx = jnp.mean(t * xhat, axis=-1, keepdims=True)
    return (t - mean_t - xhat * mean_tx) * rstd


def colsum(x):
    return jnp.sum(x, axis=0, keepdims=True)


def at_lane(i):
    return pl.ds(pl.multiple_of(i * D, 128), D)


def at_row(i, r):
    return pl.ds(pl.multiple_of(i * r, 16), r)


def place_columns(sc, own, mine, other, w_ref, r, fsdp):
    half = w_ref.shape[1] // 2
    c, f = sc[0], sc[2]
    w_ref[at_row(f, r), :] = own[0].astype(bf16)
    for j in range(1, fsdp):
        for kc, part in ((0, mine), (1, other)):
            w_ref[at_row(f ^ j, r), pl.ds(pl.multiple_of((c ^ kc) * half, 128), half)] = part[j - 1][...]


def place_rows(sc, own, mine, other, w_ref, r, fsdp):
    c, f = sc[0], sc[2]
    w_ref[at_row(f, 4 * r), :] = own[0].astype(bf16)
    for j in range(1, fsdp):
        for kc, part in ((0, mine), (1, other)):
            w_ref[at_row((f ^ j) * 2 + (c ^ kc), 2 * r), :] = part[j - 1][...]


def emit_attn(sc, acc, keep, send, r, fsdp):
    c, y, f = sc[0], sc[1], sc[2]
    for j in range(fsdp):
        for ky in range(2):
            for kc in range(2):
                blk = acc[at_row(f ^ j, r), at_lane((c ^ kc) * 2 + (y ^ ky))]
                if kc == 0:
                    keep[j, ky, 0] = blk
                else:
                    send[j, ky, 0] = blk.astype(bf16)


def emit_ffn(sc, acc1, acc2, keep, send, r, fsdp):
    c, y, f = sc[0], sc[1], sc[2]
    for kc in range(2):
        for cb in range(2):

            @pl.when((c ^ kc) == cb)
            def _(kc=kc, cb=cb):
                for j in range(fsdp):
                    for ky in range(2):
                        for i in range(2):
                            pos = (y ^ ky) * 2 + i
                            if cb == 0:
                                blk = acc1[at_row(f ^ j, r), at_lane(pos)]
                            else:
                                blk = acc2[at_row((f ^ j) * 4 + pos, r), :]
                            if kc == 0:
                                keep[j, ky, i] = blk
                            else:
                                send[j, ky, i] = blk.astype(bf16)


def half_lane():
    return lax.broadcasted_iota(jnp.int32, (1, 2 * HEAD_DIM), 1) < HEAD_DIM


def pair_lanes(qkv, third, p):
    start = third * D + 2 * HEAD_DIM * p
    return qkv[:, start : start + 2 * HEAD_DIM]


def stack_pair(v):
    low_half = half_lane()
    none = jnp.zeros_like(v)
    return jnp.concatenate([jnp.where(low_half, v, none), jnp.where(low_half, none, v)], axis=0)


def pair_probs(qkv, live_slots):
    live = lax.broadcasted_iota(jnp.int32, (1, 2 * SLOTS), 1) & (SLOTS - 1)
    live = live < live_slots
    scores = []
    for p in range(3):
        q = pair_lanes(qkv, 0, p) * jnp.asarray(HEAD_DIM ** (-0.5), bf16)
        scores.append(jnp.where(live, nt(q, stack_pair(pair_lanes(qkv, 1, p))), neg_big))
    out = []
    for s in scores:
        heads = []
        for h in range(2):
            sh = s[:, h * SLOTS : (h + 1) * SLOTS]
            e = jnp.exp(sh - jnp.max(sh, axis=-1, keepdims=True))
            heads.append(e * (1.0 / jnp.sum(e, axis=-1, keepdims=True)))
        out.append(jnp.concatenate(heads, axis=1))
    return out


def flat(v):
    return v.reshape(v.shape[0] * v.shape[1], v.shape[2])


def deep(v):
    return v.reshape(v.shape[0] // SLOTS, SLOTS, v.shape[1])


def slotsum(v):
    return jnp.sum(v, axis=1, keepdims=True)


def mod_part(mod_ref, k, group):
    if group == IMG:
        return mod_ref[0, :, k * D : (k + 1) * D][:, None, :]
    first = pl.program_id(0) * group
    rows = [mod_ref[0, pl.ds(first + i, 1), k * D : (k + 1) * D][None] for i in range(group)]
    return rows[0] if group == 1 else jnp.concatenate(rows, axis=0)


def modulated(x, mod_ref, k):
    xhat, rstd = standardize(x)
    group = x.shape[0]
    normed = (xhat * (1.0 + mod_part(mod_ref, k + 1, group)) + mod_part(mod_ref, k, group)).astype(bf16)
    return xhat, rstd, flat(normed)


def attn_forward_body(group, fsdp, r, *refs):
    sc, x_ref, mod_ref, bias_ref, own = refs[:5]
    n = fsdp - 1
    mine, other = refs[5 : 5 + n], refs[5 + n : 5 + 2 * n]
    mid_ref, qkv_ref, att_ref, w_ref = refs[-4:]
    bias_ref = bias_ref.at[0]
    step = pl.program_id(0)

    @pl.when(step == 0)
    def _():
        place_columns(sc, own, mine, other, w_ref, r, fsdp)

    x = x_ref[...].astype(f32)
    _, _, normed = modulated(x, mod_ref, 0)
    qkv_all = (nn(normed, w_ref[:, : 3 * D]) + bias_ref[:, : 3 * D]).astype(bf16)
    qkv_ref[...] = deep(qkv_all)
    for i in range(group):
        qkv = qkv_all[i * SLOTS : (i + 1) * SLOTS]
        for p, probs in enumerate(pair_probs(qkv, sc[4 + step * group + i])):
            att = nn(probs.astype(bf16), stack_pair(pair_lanes(qkv, 2, p)))
            att_ref[i, :, 2 * HEAD_DIM * p : 2 * HEAD_DIM * (p + 1)] = att.astype(bf16)
    branch = nn(flat(att_ref[...]), w_ref[:, 3 * D :]) + bias_ref[:, 3 * D :]
    mid_ref[...] = x + mod_part(mod_ref, 2, group) * deep(branch)


def gelu(v):
    return v * (0.5 + 0.5 * jnp.tanh(v * (0.7978845608 + (0.7978845608 * 0.044715) * (v * v))))


def gelu_both(v):
    sq = v * v
    half = 0.5 + 0.5 * jnp.tanh(v * (0.7978845608 + (0.7978845608 * 0.044715) * sq))
    slope = 2.0 * 0.7978845608 + (6.0 * 0.044715 * 0.7978845608) * sq
    return v * half, half + v * slope * (half - half * half)


def ffn_forward_body(group, fsdp, r, *refs):
    sc, mid_ref, mod_ref, b1_ref, b2_ref, own1, own2 = refs[:7]
    n = fsdp - 1
    parts = [refs[7 + k * n : 7 + (k + 1) * n] for k in range(4)]
    y_ref, leave_ref, w1_ref, w2_ref = refs[-4:]
    b1_ref, b2_ref = b1_ref.at[0], b2_ref.at[0]

    @pl.when(pl.program_id(0) == 0)
    def _():
        place_columns(sc, own1, parts[0], parts[1], w1_ref, r, fsdp)
        place_rows(sc, own2, parts[2], parts[3], w2_ref, r, fsdp)

    mid = mid_ref[...]
    _, _, normed = modulated(mid, mod_ref, 3)
    act = gelu(nn(normed, w1_ref[...]) + b1_ref[...]).astype(bf16)
    leaving = deep(nn(act, w2_ref[...]) + b2_ref[...])
    leave_ref[...] = leaving
    y_ref[...] = mid + mod_part(mod_ref, 5, group) * leaving


def accumulate(ref, val):
    @pl.when(pl.program_id(0) == 0)
    def _():
        ref[...] = val

    @pl.when(pl.program_id(0) > 0)
    def _():
        ref[...] += val


def ffn_back_core(
    group, g_y, xhat, rstd, normed, slope, act, leaving, mod_ref, w1, w2,
    gmid_ref, gmod_ref, bs1_ref, bs2_ref, held,
):
    normed_all, pre_all, act_all, leave_all = held
    rows = group * SLOTS
    at = pl.ds(pl.multiple_of(pl.program_id(0) * rows, rows), rows)
    g_leave = flat((mod_part(mod_ref, 5, group) * g_y).astype(bf16))
    gmod_ref[:, 2:3] = slotsum(g_y * leaving)
    g_pre = (slope * nt(g_leave, w2[...])).astype(bf16)
    normed_all[at, :] = normed
    act_all[at, :] = act
    leave_all[at, :] = g_leave
    pre_all[at, :] = g_pre
    g_n = deep(nt(g_pre, w1[...]))
    gmod_ref[:, 0:1] = slotsum(g_n)
    gmod_ref[:, 1:2] = slotsum(g_n * xhat)
    gmid_ref[...] = g_y + norm_back(g_n, xhat, rstd, mod_part(mod_ref, 4, group))
    accumulate(bs1_ref, colsum(g_pre.astype(f32)))
    accumulate(bs2_ref, colsum(g_leave.astype(f32)))


def ffn_weight_grads(sc, held, acc1, acc2, keep, send, r, fsdp):
    normed_all, pre_all, act_all, leave_all = held
    acc1[...] = tn(normed_all[...], pre_all[...])
    acc2[...] = tn(act_all[...], leave_all[...])
    emit_ffn(sc, acc1, acc2, keep, send, r, fsdp)


def ffn_last_body(group, fsdp, r, *refs):
    sc, mid_ref, cot_ref, mod_ref, b1_ref, b2_ref, own1, own2 = refs[:8]
    n = fsdp - 1
    parts = [refs[8 + k * n : 8 + (k + 1) * n] for k in range(4)]
    (out_ref, gmid_ref, gmod_ref, bs1_ref, bs2_ref, keep, send, w1_ref, w2_ref, acc1, acc2, *held) = refs[-15:]
    b1_ref, b2_ref = b1_ref.at[0], b2_ref.at[0]
    step = pl.program_id(0)

    @pl.when(step == 0)
    def _():
        place_columns(sc, own1, parts[0], parts[1], w1_ref, r, fsdp)
        place_rows(sc, own2, parts[2], parts[3], w2_ref, r, fsdp)

    mid = mid_ref[...]
    xhat, rstd, normed = modulated(mid, mod_ref, 3)
    act, slope = gelu_both(nn(normed, w1_ref[...]) + b1_ref[...])
    act = act.astype(bf16)
    leaving = deep(nn(act, w2_ref[...]) + b2_ref[...])
    out_ref[...] = (mid + mod_part(mod_ref, 5, group) * leaving).astype(bf16)
    slots = lax.broadcasted_iota(jnp.int32, (1, SLOTS, 1), 1)
    g_y = jnp.concatenate(
        [
            jnp.where(slots < sc[4 + step * group + i], cot_ref[i : i + 1].astype(f32), 0.0)
            for i in range(group)
        ],
        axis=0,
    )
    ffn_back_core(
        group, g_y, xhat, rstd, normed, slope, act, leaving, mod_ref, w1_ref, w2_ref,
        gmid_ref, gmod_ref, bs1_ref, bs2_ref, held,
    )

    @pl.when(step == IMG // group - 1)
    def _():
        ffn_weight_grads(sc, held, acc1, acc2, keep, send, r, fsdp)


def ffn_back_body(group, fsdp, r, *refs):
    sc, gy_ref, mid_ref, mod_ref, b1_ref, leave_ref, w1_ref, w2_ref = refs[:8]
    (gmid_ref, gmod_ref, bs1_ref, bs2_ref, keep, send, acc1, acc2, *held) = refs[-12:]
    xhat, rstd, normed = modulated(mid_ref[...], mod_ref, 3)
    act, slope = gelu_both(nn(normed, w1_ref[...]) + b1_ref[0])
    ffn_back_core(
        group, gy_ref[...], xhat, rstd, normed, slope, act.astype(bf16), leave_ref[...], mod_ref,
        w1_ref, w2_ref, gmid_ref, gmod_ref, bs1_ref, bs2_ref, held,
    )

    @pl.when(pl.program_id(0) == IMG // group - 1)
    def _():
        ffn_weight_grads(sc, held, acc1, acc2, keep, send, r, fsdp)


def attn_back_body(group, fsdp, r, *refs):
    (sc, gmid_ref, x_ref, mod_ref, bias_ref, qkv_ref, att_ref, w_ref) = refs[:8]
    (gx_ref, gmod_ref, bs_ref, keep, send, acc, normed_all, gproj_all, att_all, branch_all) = refs[-10:]
    bias_ref = bias_ref.at[0]
    step = pl.program_id(0)
    rows = group * SLOTS
    at = pl.ds(pl.multiple_of(step * rows, rows), rows)
    gmid = gmid_ref[...]
    att = flat(att_ref[...])
    g_branch = flat((mod_part(mod_ref, 2, group) * gmid).astype(bf16))
    g_att_all = nt(g_branch, w_ref[:, 3 * D :]).astype(bf16)
    low_half = half_lane()
    for i in range(group):
        qkv = qkv_ref[i]
        g_att = g_att_all[i * SLOTS : (i + 1) * SLOTS]
        live_slots = sc[4 + step * group + i]
        g_probs = [nt(pair_lanes(g_att, 0, p), stack_pair(pair_lanes(qkv, 2, p))) for p in range(3)]
        all_probs = pair_probs(qkv, live_slots)
        live = lax.broadcasted_iota(jnp.int32, (1, SLOTS), 1) < live_slots
        for p in range(3):
            q, k, ga = pair_lanes(qkv, 0, p), pair_lanes(qkv, 1, p), pair_lanes(g_att, 0, p)
            g_s = []
            for h in range(2):
                gp = g_probs[p][:, h * SLOTS : (h + 1) * SLOTS]
                probs = all_probs[p][:, h * SLOTS : (h + 1) * SLOTS]
                row = jnp.sum(gp * probs, axis=-1, keepdims=True)
                val = jnp.where(live, probs * (gp - row), 0.0)
                g_s.append(val.astype(bf16))
            g_s = jnp.concatenate(g_s, axis=1)
            part = jnp.asarray(HEAD_DIM ** (-0.5), bf16)
            gq = nn(g_s, stack_pair(k * part))
            gk = tn(g_s, q * part)
            gv = tn(all_probs[p].astype(bf16), ga)
            gk = jnp.where(low_half, gk[:SLOTS], gk[SLOTS:])
            gv = jnp.where(low_half, gv[:SLOTS], gv[SLOTS:])
            here = pl.ds(pl.multiple_of(step * rows + i * SLOTS, SLOTS), SLOTS)
            for t, val in enumerate((gq, gk, gv)):
                lanes = slice(t * D + 2 * HEAD_DIM * p, t * D + 2 * HEAD_DIM * (p + 1))
                gproj_all[here, lanes] = val.astype(bf16)
    branch = deep(nn(att, w_ref[:, 3 * D :]) + bias_ref[:, 3 * D :])
    gmod_ref[:, 2:3] = slotsum(gmid * branch)
    xhat, rstd, normed = modulated(x_ref[...].astype(f32), mod_ref, 0)
    normed_all[at, :] = normed
    att_all[at, :] = att
    branch_all[at, :] = g_branch
    gp = gproj_all[at, :]
    g_n = deep(nt(gp, w_ref[:, : 3 * D]))
    gmod_ref[:, 0:1] = slotsum(g_n)
    gmod_ref[:, 1:2] = slotsum(g_n * xhat)
    gx_ref[...] = gmid + norm_back(g_n, xhat, rstd, mod_part(mod_ref, 1, group))
    accumulate(bs_ref, jnp.concatenate([colsum(gp.astype(f32)), colsum(g_branch.astype(f32))], axis=1))

    @pl.when(step == IMG // group - 1)
    def _():
        acc[:, : 3 * D] = tn(normed_all[...], gproj_all[...])
        acc[:, 3 * D :] = tn(att_all[...], branch_all[...])
        emit_attn(sc, acc, keep, send, r, fsdp)


GROUP = {"attn_forward": 2, "ffn_forward": 2, "ffn_last": 1, "ffn_back": 1, "attn_back": 1}


def per_image(g, *tail):
    return pl.BlockSpec((g, *tail), lambda i, s: (i, *([0] * len(tail))))


def whole(*shape):
    return pl.BlockSpec(shape, lambda i, s: (0,) * len(shape))


def shape_of(dims, dt):
    return jax.ShapeDtypeStruct(dims, dt)


ANY = pl.BlockSpec(memory_space=pl.ANY)


def in_hbm(v):
    return pltpu.with_memory_space_constraint(v, pltpu.HBM)


def in_vmem(v):
    return pltpu.with_memory_space_constraint(v, pltpu.VMEM)


def image_call(g, limit, body, sc, ins, in_specs, outs, deps=(), scratch=(), flops=0, moved=0):
    return pl.pallas_call(
        body,
        out_shape=[o[0] for o in outs],
        grid_spec=pltpu.PrefetchScalarGridSpec(
            num_scalar_prefetch=1,
            grid=(IMG // g,),
            in_specs=[*in_specs, *[ANY] * len(deps)],
            out_specs=[o[1] for o in outs],
            scratch_shapes=list(scratch),
        ),
        compiler_params=pltpu.CompilerParams(
            dimension_semantics=("arbitrary",), vmem_limit_bytes=limit * 1024 * 1024
        ),
        cost_estimate=pl.CostEstimate(flops=flops, bytes_accessed=moved, transcendentals=0),
    )(sc, *ins, *deps)


def mod_spec(g, layer):
    return pl.BlockSpec((1, IMG, ADA), lambda i, s: (layer, 0, 0))


def bias_spec(layer, width, k):
    return pl.BlockSpec((1, 1, width), lambda i, s: (layer, 0, k))


def own_spec(layer, rows, width, k):
    return pl.BlockSpec((1, rows, width), lambda i, s: (layer, 0, k))


ROW = lambda g, dt, w=D: (shape_of((IMG, SLOTS, w), dt), per_image(g, SLOTS, w))
FAR = lambda g, dt, w=D: (pltpu.HBM((IMG, SLOTS, w), dt), per_image(g, SLOTS, w))
HELD = lambda g, dt, w=D: (pltpu.VMEM((IMG, SLOTS, w), dt), per_image(g, SLOTS, w))


def attn_forward(far, sc, layer, x, mods, biases, entry, parts, deps, r, fsdp):
    pieces = [*parts[0], *parts[1]]
    g = GROUP["attn_forward"]
    return image_call(
        g,
        VMEM_IMAGE["attn_forward"],
        partial(attn_forward_body, g, fsdp, r),
        sc,
        [x, mods, biases, entry, *pieces],
        [
            per_image(g, SLOTS, D), mod_spec(g, layer), bias_spec(layer, 4 * D, 0),
            own_spec(layer, r, 4 * D, 0), *[whole(r, 2 * D)] * len(pieces),
        ],
        [
            HELD(g, f32),
            far(g, bf16, 3 * D),
            far(g, bf16),
            ((pltpu.HBM if far is FAR else pltpu.VMEM)((D, 4 * D), bf16), whole(D, 4 * D)),
        ],
        deps,
        flops=3 * 10**9,
        moved=30 * 10**6,
    )


def ffn_part_specs(layer, parts, r):
    pieces = [*parts[0], *parts[1], *parts[2], *parts[3]]
    n = len(parts[0])
    return pieces, [
        bias_spec(layer, FF, 1), bias_spec(layer, D, 14), own_spec(layer, r, FF, 1), own_spec(layer, 4 * r, D, 0),
        *[whole(r, 2 * D)] * (2 * n), *[whole(2 * r, D)] * (2 * n),
    ]


def ffn_forward(sc, layer, mid, mods, biases, entry, exits, parts, deps, r, fsdp):
    pieces, specs = ffn_part_specs(layer, parts, r)
    g = GROUP["ffn_forward"]
    return image_call(
        g,
        VMEM_IMAGE["ffn_forward"],
        partial(ffn_forward_body, g, fsdp, r),
        sc,
        [in_vmem(mid), mods, biases, biases, entry, exits, *pieces],
        [per_image(g, SLOTS, D), mod_spec(g, layer), *specs],
        [
            HELD(g, f32),
            HELD(g, f32),
            (pltpu.VMEM((D, FF), bf16), whole(D, FF)),
            (pltpu.VMEM((FF, D), bf16), whole(FF, D)),
        ],
        deps,
        flops=3 * 10**9,
        moved=30 * 10**6,
    )


def grad_outs(fsdp, m, r):
    return [
        (shape_of((fsdp, 2, m, r, D), f32), whole(fsdp, 2, m, r, D)),
        (shape_of((fsdp, 2, m, r, D), bf16), whole(fsdp, 2, m, r, D)),
    ]


def ffn_back_outs(place, g, fsdp, r):
    return [
        place(g, f32),
        (shape_of((IMG, 3, D), f32), per_image(g, 3, D)),
        (shape_of((1, FF), f32), whole(1, FF)),
        (shape_of((1, D), f32), whole(1, D)),
        *grad_outs(fsdp, 2, r),
    ]


FFN_ACC = [
    pltpu.VMEM((D, FF), f32), pltpu.VMEM((FF, D), f32),
    pltpu.VMEM((IMG * SLOTS, D), bf16), pltpu.VMEM((IMG * SLOTS, FF), bf16),
    pltpu.VMEM((IMG * SLOTS, FF), bf16), pltpu.VMEM((IMG * SLOTS, D), bf16),
]


def ffn_last(sc, layer, mid, cot, mods, biases, entry, exits, parts, deps, r, fsdp):
    pieces, specs = ffn_part_specs(layer, parts, r)
    g = GROUP["ffn_last"]
    return image_call(
        g,
        VMEM_IMAGE["ffn_last"],
        partial(ffn_last_body, g, fsdp, r),
        sc,
        [in_vmem(mid), cot, mods, biases, biases, entry, exits, *pieces],
        [per_image(g, SLOTS, D), per_image(g, SLOTS, D), mod_spec(g, layer), *specs],
        [ROW(g, bf16), *ffn_back_outs(HELD, g, fsdp, r)],
        deps,
        scratch=[pltpu.VMEM((D, FF), bf16), pltpu.VMEM((FF, D), bf16), *FFN_ACC],
        flops=8 * 10**9,
        moved=50 * 10**6,
    )


def ffn_back(sc, layer, gy, mid, mods, biases, leaving, w1, w2, deps, r, fsdp):
    g = GROUP["ffn_back"]
    return image_call(
        g,
        VMEM_IMAGE["ffn_back"],
        partial(ffn_back_body, g, fsdp, r),
        sc,
        [in_vmem(gy), in_vmem(mid), mods, biases, in_vmem(leaving), in_vmem(w1), in_vmem(w2)],
        [
            per_image(g, SLOTS, D), per_image(g, SLOTS, D), mod_spec(g, layer), bias_spec(layer, FF, 1),
            per_image(g, SLOTS, D), whole(D, FF), whole(FF, D),
        ],
        ffn_back_outs(HELD, g, fsdp, r),
        deps,
        scratch=FFN_ACC,
        flops=6 * 10**9,
        moved=50 * 10**6,
    )


def attn_back(out_row, near, sc, layer, gmid, x, mods, biases, qkv, att, w, deps, r, fsdp):
    g = GROUP["attn_back"]
    return image_call(
        g,
        VMEM_IMAGE["attn_back"],
        partial(attn_back_body, g, fsdp, r),
        sc,
        [near(gmid), x, mods, biases, near(qkv), near(att), near(w)],
        [
            per_image(g, SLOTS, D), per_image(g, SLOTS, D), mod_spec(g, layer), bias_spec(layer, 4 * D, 0),
            per_image(g, SLOTS, 3 * D), per_image(g, SLOTS, D), whole(D, 4 * D),
        ],
        [
            out_row(g, f32),
            (shape_of((IMG, 3, D), f32), per_image(g, 3, D)),
            (shape_of((1, 4 * D), f32), whole(1, 4 * D)),
            *grad_outs(fsdp, 1, r),
        ],
        deps,
        scratch=[
            pltpu.VMEM((D, 4 * D), f32), pltpu.VMEM((IMG * SLOTS, D), bf16),
            pltpu.VMEM((IMG * SLOTS, 3 * D), bf16), pltpu.VMEM((IMG * SLOTS, D), bf16),
            pltpu.VMEM((IMG * SLOTS, D), bf16),
        ],
        flops=6 * 10**9,
        moved=50 * 10**6,
    )


def mod_body(fsdp, *refs):
    ws, conds, outs = refs[:3], refs[3][...], refs[4:]
    for k in range(3):
        val = nn(conds, ws[k][0].astype(bf16))
        for j in range(fsdp):
            outs[j][0, :, 2 * D * k : 2 * D * (k + 1)] = val[j * IMG : (j + 1) * IMG]


def mod_partial(entry, cond_rows, r, fsdp):
    return pl.pallas_call(
        partial(mod_body, fsdp),
        out_shape=[shape_of((LAYERS, IMG, ADA), f32)] * fsdp,
        grid=(LAYERS,),
        in_specs=[
            *[pl.BlockSpec((1, r, 2 * D), lambda l, k=k: (l, 0, 4 + k)) for k in range(3)],
            pl.BlockSpec((fsdp * IMG, r), lambda l: (0, 0)),
        ],
        out_specs=[pl.BlockSpec((1, IMG, ADA), lambda l: (l, 0, 0))] * fsdp,
        compiler_params=pltpu.CompilerParams(vmem_limit_bytes=VMEM_BYTES),
        cost_estimate=pl.CostEstimate(flops=0, bytes_accessed=8 * 10**6, transcendentals=0),
    )(entry, entry, entry, cond_rows)


def cond_back_body(*refs):
    gs, ws, out_ref = refs[:3], refs[3:6], refs[6]
    val = nt(gs[0][...], ws[0][0].astype(bf16))
    for k in range(1, 3):
        val = val + nt(gs[k][...], ws[k][0].astype(bf16))

    @pl.when(pl.program_id(0) == 0)
    def _():
        out_ref[...] = val

    @pl.when(pl.program_id(0) > 0)
    def _():
        out_ref[...] += val


def cond_back(g_rows, entry, r):
    rows = g_rows.shape[0]
    return pl.pallas_call(
        cond_back_body,
        out_shape=shape_of((rows, r), f32),
        grid=(LAYERS,),
        in_specs=[
            *[pl.BlockSpec((rows, 2 * D), lambda l, k=k: (0, l * 3 + k)) for k in range(3)],
            *[pl.BlockSpec((1, r, 2 * D), lambda l, k=k: (l, 0, 4 + k)) for k in range(3)],
        ],
        out_specs=pl.BlockSpec((rows, r), lambda l: (0, 0)),
        compiler_params=pltpu.CompilerParams(vmem_limit_bytes=VMEM_BYTES),
        cost_estimate=pl.CostEstimate(flops=0, bytes_accessed=8 * 10**6, transcendentals=0),
    )(*[g_rows] * 3, *[entry] * 3)


def adam_math(gradient, master, moment, square):
    new_moment = beta_one * moment + (1.0 - beta_one) * gradient
    new_square = beta_two * square + (1.0 - beta_two) * gradient * gradient
    first_fix = 1.0 / (1.0 - beta_one**STEP)
    second_fix = 1.0 / (1.0 - beta_two**STEP)
    direction = (
        new_moment * first_fix / (jnp.sqrt(new_square * second_fix) + adam_eps) + decay_rate * master
    )
    new_master = master - learn_rate * direction
    return new_moment, new_square, new_master


def pick_part(grads, kc, ky, i):
    low = jnp.where(ky == 0, grads[0][i], grads[1][i])
    high = jnp.where(ky == 0, grads[2][i], grads[3][i])
    return jnp.where(kc == 0, low, high).astype(f32)


def attn_gradient(sc, grads, cb):
    both = [pick_part(grads, sc[0] ^ cb, sc[1] ^ yb, 0) for yb in range(2)]
    return jnp.concatenate(both, axis=1)


def ffn_gradient(sc, grads, cb, yb):
    both = [pick_part(grads, sc[0] ^ cb, sc[1] ^ yb, i) for i in range(2)]
    return jnp.concatenate(both, axis=1 - cb)


def ada_gradient(sc, grads, layer, k):
    cond, gmod = grads
    at = slice((layer * 3 + k) * 2 * D, (layer * 3 + k + 1) * 2 * D)
    return tn(cond[...], gmod[:, at])


def some_rows(gradient, low, high, sc, grads):
    return gradient(sc, grads)[low:high]


def cut(pieces, shapes, r):
    if r % 32:
        return pieces, shapes
    out, sizes = [], []
    for (group, (layer, rows, cols), gradient), shape in zip(pieces, shapes):
        first, half = rows.start or 0, shape[0] // 2
        for k in range(2):
            at = slice(first + k * half, first + (k + 1) * half)
            out.append((group, (layer, at, cols), partial(some_rows, gradient, k * half, (k + 1) * half)))
            sizes.append((half, shape[1]))
    return out, sizes


def adam_body(pieces, n_grad, n_group, n_prev, scale, sc, *refs):
    grads = refs[:n_grad]
    states = [refs[n_grad + 3 * k : n_grad + 3 * k + 3] for k in range(n_group)]
    at = n_grad + 3 * n_group + n_prev
    outs = [refs[at + 5 * k : at + 5 * k + 5] for k in range(n_group)]
    scratch = refs[at + 5 * n_group :]
    sem_in, sem_out = scratch[-2:]
    held = [scratch[5 * p : 5 * p + 5] for p in range(len(pieces))]
    fetches = []
    for p, (group, place, _) in enumerate(pieces):
        mine = [
            pltpu.make_async_copy(states[group][t].at[place], held[p][t], sem_in.at[p, t]) for t in range(3)
        ]
        for copy in mine:
            copy.start()
        fetches.append(mine)
    writes = []
    for p, (group, place, gradient) in enumerate(pieces):
        for copy in fetches[p]:
            copy.wait()
        master_ref, moment_ref, square_ref, grad_ref, weight_ref = held[p]
        grad = gradient(sc, grads) * scale
        moment, square, master = adam_math(grad, master_ref[...], moment_ref[...], square_ref[...])
        grad_ref[...] = grad
        moment_ref[...] = moment
        square_ref[...] = square
        master_ref[...] = master
        weight_ref[...] = master.astype(bf16)
        order = (grad_ref, moment_ref, square_ref, master_ref, weight_ref)
        for t in range(5):
            copy = pltpu.make_async_copy(order[t], outs[group][t].at[place], sem_out.at[p, t])
            copy.start()
            writes.append(copy)
    for copy in writes:
        copy.wait()


def adam_call(sc, pieces, shapes, grads, groups, scale):
    ins = [*grads]
    for states, _ in groups:
        ins += states
    prev, aliases = [], {}
    for k, (_, done) in enumerate(groups):
        if done is not None:
            for t in range(5):
                aliases[1 + len(ins) + len(prev) + t] = 5 * k + t
            prev += [in_hbm(v) for v in done]
    outs, scratch = [], []
    for states, _ in groups:
        outs += [pltpu.HBM(states[0].shape, f32)] * 4 + [pltpu.HBM(states[0].shape, bf16)]
    for shape in shapes:
        scratch += [pltpu.VMEM(shape, f32)] * 4 + [pltpu.VMEM(shape, bf16)]
    scratch += [pltpu.SemaphoreType.DMA((len(pieces), 3)), pltpu.SemaphoreType.DMA((len(pieces), 5))]
    got = pl.pallas_call(
        partial(adam_body, pieces, len(grads), len(groups), len(prev), scale),
        out_shape=outs,
        grid_spec=pltpu.PrefetchScalarGridSpec(
            num_scalar_prefetch=1,
            grid=(1,),
            in_specs=[
                *[pl.BlockSpec(g.shape, lambda i, s, n=len(g.shape): (0,) * n) for g in grads],
                *[ANY] * (len(ins) - len(grads) + len(prev)),
            ],
            out_specs=[ANY] * len(outs),
            scratch_shapes=scratch,
        ),
        input_output_aliases=aliases,
        compiler_params=pltpu.CompilerParams(
            dimension_semantics=("arbitrary",), vmem_limit_bytes=VMEM_BYTES
        ),
        cost_estimate=pl.CostEstimate(flops=0, bytes_accessed=10**7, transcendentals=0),
    )(sc, *ins, *prev)
    return [list(got[5 * k : 5 * k + 5]) for k in range(len(groups))]


def adam_attn(sc, grads, states, layer, scale, prev, r):
    pieces = [
        (0, (layer, slice(None), slice(cb * 2 * D, (cb + 1) * 2 * D)), partial(attn_gradient, cb=cb))
        for cb in range(2)
    ]
    pieces, shapes = cut(pieces, [(r, 2 * D)] * 2, r)
    return adam_call(sc, pieces, shapes, grads, [(states, prev)], scale)[0]


def adam_ffn(sc, grads, entry, exits, layer, scale, prev_e, prev_x, r):
    pieces = [
        (0, (layer, slice(None), slice((2 + yb) * 2 * D, (3 + yb) * 2 * D)), partial(ffn_gradient, cb=0, yb=yb))
        for yb in range(2)
    ]
    pieces += [
        (1, (layer, slice(yb * 2 * r, (yb + 1) * 2 * r), slice(None)), partial(ffn_gradient, cb=1, yb=yb))
        for yb in range(2)
    ]
    shapes = [(r, 2 * D)] * 2 + [(2 * r, D)] * 2
    return adam_call(sc, pieces, shapes, grads, [(entry, prev_e), (exits, prev_x)], scale)


def adam_ada(sc, cond_own, gmod_all, states, scale, prev, r):
    pieces = [
        (0, (layer, slice(None), slice((4 + k) * 2 * D, (5 + k) * 2 * D)), partial(ada_gradient, layer=layer, k=k))
        for layer in range(LAYERS)
        for k in range(3)
    ]
    return adam_call(sc, pieces, [(r, 2 * D)] * 6, [cond_own, gmod_all], [(states, prev)], scale)[0]


def swap(v, axis, bit):
    size = lax.axis_size(axis)
    return lax.ppermute(v, axis, [(i, i ^ bit) for i in range(size)])


def spread_fsdp(v, fsdp):
    held = [v]
    bit = 1
    while bit < fsdp:
        held = held + [swap(a, "fsdp", bit) for a in held]
        bit *= 2
    return held


def low_round(v):
    return lax.reduce_precision(v, 8, 7)


def swap_both(v, j, bit):
    size = lax.axis_size("dp") * lax.axis_size("fsdp")
    mask = bit * lax.axis_size("fsdp") + j
    return lax.ppermute(v, ("dp", "fsdp"), [(i, i ^ mask) for i in range(size)])


class Unit:
    def __init__(self, keep, send, dp, fsdp):
        self.fsdp = fsdp
        self.total, self.out = keep, send
        self.plan = [("core", 0), ("scatter", 0)]
        bit = 4
        while bit < dp:
            self.plan.append(("sum", bit))
            bit *= 2
        self.plan += [("share", 2), ("pair", 1)]
        self.at = 0
        self.got = None

    def step(self):
        kind, bit = self.plan[self.at]
        self.at += 1
        if kind == "core":
            self.got = swap(self.out, "dp", 1)
            return [self.out]
        if kind == "scatter":
            total = self.total + self.got.astype(f32)
            outs, self.got = [], []
            for j in range(self.fsdp):
                for ky in range(2):
                    if j or ky:
                        outs.append(total[j, ky].astype(bf16))
                        self.got.append(swap_both(outs[-1], j, 2 * ky))
            self.total = total[0, 0]
            return outs
        if kind in ("sum", "share"):
            got = self.got if isinstance(self.got, (list, tuple)) else [self.got]
            for part in got:
                self.total = self.total + part.astype(f32)
        if kind == "sum":
            self.total = low_round(self.total)
            out = self.total.astype(bf16)
            self.got = swap(out, "dp", bit)
        elif kind == "share":
            out = self.total.astype(bf16)
            self.total = out
            self.got = swap(out, "dp", bit)
        else:
            out = self.got
            self.total = (self.total, self.got)
            self.got = tuple(swap(v, "dp", 1) for v in self.total)
        return [out]

    def result(self):
        return (*self.total, *self.got)

    def done(self):
        return self.at == len(self.plan)


def hold(movers, values):
    tied = lax.optimization_barrier((tuple(values), tuple((m.total, m.got) for m in movers)))
    for m, (total, got) in zip(movers, tied[1]):
        m.total, m.got = total, got
    return tied[0]


class Chain:
    def __init__(self, rows, sums, hops):
        self.total, self.hops, self.got = (rows, sums), hops, None
        self.at = 0

    def step(self):
        self.settle()
        axis, bit = self.hops[self.at]
        self.at += 1
        self.got = tuple(swap(v, axis, bit) for v in self.total)

    def settle(self):
        if self.got is None:
            return
        axis, bit = self.hops[self.at - 1]
        rows, sums = self.total
        upper = (lax.axis_index(axis) & bit) != 0
        got = self.got[0]
        rows = jnp.concatenate([jnp.where(upper, got, rows), jnp.where(upper, rows, got)], axis=0)
        self.total = (rows, sums + self.got[1])
        self.got = None


def join(v, axis, bit):
    got = swap(v, axis, bit)
    upper = (lax.axis_index(axis) & bit) != 0
    return jnp.stack([jnp.where(upper, got, v), jnp.where(upper, v, got)], axis=0)


def per_device(
    tokens, condition, image_grid, image_counts, cotangent,
    entry_master, exit_master, bias_master,
    entry_moment, exit_moment, bias_moment,
    entry_square, exit_square, bias_square,
):
    dp, fsdp = lax.axis_size("dp"), lax.axis_size("fsdp")
    r = D // fsdp
    dp_at, f_at = lax.axis_index("dp"), lax.axis_index("fsdp")
    scale = (IMG * SLOTS * dp * fsdp) ** (-0.5)

    cond_float = condition.astype(f32)
    cond_act = jax.nn.silu(cond_float).astype(bf16)
    cond_rel = spread_fsdp(cond_act, fsdp)
    core = dp_at & 1

    def columns(layer, start, core):
        return lax.dynamic_slice(
            entry_master, (layer, 0, start + core * 2 * D), (1, r, 2 * D)
        )[0].astype(bf16)

    def ffn_halves(layer, core):
        low = lax.dynamic_slice(exit_master, (layer, core * 2 * r, 0), (1, 2 * r, D))[0].astype(bf16)
        return columns(layer, 4 * D, core), low

    def send_over(v):
        held = spread_fsdp(v, fsdp)
        return held[1:]

    def to_pair(parts):
        return [swap(v, "dp", 1) for v in parts]

    cond_rows = jnp.concatenate(
        [lax.dynamic_slice_in_dim(v, f_at * r, r, 1) for v in cond_rel], axis=0
    )
    first_send, held_bias = lax.optimization_barrier((columns(0, 0, core), bias_master))
    attn0 = send_over(first_send)
    bias_low = held_bias.astype(bf16)
    bias_all = bias_low[None]
    bit = 1
    while bit < fsdp:
        bias_all = join(bias_all, "fsdp", bit).reshape(-1, *bias_low.shape)
        bit *= 2
    biases = jnp.moveaxis(bias_all, 0, 1).reshape(LAYERS, 1, -1).astype(f32)
    partial_mod = mod_partial(in_hbm(entry_master), cond_rows, r, fsdp)
    core_one, partial_mod, ffn_cols, ffn_rows, counts, grid = lax.optimization_barrier(
        (core, partial_mod, *ffn_halves(0, core), image_counts, image_grid)
    )
    counted = jnp.where(
        jnp.arange(IMG) < counts[0], grid[:, 0] * grid[:, 1], 0
    ).astype(jnp.int32)
    sc = jnp.concatenate(
        [jnp.stack([dp_at & 1, (dp_at >> 1) & 1, f_at, f_at]).astype(jnp.int32), counted]
    )
    mod_got = [swap(partial_mod[j], "fsdp", j) for j in range(1, fsdp)]
    ffn0 = send_over(ffn_cols), send_over(ffn_rows)
    core_two, attn0, mod_got, sc = lax.optimization_barrier((core_one, attn0, mod_got, sc))
    attn0_pair = to_pair(attn0)
    mod = partial_mod[0]
    for got in mod_got:
        mod = mod + got
    hidden_end, ada_end = 4 * D + FF, 10 * D + FF
    mods = mod + biases[:, :, hidden_end:ada_end]
    held_entry, held_exit = in_hbm(entry_master), in_hbm(exit_master)

    mid0, qkv0, att0, wa0 = attn_forward(
        HELD, sc, 0, tokens, mods, biases, held_entry, (attn0, attn0_pair), (), r, fsdp
    )
    send = (columns(1, 0, core_two), *ffn_halves(1, core_two))
    mid0, ffn0, send = lax.optimization_barrier((mid0, ffn0, send))
    ffn0_pair = to_pair(ffn0[0]), to_pair(ffn0[1])
    attn1 = send_over(send[0])
    ffn1 = send_over(send[1]), send_over(send[2])
    x1, lv0, w10, w20 = ffn_forward(
        sc, 0, mid0, mods, biases, held_entry, held_exit,
        (ffn0[0], ffn0_pair[0], ffn0[1], ffn0_pair[1]), (), r, fsdp,
    )
    x1, attn1 = lax.optimization_barrier((x1, attn1))
    attn1_pair = to_pair(attn1)
    mid1, qkv1, att1, wa1 = attn_forward(
        HELD, sc, 1, in_vmem(x1), mods, biases, held_entry, (attn1, attn1_pair), (), r, fsdp
    )
    mid1, ffn1 = lax.optimization_barrier((mid1, ffn1))
    ffn1_pair = to_pair(ffn1[0]), to_pair(ffn1[1])
    block_output, gmid1, gm1b, bs1_1, bs1_2, keep, send = ffn_last(
        sc, 1, mid1, cotangent, mods, biases, held_entry, held_exit,
        (ffn1[0], ffn1_pair[0], ffn1[1], ffn1_pair[1]), (), r, fsdp,
    )
    u_a = Unit(keep, send, dp, fsdp)
    u_a.step()
    deps = u_a.step()
    gx1, gm1a, bs1_a, keep, send = attn_back(
        HELD, in_vmem, sc, 1, gmid1, in_vmem(x1), mods, biases, qkv1, att1, wa1, deps, r, fsdp
    )
    gx1, keep, send = hold([u_a], [gx1, keep, send])
    u_b = Unit(keep, send, dp, fsdp)
    u_b.step()
    deps = u_a.step() + u_b.step()
    gmid0, gm0b, bs0_1, bs0_2, keep, send = ffn_back(
        sc, 0, gx1, mid0, mods, biases, lv0, w10, w20, deps, r, fsdp
    )
    gmid0, keep, send = hold([u_a, u_b], [gmid0, keep, send])
    u_c = Unit(keep, send, dp, fsdp)
    u_c.step()
    deps = u_a.step() + u_b.step() + u_c.step()
    grad_tokens, gm0a, bs0_a, keep, send = attn_back(
        ROW, in_vmem, sc, 0, gmid0, tokens, mods, biases, qkv0, att0, wa0, deps, r, fsdp
    )
    g_mods = [gm0a, gm0b, gm1a, gm1b]
    b_sums = [bs0_a, bs0_1, bs0_2, bs1_a, bs1_1, bs1_2]
    grad_tokens, keep, send, *tied = hold(
        [u_a, u_b, u_c], [grad_tokens, keep, send, *g_mods, *b_sums]
    )
    g_mods, b_sums = tied[:4], tied[4:]
    u_d = Unit(keep, send, dp, fsdp)
    u_d.step()
    units = [u_a, u_b, u_c, u_d]
    outs = u_d.step()
    for unit in (u_c, u_a, u_b):
        unit.step()
    wide = LAYERS * ADA
    g_mod = jnp.concatenate(g_mods, axis=1).astype(bf16).reshape(IMG, wide)
    hops = []
    bit = 1
    while bit < fsdp:
        hops.append(("fsdp", bit))
        bit *= 2
    group_hops = len(hops)
    bit = 2
    while bit < dp:
        hops.append(("dp", bit))
        bit *= 2
    hops.append(("dp", 1))
    chain = Chain(jnp.concatenate([g_mod, cond_act], axis=1), jnp.concatenate(b_sums, axis=1), hops)
    for _ in range(group_hops):
        chain.step()
    chain.settle()
    group_rows, _ = lax.optimization_barrier((chain.total[0], outs))
    back = cond_back(group_rows, held_entry, r)
    (back,) = hold([chain, *units], [back])
    back = back.reshape(fsdp, IMG, r)

    entry = [held_entry, in_hbm(entry_moment), in_hbm(entry_square)]
    exits = [held_exit, in_hbm(exit_moment), in_hbm(exit_square)]
    e = x = None
    updates = [(u_a, 1, True), (u_b, 1, False), (u_c, 0, True), (u_d, 0, False)]
    while True:
        for unit in units:
            if not unit.done():
                unit.step()
        if chain.at < len(hops) - 1:
            chain.step()
        for item in [u for u in updates if u[0].done()]:
            unit, layer, ffn = item
            updates.remove(item)
            if ffn:
                e, x = adam_ffn(sc, unit.result(), entry, exits, layer, scale, e, x, r)
            else:
                e = adam_attn(sc, unit.result(), entry, layer, scale, e, r)
        if not updates:
            break
        kept = [*(e or []), *(x or []), back]
        slow = [] if chain.at == len(hops) - 1 else [chain]
        tied = hold([*slow, *[u for u in units if not u.done()]], kept)
        back = tied[-1]
        e = tied[:5] if e else None
        x = tied[5:10] if x else None

    pieces = [lax.dynamic_index_in_dim(back, f_at, 0, keepdims=False)]
    for j in range(1, fsdp):
        pieces.append(swap(lax.dynamic_index_in_dim(back, f_at ^ j, 0, keepdims=False), "fsdp", j))
    tied = hold([chain], [*pieces, *e])
    pieces, e = tied[:fsdp], list(tied[fsdp:])
    while chain.at < len(hops):
        chain.step()
    chain.settle()
    rows, bias_sum = chain.total
    cond_own = lax.dynamic_slice_in_dim(rows, wide + f_at * r, r, 1)
    e = adam_ada(sc, cond_own, rows, entry, scale, e, r)
    g_cond = jnp.zeros((fsdp, IMG, r), f32)
    for j in range(fsdp):
        g_cond = lax.dynamic_update_index_in_dim(g_cond, pieces[j], f_at ^ j, 0)
    g_cond = jnp.moveaxis(g_cond, 0, 1).reshape(IMG, D)
    grad_condition = jax.vjp(jax.nn.silu, cond_float)[1](g_cond)[0]
    ada_bias = jnp.sum(rows[:, :wide].astype(f32), axis=0).reshape(LAYERS, ADA)
    bias_sum = bias_sum.reshape(LAYERS, -1)
    bias_sum = jnp.concatenate([bias_sum[:, :hidden_end], ada_bias, bias_sum[:, hidden_end:]], axis=1)
    width = bias_master.shape[1]
    bias_grad = lax.dynamic_slice_in_dim(bias_sum, f_at * width, width, 1) * scale
    exit_bias_grad = lax.dynamic_slice_in_dim(bias_sum[:, ada_end:], f_at * r, r, 1) * scale
    bias_moment_new, bias_square_new, bias_master_new = adam_math(
        bias_grad, bias_master, bias_moment, bias_square
    )
    return (
        block_output, grad_tokens, grad_condition,
        *e, *x,
        bias_grad, bias_moment_new, bias_square_new, bias_master_new,
        bias_master_new.astype(bf16), exit_bias_grad,
    )


def solution(mesh):
    rows = P(("dp", "fsdp"), None, None)
    flat = P(("dp", "fsdp"), None)
    mat = P(None, "fsdp", None)
    vec = P(None, "fsdp")
    return jax.shard_map(
        per_device,
        mesh=mesh,
        in_specs=(rows, flat, flat, P(("dp", "fsdp")), rows, mat, mat, vec, mat, mat, vec, mat, mat, vec),
        out_specs=(rows, rows, flat, *[mat] * 10, *[vec] * 6),
        check_vma=False,
    )
```
